32 devices in a mesh: stream: 2 (over y), clip: 16 (over z, x, core).
Axes of the slice: x: 2, y: 2, z: 4, core: 2. Of those that a mesh axis runs over, the one named last changes fastest.
Arguments:
- tokens: bfloat16 [16384, 1024], P(('stream', 'clip')), may hold values from -6 to 6
- w_qkv: float32 [1024, 3072], P(('stream', 'clip')), may hold values from -0.1875 to 0.1875
- w_proj: float32 [1024, 1024], P(('stream', 'clip')), may hold values from -0.75 to 0.75
- w_fc1: float32 [1024, 4096], P(('stream', 'clip')), may hold values from -0.1875 to 0.1875
- w_fc2: float32 [4096, 1024], P(('stream', 'clip')), may hold values from -0.09375 to 0.09375
- norm1_gain: float32 [1024], P(('stream', 'clip')), may hold values from 0.1 to 1.9
- norm2_gain: float32 [1024], P(('stream', 'clip')), may hold values from 0.1 to 1.9
- clip_index: int32 [16384], P(('stream', 'clip')), may hold values from -1 to 4, as said below
- frame_index: int32 [16384], P(('stream', 'clip')), may hold values from 0 to 15, as said below
- cotangent: bfloat16 [16384, 1024], P(('stream', 'clip')), may hold values from -6 to 6
Outputs:
- output: bfloat16 [16384, 1024], P(('stream', 'clip'))
- input_grad: bfloat16 [16384, 1024], P(('stream', 'clip'))
- grad_qkv: float32 [1024, 3072], P(('stream', 'clip'))
- grad_proj: float32 [1024, 1024], P(('stream', 'clip'))
- grad_fc1: float32 [1024, 4096], P(('stream', 'clip'))
- grad_fc2: float32 [4096, 1024], P(('stream', 'clip'))
- grad_gain1: float32 [1024], P(('stream', 'clip'))
- grad_gain2: float32 [1024], P(('stream', 'clip'))
The draws below stay inside these ranges and needn't reach their ends.
Inputs may be any that keep to these rules, and one draw needn't show every extreme that they name: `clip_index`: each device row holds whole clips of 4 to 16 frames numbered 0, 1, ... in order, then padding marked -1. On stream index 1 a frame is 16 consecutive tokens, starting at a multiple of 16; on stream index 0 it is 2 consecutive tokens, and the row of clip index c holds, in the same order, 2 tokens for every frame of the row of stream index 1 and clip index c, then padding. One of the first two clips of every row has 16 frames. In the first device row of each stream every other clip has 4 frames. `frame_index`: frame of each token within its clip, counted from 0; 0 on padding.
All inputs are finite; a program needn't handle non-finite values.
Results may differ from the reference program's by a relative error of at most 0.012.
The reference program's roundings to bfloat16 on the way count: a program that leaves them out, or rounds other values in their place, can miss the bound.
Values may be sent and summed in bfloat16 or wider, within the bound.
A program may use at most 256 MiB of HBM per device.

```python
import jax
import jax.numpy as jnp
from jax import lax

D = 1024
FF = 4096
H = 16
HD = 64
RT = 16
GW = 4
FA = 2
MINF = 4
MAXF = 16
TOK_DEV = 512
FV = 16
TOKENS = 16384


def clip_layout(key):
    rows = TOKENS // (2 * TOK_DEV)
    frames_row = TOK_DEV // FV
    slots = frames_row // MINF
    count_key, pick_key = jax.random.split(jax.random.fold_in(key, 11))
    counts = jax.random.randint(count_key, (rows, slots), MINF, MAXF + 1)
    counts = jnp.where(jnp.arange(rows)[:, None] == 0, MINF, counts)
    pick = jax.random.randint(pick_key, (rows, 1), 0, 2)
    counts = jnp.where(jnp.arange(slots)[None, :] == pick, MAXF, counts)
    ends = jnp.cumsum(counts, axis=1)
    starts = ends - counts
    kept = ends <= frames_row
    place = jnp.arange(frames_row)[None, :, None]
    inside = kept[:, None, :] & (starts[:, None, :] <= place) & (place < ends[:, None, :])
    filled = jnp.any(inside, axis=2)
    number = jnp.sum(jnp.where(inside, jnp.arange(slots)[None, None, :], 0), axis=2)
    offset = jnp.sum(jnp.where(inside, place - starts[:, None, :], 0), axis=2)
    frame_clip = jnp.where(filled, number, -1).astype(jnp.int32)
    frame_num = offset.astype(jnp.int32)
    spare = TOK_DEV - frames_row * FA
    cond_clip = jnp.concatenate([jnp.repeat(frame_clip, FA, axis=1), jnp.full((rows, spare), -1, jnp.int32)], axis=1)
    cond_frame = jnp.concatenate([jnp.repeat(frame_num, FA, axis=1), jnp.zeros((rows, spare), jnp.int32)], axis=1)
    visual_clip = jnp.repeat(frame_clip, FV, axis=1)
    visual_frame = jnp.repeat(frame_num, FV, axis=1)
    clips = jnp.concatenate([cond_clip.reshape(-1), visual_clip.reshape(-1)]).astype(jnp.int32)
    frames = jnp.concatenate([cond_frame.reshape(-1), visual_frame.reshape(-1)]).astype(jnp.int32)
    return (clips, frames)


def draw_clip_index(key, part):
    clips, frames = clip_layout(key)
    return clips


def draw_frame_index(key, part):
    clips, frames = clip_layout(key)
    return frames


def levels(key, dims, cuts, low, top_value):
    level = 1.0
    for axis_at, shards_of in cuts:
        steps = jax.random.uniform(jax.random.fold_in(jax.random.fold_in(key, 6), axis_at), (shards_of,), jnp.float32, low / len(cuts), top_value / len(cuts))
        level = level * jnp.repeat(jnp.exp(steps), dims[axis_at] // shards_of).reshape((-1,) + (1,) * (len(dims) - 1 - axis_at))
    return level


def bell_draw(rng, shape, scale, limit, shards=(), dtype=jnp.bfloat16):
    loudness = levels(rng, shape, shards, -0.22, 0.18) if shards else 1.0
    values = jax.random.normal(rng, shape, jnp.float32) * scale * loudness
    return jnp.minimum(jnp.maximum(values, -limit), limit).astype(dtype)


def setup_inputs(seed: int = 0) -> dict:
    key_of = jax.random.split(jax.random.key(seed), 11)
    return {
        "tokens": bell_draw(key_of[0], (TOKENS, D), 1.0, 6.0, ((0, 32),)),
        "w_qkv": bell_draw(key_of[1], (D, 3 * D), D ** -0.5, 0.1875, ((0, 32),), jnp.float32),
        "w_proj": bell_draw(key_of[2], (D, D), (D // 16) ** -0.5, 0.75, ((0, 32),), jnp.float32),
        "w_fc1": bell_draw(key_of[3], (D, FF), D ** -0.5, 0.1875, ((0, 32),), jnp.float32),
        "w_fc2": bell_draw(key_of[4], (FF, D), FF ** -0.5, 0.09375, ((0, 32),), jnp.float32),
        "norm1_gain": jnp.clip(1.0 + 0.18 * jax.random.normal(key_of[5], (D,), jnp.float32), 0.1, 1.9),
        "norm2_gain": jnp.clip(1.0 + 0.18 * jax.random.normal(key_of[6], (D,), jnp.float32), 0.1, 1.9),
        "clip_index": draw_clip_index(jax.random.fold_in(key_of[10], 71), 0),
        "frame_index": draw_frame_index(jax.random.fold_in(key_of[10], 71), 0),
        "cotangent": bell_draw(key_of[9], (TOKENS, D), 1.0, 6.0, ((0, 32),)),
    }


EPSILON = 1e-06
THETA = 10000.0
MASKED = -1e+30
HIGH = lax.Precision.HIGHEST

@jax.custom_vjp
def low(v):
    return lax.optimization_barrier(v.astype(jnp.bfloat16)).astype(jnp.float32)

@jax.custom_vjp
def low_back(v):
    return v

def low_keep(v):
    return (low(v), None)

def low_pass(kept, grad):
    return (grad,)

def back_keep(v):
    return (v, None)

def back_low(kept, grad):
    return (low(grad),)
low.defvjp(low_keep, low_pass)
low_back.defvjp(back_keep, back_low)

def frequencies(width):
    counter = jnp.arange(width // 2).astype(jnp.float32)
    return jnp.power(THETA, -2.0 * counter / width)

def angle_sets(frames, visual_flag, rows):
    place = jnp.arange(rows)
    inner = place % FV
    down_pos = inner // GW * visual_flag
    across_pos = inner % GW * visual_flag
    side = (HD - RT) // 2
    time_angles = frames.astype(jnp.float32)[:, None] * frequencies(RT)[None, :]
    down_angles = down_pos.astype(jnp.float32)[:, None] * frequencies(side)[None, :]
    across_angles = across_pos.astype(jnp.float32)[:, None] * frequencies(side)[None, :]
    return (time_angles, down_angles, across_angles)

def rotate(block, angles):
    half = block.shape[-1] // 2
    cosine = jnp.cos(angles)[:, None, :]
    sine = jnp.sin(angles)[:, None, :]
    first = block[..., :half]
    second = block[..., half:]
    return jnp.concatenate([first * cosine - second * sine, first * sine + second * cosine], axis=-1)

def rotary(flat, sets, sign):
    rows = flat.shape[0]
    block = flat.reshape(rows, flat.shape[1] // HD, HD)
    side = (HD - RT) // 2
    pieces = (block[..., :RT], block[..., RT:RT + side], block[..., RT + side:])
    turned = [rotate(piece, sign * angles) for piece, angles in zip(pieces, sets)]
    return jnp.concatenate(turned, axis=-1).reshape(rows, -1)

def layernorm(values, gain):
    centred = values - lax.optimization_barrier(jnp.mean(values, axis=-1, keepdims=True))
    inverse = lax.rsqrt(lax.optimization_barrier(jnp.mean(centred * centred, axis=-1, keepdims=True)) + EPSILON)
    return centred * inverse * gain

def local_mask(clips, frames):
    rows = clips.shape[0]
    same = (clips[:, None] == clips[None, :]) & (clips[:, None] >= 0) & (frames[None, :] <= frames[:, None])
    return same | (jnp.arange(rows)[:, None] == jnp.arange(rows)[None, :])

def cross_mask(clips, frames, far_clips, far_frames):
    return (clips[:, None] == far_clips[None, :]) & (clips[:, None] >= 0) & (far_frames[None, :] <= frames[:, None])

def attend(queries, key_rows, values, allowed):
    rows = queries.shape[0]
    query_heads = queries.reshape(rows, H, HD)
    key_heads = key_rows.reshape(-1, H, HD)
    value_heads = values.reshape(-1, H, HD)
    scores = jnp.einsum('qhd,khd->hqk', query_heads, key_heads, precision=HIGH) * HD ** (-0.5)
    scores = low_back(scores)
    scores = jnp.where(allowed[None], scores, MASKED)
    peak = lax.optimization_barrier(jnp.max(scores, axis=-1, keepdims=True))
    weights = jnp.exp(scores - peak)
    probs = low(weights / lax.optimization_barrier(jnp.sum(weights, axis=-1, keepdims=True)))
    mixed = jnp.einsum('hqk,khd->qhd', probs, value_heads, precision=HIGH).reshape(rows, H * HD)
    return low(low_back(mixed))

def layer_pair(block, lowered):
    values_in, clips, frames = block
    full_qkv, full_proj, full_fc1, full_fc2, gain_one, gain_two = lowered
    rows = values_in.shape[1]
    normed = low(layernorm(values_in, gain_one))
    projected = low_back(jnp.matmul(normed, full_qkv, precision=HIGH))
    query_all = projected[..., :D]
    key_all = projected[..., D:2 * D]
    value_all = low(projected[..., 2 * D:])
    sets = [angle_sets(frames[0], 0, rows), angle_sets(frames[1], 1, rows)]
    turned_q = [low(rotary(query_all[side_index], sets[side_index], 1.0)) for side_index in range(2)]
    turned_k = [low(rotary(key_all[side_index], sets[side_index], 1.0)) for side_index in range(2)]
    both_keys = jnp.concatenate([turned_k[0], turned_k[1]], axis=0)
    both_values = jnp.concatenate([value_all[0], value_all[1]], axis=0)
    cond_allowed = jnp.concatenate([local_mask(clips[0], frames[0]), cross_mask(clips[0], frames[0], clips[1], frames[1])], axis=1)
    cond_out = attend(turned_q[0], both_keys, both_values, cond_allowed)
    visual_allowed = jnp.concatenate([cross_mask(clips[1], frames[1], clips[0], frames[0]), local_mask(clips[1], frames[1])], axis=1)
    visual_out = attend(turned_q[1], both_keys, both_values, visual_allowed)
    mixed = jnp.stack([cond_out, visual_out])
    hidden_one = values_in + low_back(jnp.matmul(mixed, full_proj, precision=HIGH))
    normed_two = low(layernorm(hidden_one, gain_two))
    inner = low_back(jnp.matmul(normed_two, full_fc1, precision=HIGH))
    active = low(jax.nn.gelu(inner, approximate=False))
    return hidden_one + low_back(jnp.matmul(active, full_fc2, precision=HIGH))

def reference(tokens, w_qkv, w_proj, w_fc1, w_fc2, norm1_gain, norm2_gain, clip_index, frame_index, cotangent):
    pairs = TOKENS // (2 * TOK_DEV)

    def to_pairs(array):
        return jnp.swapaxes(array.reshape((2, pairs, TOK_DEV) + array.shape[1:]), 0, 1)

    def from_pairs(array):
        return jnp.swapaxes(array, 0, 1).reshape((TOKENS,) + array.shape[3:])
    clips = to_pairs(clip_index)
    frames = to_pairs(frame_index)

    def forward(values_in, wq, wp, wone, wtwo, gone, gtwo):
        lowered = (low(wq), low(wp), low(wone), low(wtwo), low(gone), low(gtwo))
        step = jax.checkpoint(lambda block: layer_pair(block, lowered))
        return lax.map(step, (values_in, clips, frames))
    result, pull = jax.vjp(forward, to_pairs(tokens.astype(jnp.float32)), w_qkv, w_proj, w_fc1, w_fc2, norm1_gain, norm2_gain)
    grads = pull(to_pairs(cotangent.astype(jnp.float32)))
    return (from_pairs(result).astype(jnp.bfloat16), from_pairs(grads[0]).astype(jnp.bfloat16), grads[1], grads[2], grads[3], grads[4], grads[5], grads[6])
```

```python
import jax
import jax.numpy as jnp
from jax import lax
from jax.experimental import pallas as pl
from jax.experimental.pallas import tpu as pltpu
from jax.sharding import PartitionSpec as P

HD = 64
RT = 16
GW = 4
FA = 2
FV = 16


EPSILON = 1e-06
THETA = 10000.0
MASKED = -1e30
LOG_THETA = 9.210340371976184
VMEM_LIMIT = 63 * 1024 * 1024


def shifted(value, axis, steps):
    count = lax.axis_size(axis)
    initial, last = (max(0, -steps), min(count, count - steps))
    return lax.ppermute(value, axis, [(source, source + steps) for source in range(initial, last)])


def frequencies(width):
    counter = jnp.arange(width // 2).astype(jnp.float32)
    return jnp.power(THETA, -2.0 * counter / width)


def angle_sets(frames, visual_flag, rows):
    place = jnp.arange(rows)
    inner = place % FV
    down_pos = inner // GW * visual_flag
    across_pos = inner % GW * visual_flag
    side = (HD - RT) // 2
    time_angles = frames.astype(jnp.float32)[:, None] * frequencies(RT)[None, :]
    down_angles = down_pos.astype(jnp.float32)[:, None] * frequencies(side)[None, :]
    across_angles = across_pos.astype(jnp.float32)[:, None] * frequencies(side)[None, :]
    return (time_angles, down_angles, across_angles)


def rotate(block, angles):
    half = block.shape[-1] // 2
    cosine = jnp.cos(angles)[:, None, :]
    sine = jnp.sin(angles)[:, None, :]
    first = block[..., :half]
    second = block[..., half:]
    return jnp.concatenate(
        [first * cosine - second * sine, first * sine + second * cosine], axis=-1
    )


def rotary(flat, sets, sign):
    rows = flat.shape[0]
    block = flat.reshape(rows, flat.shape[1] // HD, HD)
    side = (HD - RT) // 2
    pieces = (block[..., :RT], block[..., RT : RT + side], block[..., RT + side :])
    turned = [rotate(piece, sign * angles) for piece, angles in zip(pieces, sets)]
    return jnp.concatenate(turned, axis=-1).reshape(rows, -1)


def normalize(values, gain):
    centred = values - jnp.mean(values, axis=-1, keepdims=True)
    inverse = lax.rsqrt(jnp.mean(centred * centred, axis=-1, keepdims=True) + EPSILON)
    unit = centred * inverse
    return (unit * gain, unit, inverse)


def norm_back(grad_out, gain, unit, inverse):
    scaled = grad_out * gain
    centred = (
        scaled
        - jnp.mean(scaled, axis=-1, keepdims=True)
        - unit * jnp.mean(scaled * unit, axis=-1, keepdims=True)
    )
    return (inverse * centred, jnp.sum(grad_out * unit, axis=0))


def local_mask(clips, frames):
    rows = clips.shape[0]
    same = (
        (clips[:, None] == clips[None, :])
        & (clips[:, None] >= 0)
        & (frames[None, :] <= frames[:, None])
    )
    return same | (jnp.arange(rows)[:, None] == jnp.arange(rows)[None, :])


def cross_mask(clips, frames, far_clips, far_frames):
    return (
        (clips[:, None] == far_clips[None, :])
        & (clips[:, None] >= 0)
        & (far_frames[None, :] <= frames[:, None])
    )


def times_transpose(left, right):
    return lax.dot_general(
        left, right, (((1,), (1,)), ((), ())), preferred_element_type=jnp.float32
    )


def transpose_times(left, right):
    return lax.dot_general(
        left, right, (((0,), (0,)), ((), ())), preferred_element_type=jnp.float32
    )


def head_scores(query_part, key_part, allowed):
    query_heads = query_part.reshape(query_part.shape[0], 2, HD)
    key_heads = key_part.reshape(key_part.shape[0], 2, HD)
    scores = jnp.einsum(
        "qhd,khd->hqk", query_heads, key_heads, preferred_element_type=jnp.float32
    ) * HD ** (-0.5)
    return (jnp.where(allowed[None], scores, MASKED), query_heads, key_heads)


def attend_forward(query_part, key_part, value_part, allowed):
    rows = query_part.shape[0]
    scores, query_heads, key_heads = head_scores(query_part, key_part, allowed)
    peak = jnp.max(scores, axis=-1, keepdims=True)
    weights = jnp.exp(scores - peak)
    total = jnp.sum(weights, axis=-1, keepdims=True)
    probs = (weights / total).astype(jnp.bfloat16)
    value_heads = value_part.reshape(value_part.shape[0], 2, HD)
    mixed = jnp.einsum("hqk,khd->qhd", probs, value_heads, preferred_element_type=jnp.float32)
    return (mixed.reshape(rows, 2 * HD), (peak + jnp.log(total))[..., 0])


def attend_back(query_part, key_part, value_part, grad_part, allowed, log_total):
    rows = query_part.shape[0]
    scores, query_heads, key_heads = head_scores(query_part, key_part, allowed)
    probs = jnp.exp(scores - log_total[..., None])
    value_heads = value_part.reshape(value_part.shape[0], 2, HD)
    grad_heads = grad_part.reshape(rows, 2, HD)
    grad_probs = jnp.einsum(
        "qhd,khd->hqk", grad_heads, value_heads, preferred_element_type=jnp.float32
    )
    centre = jnp.sum(probs * grad_probs, axis=-1, keepdims=True)
    grad_scores = (probs * (grad_probs - centre)).astype(jnp.bfloat16)
    factor = HD ** (-0.5)
    grad_query = (
        jnp.einsum("hqk,khd->qhd", grad_scores, key_heads, preferred_element_type=jnp.float32)
        * factor
    )
    grad_key = (
        jnp.einsum("hqk,qhd->khd", grad_scores, query_heads, preferred_element_type=jnp.float32)
        * factor
    )
    grad_value = jnp.einsum(
        "hqk,qhd->khd", probs.astype(jnp.bfloat16), grad_heads, preferred_element_type=jnp.float32
    )
    key_count = key_part.shape[0]
    return (
        grad_query.reshape(rows, 2 * HD),
        grad_key.reshape(key_count, 2 * HD),
        grad_value.reshape(key_count, 2 * HD),
    )


def column_block(array, group_index):
    return lax.dynamic_slice_in_dim(array, group_index * 2 * HD, 2 * HD, 1)


def join_groups(stacked):
    return jnp.transpose(stacked, (1, 0, 2)).reshape(stacked.shape[1], -1)


def body(
    tokens, w_qkv, w_proj, w_fc1, w_fc2, norm1_gain, norm2_gain, clip_index, frame_index, cotangent
):
    rows = tokens.shape[0]
    width = tokens.shape[1]
    groups = width // (2 * HD)
    visual = lax.axis_index("stream") == 1
    visual_flag = visual.astype(jnp.int32)
    shards = (
        w_qkv.astype(jnp.bfloat16),
        w_proj.astype(jnp.bfloat16),
        w_fc1.astype(jnp.bfloat16),
        w_fc2.astype(jnp.bfloat16),
        norm1_gain.astype(jnp.bfloat16),
        norm2_gain.astype(jnp.bfloat16),
    )
    full_qkv, full_proj, full_fc1, full_fc2, gain_one, gain_two = (
        lax.all_gather(shards[0], ("stream", "clip"), axis=0, tiled=True),
        lax.all_gather(shards[1], ("stream", "clip"), axis=0, tiled=True),
        lax.all_gather(shards[2], ("stream", "clip"), axis=0, tiled=True),
        lax.all_gather(shards[3], ("stream", "clip"), axis=0, tiled=True),
        lax.all_gather(shards[4], ("stream", "clip"), axis=0, tiled=True),
        lax.all_gather(shards[5], ("stream", "clip"), axis=0, tiled=True),
    )
    gain_first = gain_one.astype(jnp.float32)
    gain_second = gain_two.astype(jnp.float32)
    values_in = tokens.astype(jnp.float32)
    normed, unit_one, inverse_one = normalize(values_in, gain_first)
    normed_b = normed.astype(jnp.bfloat16)
    projected = jnp.dot(normed_b, full_qkv, preferred_element_type=jnp.float32)
    sets = angle_sets(frame_index, visual_flag, rows)
    queries = rotary(projected[:, :width], sets, 1.0).astype(jnp.bfloat16)
    key_rows = rotary(projected[:, width : 2 * width], sets, 1.0).astype(jnp.bfloat16)
    values = projected[:, 2 * width :].astype(jnp.bfloat16)
    frames_row = rows // FV
    cond_rows = frames_row * FA
    near_keys, near_values = shifted((key_rows[:cond_rows], values[:cond_rows]), "stream", 1)
    far_keys, far_values = shifted((key_rows, values), "stream", -1)
    clip_seen = clip_index.reshape(frames_row, FV)[:, 0]
    clip_cond = clip_index[:cond_rows].reshape(frames_row, FA)[:, 0]
    frame_seen = frame_index.reshape(frames_row, FV)[:, 0]
    frame_cond = frame_index[:cond_rows].reshape(frames_row, FA)[:, 0]
    frame_clip = jnp.where(visual, clip_seen, clip_cond)
    frame_num = jnp.where(visual, frame_seen, frame_cond)
    partner_cond = (
        cross_mask(clip_index, frame_index, jnp.repeat(frame_clip, FA), jnp.repeat(frame_num, FA))
        & visual
    )
    partner_seen = cross_mask(
        clip_index, frame_index, jnp.repeat(frame_clip, FV), jnp.repeat(frame_num, FV)
    ) & jnp.logical_not(visual)
    allowed = jnp.concatenate(
        [partner_cond, partner_seen, local_mask(clip_index, frame_index)], axis=1
    )
    key_all = jnp.concatenate([near_keys, far_keys, key_rows], axis=0)
    value_all = jnp.concatenate([near_values, far_values, values], axis=0)

    def forward_group(group_index):
        return attend_forward(
            column_block(queries, group_index),
            column_block(key_all, group_index),
            column_block(value_all, group_index),
            allowed,
        )

    mixed_groups, log_totals = lax.map(forward_group, jnp.arange(groups))
    mixed_b = join_groups(mixed_groups).astype(jnp.bfloat16)
    hidden_one = values_in + jnp.dot(mixed_b, full_proj, preferred_element_type=jnp.float32)
    normed_two, unit_two, inverse_two = normalize(hidden_one, gain_second)
    normed_two_b = normed_two.astype(jnp.bfloat16)
    inner = jnp.dot(normed_two_b, full_fc1, preferred_element_type=jnp.float32)
    active, gelu_pull = jax.vjp(lambda given: jax.nn.gelu(given, approximate=False), inner)
    active_b = active.astype(jnp.bfloat16)
    result = hidden_one + jnp.dot(active_b, full_fc2, preferred_element_type=jnp.float32)
    full_qkv, full_proj, full_fc1, full_fc2, gain_one, gain_two = (
        lax.all_gather(shards[0], ("stream", "clip"), axis=0, tiled=True),
        lax.all_gather(shards[1], ("stream", "clip"), axis=0, tiled=True),
        lax.all_gather(shards[2], ("stream", "clip"), axis=0, tiled=True),
        lax.all_gather(shards[3], ("stream", "clip"), axis=0, tiled=True),
        lax.all_gather(shards[4], ("stream", "clip"), axis=0, tiled=True),
        lax.all_gather(shards[5], ("stream", "clip"), axis=0, tiled=True),
    )
    gain_first = gain_one.astype(jnp.float32)
    gain_second = gain_two.astype(jnp.float32)
    grad_out = cotangent.astype(jnp.float32)
    grad_fc2 = transpose_times(active_b, cotangent)
    grad_active = times_transpose(cotangent, full_fc2)
    grad_inner = gelu_pull(grad_active)[0].astype(jnp.bfloat16)
    grad_fc1 = transpose_times(normed_two_b, grad_inner)
    grad_normed_two = times_transpose(grad_inner, full_fc1)
    back_two, grad_gain2 = norm_back(grad_normed_two, gain_second, unit_two, inverse_two)
    grad_hidden = grad_out + back_two
    grad_attn = grad_hidden.astype(jnp.bfloat16)
    grad_proj = transpose_times(mixed_b, grad_attn)
    grad_mixed = times_transpose(grad_attn, full_proj).astype(jnp.bfloat16)

    def backward_group(inputs):
        group_index, log_total = inputs
        return attend_back(
            column_block(queries, group_index),
            column_block(key_all, group_index),
            column_block(value_all, group_index),
            column_block(grad_mixed, group_index),
            allowed,
            log_total,
        )

    grad_q_groups, grad_k_groups, grad_v_groups = lax.map(
        backward_group, (jnp.arange(groups), log_totals)
    )
    grad_queries = join_groups(grad_q_groups)
    grad_key_all = join_groups(grad_k_groups)
    grad_value_all = join_groups(grad_v_groups)
    outer = cond_rows + rows
    cond_keys_back, cond_values_back = (
        shifted(grad_key_all[:cond_rows].astype(jnp.bfloat16), "stream", -1).astype(jnp.float32),
        shifted(grad_value_all[:cond_rows].astype(jnp.bfloat16), "stream", -1).astype(jnp.float32),
    )
    seen_keys_back, seen_values_back = (
        shifted(grad_key_all[cond_rows:outer].astype(jnp.bfloat16), "stream", 1).astype(
            jnp.float32
        ),
        shifted(grad_value_all[cond_rows:outer].astype(jnp.bfloat16), "stream", 1).astype(
            jnp.float32
        ),
    )
    filler = jnp.zeros((rows - cond_rows, width), jnp.float32)
    grad_keys = (
        grad_key_all[outer:] + seen_keys_back + jnp.concatenate([cond_keys_back, filler], axis=0)
    )
    grad_values = (
        grad_value_all[outer:]
        + seen_values_back
        + jnp.concatenate([cond_values_back, filler], axis=0)
    )
    grad_projected = jnp.concatenate(
        [rotary(grad_queries, sets, -1.0), rotary(grad_keys, sets, -1.0), grad_values], axis=1
    ).astype(jnp.bfloat16)
    grad_qkv = transpose_times(normed_b, grad_projected)
    grad_normed = times_transpose(grad_projected, full_qkv)
    back_one, grad_gain1 = norm_back(grad_normed, gain_first, unit_one, inverse_one)
    input_grad = (grad_hidden + back_one).astype(jnp.bfloat16)
    sums = (
        lax.psum_scatter(grad_qkv, ("stream", "clip"), scatter_dimension=0, tiled=True),
        lax.psum_scatter(grad_proj, ("stream", "clip"), scatter_dimension=0, tiled=True),
        lax.psum_scatter(grad_fc1, ("stream", "clip"), scatter_dimension=0, tiled=True),
        lax.psum_scatter(grad_fc2, ("stream", "clip"), scatter_dimension=0, tiled=True),
        lax.psum_scatter(grad_gain1, ("stream", "clip"), scatter_dimension=0, tiled=True),
        lax.psum_scatter(grad_gain2, ("stream", "clip"), scatter_dimension=0, tiled=True),
    )
    return (
        result.astype(jnp.bfloat16),
        input_grad,
        sums[0],
        sums[1],
        sums[2],
        sums[3],
        sums[4],
        sums[5],
    )


MESH = pl.DeviceIdType.MESH
F32 = jnp.float32
BF16 = jnp.bfloat16
MB = 1 << 20
NU = 12
ORDER = (8, 9, 10, 11, 4, 5, 6, 7, 3, 0, 1, 2)
WIDE = 1024
NEG = -1e30


class Place:
    def __init__(self):
        self.y = lax.axis_index("stream")
        clip = lax.axis_index("clip")
        self.z, self.x, self.c = clip // 4, (clip // 2) % 2, clip % 2
        self.X = self.dev(self.y, self.z, 1 - self.x, self.c)
        self.Y = self.dev(1 - self.y, self.z, self.x, self.c)
        self.C = self.dev(self.y, self.z, self.x, 1 - self.c)

    def dev(self, y, z, x, c):
        return (y, z * 4 + x * 2 + c)

    def up(self, d):
        return lax.rem(self.z + d, 4)

    def above(self, d):
        return self.dev(self.y, self.up(d), self.x, self.c)

    def peers(self):
        return [self.X, self.Y, self.C] + [self.above(d) for d in (1, 2, 3)]


class Link:
    def __init__(self, place, sent, got):
        self.p, self.sent, self.got, self.open = place, sent, got, []

    def copy(self, u, slot, src, dst, to):
        return pltpu.make_async_remote_copy(
            src_ref=src,
            dst_ref=dst,
            send_sem=self.sent.at[u, slot],
            recv_sem=self.got.at[u, slot],
            device_id=to,
            device_id_type=MESH,
        )

    def send(self, u, slot, src, dst, to):
        c = self.copy(u, slot, src, dst, to)
        c.start()
        self.open.append((u, c))

    def recv(self, u, slot, dst):
        self.copy(u, slot, dst, dst, self.p.X).wait_recv()

    def flush(self, unit=None):
        rest = []
        for u, c in self.open:
            if unit is None or u == unit:
                c.wait_send()
            else:
                rest.append((u, c))
        self.open = rest


class Gather(Link):
    def __init__(self, place, own, whole, sent, got):
        super().__init__(place, sent, got)
        self.own, self.W = own, whole

    def first(self, u):
        p = self.p
        me = self.W.at[u, p.y, p.z, p.x, p.c]
        for d in (1, 2, 3):
            self.send(u, d - 1, self.own.at[u], me, p.above(d))

    def second(self, u):
        p = self.p
        me = self.W.at[u, p.y, p.z, p.x, p.c]
        self.send(u, 3, self.own.at[u], me, p.X)
        self.send(u, 7, self.own.at[u], me, p.Y)

    def g1(self, u):
        p, W = self.p, self.W
        for d in (1, 2, 3):
            b = W.at[u, p.y, p.up(4 - d), p.x, p.c]
            self.recv(u, d - 1, b)
            self.send(u, 3 + d, b, b, p.X)
            self.send(u, 7 + d, b, b, p.Y)
        b = W.at[u, p.y, :, p.x, p.c]
        self.send(u, 13, b, b, p.C)

    def g2(self, u):
        p, W = self.p, self.W
        for k in range(4):
            z = p.up(4 - k)
            self.recv(u, 3 + k, W.at[u, p.y, z, 1 - p.x, p.c])
            self.recv(u, 7 + k, W.at[u, 1 - p.y, z, p.x, p.c])
        b = W.at[u, p.y, pl.ds(0, 2), 1 - p.x, p.c]
        self.send(u, 11, b, b, p.Y)
        b = W.at[u, 1 - p.y, pl.ds(2, 2), p.x, p.c]
        self.send(u, 12, b, b, p.X)
        b = W.at[u, p.y, :, 1 - p.x, p.c]
        self.send(u, 14, b, b, p.C)
        b = W.at[u, 1 - p.y, :, p.x, p.c]
        self.send(u, 15, b, b, p.C)

    def g3(self, u):
        p, W = self.p, self.W
        self.recv(u, 11, W.at[u, 1 - p.y, pl.ds(0, 2), 1 - p.x, p.c])
        self.recv(u, 12, W.at[u, 1 - p.y, pl.ds(2, 2), 1 - p.x, p.c])
        b = W.at[u, 1 - p.y, :, 1 - p.x, p.c]
        self.send(u, 16, b, b, p.C)

    def g4(self, u):
        p, W = self.p, self.W
        o = 1 - p.c
        self.recv(u, 13, W.at[u, p.y, :, p.x, o])
        self.recv(u, 14, W.at[u, p.y, :, 1 - p.x, o])
        self.recv(u, 15, W.at[u, 1 - p.y, :, p.x, o])
        self.recv(u, 16, W.at[u, 1 - p.y, :, 1 - p.x, o])


class Scatter(Link):
    def __init__(self, place, part, land, out, sent, got):
        super().__init__(place, sent, got)
        self.part, self.land, self.out = part, land, out

    def col(self, i, a, b):
        return self.land(i, (a * 2 + b) * 4, 4)

    def blk(self, i, a, b, z):
        return self.land(i, (a * 2 + b) * 4 + z, 1).at[0]

    def add(self, n, dst, *srcs):
        @pl.loop(0, n)
        def _(k):
            t = srcs[0](k)[...].astype(F32)
            for r in srcs[1:]:
                t = t + r(k)[...].astype(F32)
            d = dst(k)
            d[...] = t.astype(d.dtype)

    def r0(self, i):
        p = self.p
        y, x, o, q = p.y, p.x, 1 - p.c, self.part(i)
        for k, (a, b) in enumerate(((1 - y, 1 - x), (1 - y, x), (y, 1 - x), (y, x))):
            self.send(i, k, q.at[a, :, b, o], self.col(i, a, b), p.C)

    def r1(self, i):
        p = self.p
        y, x, c, q = p.y, p.x, p.c, self.part(i)
        self.recv(i, 0, self.col(i, 1 - y, 1 - x))
        own = lambda k: q.at[1 - y, k, 1 - x, c]
        self.add(4, own, own, lambda k: self.blk(i, 1 - y, 1 - x, k))
        self.send(i, 4, q.at[1 - y, pl.ds(0, 2), 1 - x, c], self.land(i, 16, 2), p.X)
        self.send(i, 5, q.at[1 - y, pl.ds(2, 2), 1 - x, c], self.land(i, 18, 2), p.Y)

    def r2(self, i):
        p = self.p
        y, x, c, q = p.y, p.x, p.c, self.part(i)
        self.recv(i, 1, self.col(i, 1 - y, x))
        self.recv(i, 2, self.col(i, y, 1 - x))
        ny = lambda k: q.at[1 - y, k, x, c]
        my = lambda k: self.blk(i, 1 - y, x, k)
        nx = lambda k: q.at[y, k, 1 - x, c]
        mx = lambda k: self.blk(i, y, 1 - x, k)
        self.add(2, lambda k: ny(k + 2), lambda k: ny(k + 2), lambda k: my(k + 2))
        self.add(2, nx, nx, mx)
        self.recv(i, 4, self.land(i, 16, 2))
        self.add(2, ny, ny, my, lambda k: self.land(i, 16 + k, 1).at[0])
        self.send(i, 6, q.at[1 - y, :, x, c], self.land(i, 28, 4), p.Y)
        self.recv(i, 5, self.land(i, 18, 2))
        self.add(
            2,
            lambda k: nx(k + 2),
            lambda k: nx(k + 2),
            lambda k: mx(k + 2),
            lambda k: self.land(i, 18 + k, 1).at[0],
        )
        self.send(i, 7, q.at[y, :, 1 - x, c], self.land(i, 24, 4), p.X)

    def r3(self, i):
        p = self.p
        y, x, c, q = p.y, p.x, p.c, self.part(i)
        self.recv(i, 3, self.col(i, y, x))
        self.recv(i, 6, self.land(i, 28, 4))
        self.recv(i, 7, self.land(i, 24, 4))
        own = lambda k: q.at[y, k, x, c]
        self.add(
            4,
            own,
            own,
            lambda k: self.blk(i, y, x, k),
            lambda k: self.land(i, 28 + k, 1).at[0],
            lambda k: self.land(i, 24 + k, 1).at[0],
        )
        for d in (1, 2, 3):
            self.send(i, 8 + d, q.at[y, p.up(d), x, c], self.land(i, 19 + d, 1).at[0], p.above(d))

    def r4(self, i):
        p = self.p
        q = self.part(i)
        for d in (1, 2, 3):
            self.recv(i, 8 + d, self.land(i, 19 + d, 1).at[0])
        t = q[p.y, p.z, p.x, p.c].astype(F32)
        for d in (1, 2, 3):
            t = t + self.land(i, 19 + d, 1)[0].astype(F32)
        self.out(i)[...] = t


def unit_rows(v):
    centred = v - jnp.mean(v, axis=-1, keepdims=True)
    inverse = lax.rsqrt(jnp.mean(centred * centred, axis=-1, keepdims=True) + EPSILON)
    return centred * inverse, inverse


def back_rows(d, gain, unit, inverse):
    e = d * gain
    return inverse * (
        e - jnp.mean(e, axis=-1, keepdims=True) - unit * jnp.mean(e * unit, axis=-1, keepdims=True)
    )


def dot(a, b):
    return jnp.dot(a, b, preferred_element_type=F32)


def rope_lane(shape):
    lane = lax.broadcasted_iota(jnp.int32, shape, 1)
    return lane, lane % 32


def layer_kernel(
    x, cot, own, gown, codes,
    out_hbm, xg_hbm, gw, gg, spill,
    W, G, Q, K, V, ob, dob, h1, a2, gbuf, gp, PS, obuf,
    bias, cbias, ct, st, lse, dk, dv, gain, ggp, gland,
    ss, rs, gss, grs, sss, srs, mss, mrs, xss, xrs, loc, credit,
):
    p = Place()
    vis = p.y == 1
    rows = x.shape[0]
    C = Q.shape[0] - rows
    R = rows + C
    W3 = W.reshape(NU, WIDE, WIDE)
    Wf = W.reshape(NU, 64, 16, WIDE) if False else W.reshape(NU, 32, 32, WIDE)
    gb = gbuf.reshape(4, rows, WIDE)
    P3 = PS.reshape(4, WIDE, WIDE)
    G3 = gbuf.reshape(2, WIDE, WIDE)

    def slot(i):
        return (0, i) if i < 4 else (1, i - 4) if i < 6 else (0, i - 6) if i < 10 else (1, i - 10)

    def part(i):
        k, n = slot(i)
        return (PS, gbuf)[k].at[n]

    def part3(i):
        k, n = slot(i)
        return (P3, G3)[k].at[n]

    def land(i, at, n):
        u = i if i < 4 else i + 4 if i < 8 else i - 8
        return Wf.at[u, pl.ds(at, n)]

    ga = Gather(p, own, W, ss, rs)
    mini = Gather(p, gown, G, gss, grs)
    sc = Scatter(p, part, land, lambda i: gw.at[ORDER[i]], sss, srs)
    msc = Scatter(
        p, lambda i: ggp.at[0], lambda i, at, n: gland.at[pl.ds(at, n)], lambda i: gg, mss, mrs
    )

    bar = pltpu.get_barrier_semaphore()
    for q in p.peers():
        pl.semaphore_signal(bar, inc=1, device_id=q, device_id_type=MESH)
    pl.semaphore_wait(bar, 6)

    def place_own():
        for u in range(NU):
            W[u, p.y, p.z, p.x, p.c] = own[u]
        G[0, p.y, p.z, p.x, p.c] = gown[0]

    def gains():
        for y in range(2):
            for z in range(4):
                t = G[0, y, z, 0, 0] + G[0, y, z, 0, 1] + G[0, y, z, 1, 0] + G[0, y, z, 1, 1]
                gain[:, (y * 4 + z) * 128 : (y * 4 + z + 1) * 128] = t

    def column(row, at):
        return jnp.transpose(jnp.broadcast_to(codes[row : row + 1, at : at + 128], (128, 128)))

    def tables():
        side = (HD - RT) // 2
        for at in range(0, R, 128):
            n = min(128, R - at)
            shape = (n, 128)
            lane, i = rope_lane(shape)
            t = column(3, at)[:n]
            place = lax.broadcasted_iota(jnp.int32, shape, 0) + (at - C)
            inner = place % FV
            own_row = (place >= 0) & vis
            down = jnp.where(own_row, inner // GW, 0).astype(F32)
            across = jnp.where(own_row, inner % GW, 0).astype(F32)
            first, second = RT // 2, RT // 2 + side // 2
            k = jnp.where(i < first, i, jnp.where(i < second, i - first, i - second)).astype(F32)
            n_at = jnp.where(i < first, t, jnp.where(i < second, down, across))
            width = jnp.where(i < first, float(RT), float(side))
            angle = n_at * jnp.exp(k / width * (-2.0 * LOG_THETA))
            ct[at : at + n, :] = jnp.cos(angle)
            sine = jnp.sin(angle)
            st[at : at + n, :] = jnp.where(lane < 64, -sine, sine)

    def biases():
        for at in range(0, R, 128):
            n = min(128, R - at)
            kc = column(0, at)[:n]
            key = lax.broadcasted_iota(jnp.int32, (n, 128), 0) + at
            lane = lax.broadcasted_iota(jnp.int32, (n, 128), 1)
            for qa in range(0, rows, 128):
                lo = codes[1:2, C + qa : C + qa + 128]
                hi = codes[2:3, C + qa : C + qa + 128]
                ok = ((kc >= lo) & (kc <= hi)) | (key == lane + (qa + C))
                bias[at : at + n, qa : qa + 128] = jnp.where(ok, 0.0, NEG)
            lo, hi = codes[4:5, 0:128], codes[5:6, 0:128]
            ok = ((kc >= lo) & (kc <= hi)) | (key == lane % 64)
            cbias[at : at + n, :] = jnp.where(ok, 0.0, NEG)

    def norm_one():
        @pl.loop(0, rows // 64)
        def _(k):
            r = pl.ds(pl.multiple_of(k * 64, 64), 64)
            unit, _ = unit_rows(x[r, :].astype(F32))
            gp[0, r, :] = (unit * gain[0:1, :]).astype(BF16)

    def turned(v, rowset, sign):
        return v * ct[rowset, :] + pltpu.roll(v, 64, 1) * (st[rowset, :] * sign)

    def project(u):
        dst = (Q, K, V)[u]

        @pl.loop(0, WIDE // 256)
        def _(k):
            at = pl.multiple_of(k * 256, 256)
            v = dot(gp[0], W3[u, :, pl.ds(at, 256)])
            for h in range(2):
                part_v = v[:, h * 128 : (h + 1) * 128]
                if u < 2:
                    part_v = turned(part_v, slice(C, R), 1.0)
                dst[C:R, pl.ds(pl.multiple_of(at + h * 128, 128), 128)] = part_v.astype(BF16)

    def xcopy(k, src, dst):
        return pltpu.make_async_remote_copy(
            src_ref=src, dst_ref=dst, send_sem=xss.at[k], recv_sem=xrs.at[k],
            device_id=p.Y, device_id_type=MESH,
        )

    def to_visual(k, ref):
        @pl.when(p.y == 0)
        def _():
            xcopy(k, ref.at[pl.ds(C, C)], ref.at[pl.ds(0, C)]).start()

    def at_visual(k, ref):
        @pl.when(vis)
        def _():
            xcopy(k, ref.at[pl.ds(C, C)], ref.at[pl.ds(0, C)]).wait_recv()

    def from_visual(k, ref):
        @pl.when(vis)
        def _():
            xcopy(k, ref.at[pl.ds(0, C)], ref.at[pl.ds(C, C)]).start()

    def at_cond(k, ref):
        @pl.when(p.y == 0)
        def _():
            xcopy(k, ref.at[pl.ds(0, C)], ref.at[pl.ds(C, C)]).wait_recv()

    def sent_to_visual(*pairs):
        for k, ref in pairs:
            @pl.when(p.y == 0)
            def _(k=k, ref=ref):
                xcopy(k, ref.at[pl.ds(C, C)], ref.at[pl.ds(0, C)]).wait_send()

    def xflush():
        sent_to_visual((4, dob))
        for k, ref in ((3, ob), (5, Q), (6, K), (7, V)):
            @pl.when(vis)
            def _(k=k, ref=ref):
                xcopy(k, ref.at[pl.ds(0, C)], ref.at[pl.ds(C, C)]).wait_send()

    blocks = [(0, C, R)] + [(C + 128 * b, 128, C + 128 * (b + 1)) for b in range(rows // 128)]

    def masks():
        lane, _ = rope_lane((1, 128))
        even = (lane % 64) < 32
        first = lane < 64
        return even, first

    def stack(v, m, scale):
        zero = jnp.zeros_like(v)
        both = jnp.concatenate([jnp.where(m, v, zero), jnp.where(m, zero, v)], axis=0)
        return both * jnp.asarray(scale, BF16) if scale != 1.0 else both

    def scores(b, q0, nq, n, k, rq):
        s = lax.dot_general(k[:n], rq, (((1,), (1,)), ((), ())), preferred_element_type=F32)
        if b == 0:
            return s + cbias[0:n, :]
        t = bias[0:n, q0 - C : q0 - C + nq]
        return s + jnp.concatenate([t, t], axis=1)

    def attend(lo, hi):
        @pl.when(vis)
        def _():
            even, first = masks()

            @pl.loop(lo, hi)
            def _(pair):
                cols = pl.ds(pl.multiple_of(pair * 128, 128), 128)
                k, v = K[:, cols], V[:, cols]
                for b, (q0, nq, n) in enumerate(blocks):
                    rq = stack(Q[q0 : q0 + nq, cols], even, HD ** -0.5)
                    s = scores(b, q0, nq, n, k, rq)
                    top = jnp.max(s, axis=0, keepdims=True)
                    e = jnp.exp(s - top)
                    total = jnp.sum(e, axis=0, keepdims=True)
                    prob = (e * (1.0 / total)).astype(BF16)
                    lse[pair, b : b + 1, 0 : 2 * nq] = top + jnp.log(total)
                    o = lax.dot_general(
                        v[:n], prob, (((0,), (0,)), ((), ())), preferred_element_type=F32
                    )
                    o = jnp.transpose(o)
                    ob[q0 : q0 + nq, cols] = jnp.where(first, o[:nq], o[nq:]).astype(BF16)

    def attend_back(lo, hi):
        @pl.when(vis)
        def _():
            even, first = masks()

            @pl.loop(lo, hi)
            def _(pair):
                cols = pl.ds(pl.multiple_of(pair * 128, 128), 128)
                k, v = K[:, cols], V[:, cols]
                for b, (q0, nq, n) in enumerate(blocks):
                    rq = stack(Q[q0 : q0 + nq, cols], even, HD ** -0.5)
                    rd = stack(dob[q0 : q0 + nq, cols], first, 1.0)
                    s = scores(b, q0, nq, n, k, rq)
                    prob = jnp.exp(s - lse[pair, b : b + 1, 0 : 2 * nq])
                    dp = lax.dot_general(
                        v[:n], rd, (((1,), (1,)), ((), ())), preferred_element_type=F32
                    )
                    centre = jnp.sum(prob * dp, axis=0, keepdims=True)
                    ds = (prob * (dp - centre)).astype(BF16)
                    dvn = dot(prob.astype(BF16), rd)
                    dkn = dot(ds, rq)
                    if b == 0:
                        dv[...] = dvn
                        dk[...] = dkn
                    else:
                        dv[0:n, :] += dvn
                        dk[0:n, :] += dkn
                    t = lax.dot_general(
                        k[:n], ds, (((0,), (0,)), ((), ())), preferred_element_type=F32
                    )
                    t = jnp.transpose(t)
                    dq = jnp.where(even, t[:nq], t[nq:]) * HD ** -0.5
                    Q[q0 : q0 + nq, cols] = turned(dq, slice(q0, q0 + nq), -1.0).astype(BF16)
                K[:, cols] = turned(dk[...], slice(0, R), -1.0).astype(BF16)
                V[:, cols] = dv[...].astype(BF16)

    def pad_forward():
        @pl.when(p.y == 0)
        def _():
            ob[2 * C : R, :] = V[2 * C : R, :]

    def pad_back():
        @pl.when(p.y == 0)
        def _():
            Q[2 * C : R, :] = jnp.zeros((R - 2 * C, WIDE), BF16)
            K[2 * C : R, :] = jnp.zeros((R - 2 * C, WIDE), BF16)
            V[2 * C : R, :] = dob[2 * C : R, :]

    def hidden():
        @pl.loop(0, rows // 256)
        def _(k):
            r = pl.ds(pl.multiple_of(k * 256, 256), 256)
            ro = pl.ds(pl.multiple_of(k * 256 + C, 64), 256)
            h1[r, :] = x[r, :].astype(F32) + dot(ob[ro, :], W3[3])

        @pl.loop(0, rows // 64)
        def _(k):
            r = pl.ds(pl.multiple_of(k * 64, 64), 64)
            unit, _ = unit_rows(h1[r, :])
            a2[r, :] = (unit * gain[1:2, :]).astype(BF16)

    def inner(j):
        @pl.loop(0, WIDE // 256)
        def _(k):
            at = pl.ds(pl.multiple_of(k * 256, 256), 256)
            u = dot(a2[...], W3[4 + j, :, at])
            phi = 0.5 + 0.5 * lax.erf(u * 0.7071067811865476)
            gb[j, :, at] = (u * phi).astype(BF16)
            gp[j, :, at] = (phi + u * (jnp.exp(u * u * -0.5) * 0.3989422804014327)).astype(BF16)

    def weight_grad(i, left, right):
        dst = part3(i)

        @pl.loop(0, WIDE // 256)
        def _(k):
            at = pl.ds(pl.multiple_of(k * 256, 256), 256)
            t = lax.dot_general(
                left(at), right(), (((0,), (0,)), ((), ())), preferred_element_type=F32
            )
            dst[at, :] = t.astype(BF16)

    def grad2(j):
        weight_grad(j, lambda at: gb[j, :, at], lambda: cot[...])

    def grad1(j):
        weight_grad(4 + j, lambda at: a2[:, at], lambda: gp[j])

    def du(j):
        @pl.loop(0, WIDE // 256)
        def _(k):
            at = pl.ds(pl.multiple_of(k * 256, 256), 256)
            d = lax.dot_general(
                cot[...], W3[8 + j, at, :], (((1,), (1,)), ((), ())), preferred_element_type=F32
            )
            gp[j, :, at] = (d * gp[j, :, at].astype(F32)).astype(BF16)

    def result():
        @pl.loop(0, WIDE // 256)
        def _(k):
            at = pl.ds(pl.multiple_of(k * 256, 256), 256)
            t = h1[:, at]
            for j in range(4):
                t = t + dot(gb[j], W3[8 + j, :, at])
            obuf[:, at] = t.astype(BF16)

    def hidden_back():
        gain[4:6, :] = jnp.zeros((2, WIDE), F32)

        @pl.loop(0, rows // 256)
        def _(k):
            r = pl.ds(pl.multiple_of(k * 256, 256), 256)
            t = lax.dot_general(
                gp[0, r, :], W3[4], (((1,), (1,)), ((), ())), preferred_element_type=F32
            )
            for j in range(1, 4):
                t = t + lax.dot_general(
                    gp[j, r, :], W3[4 + j], (((1,), (1,)), ((), ())), preferred_element_type=F32
                )
            unit, inverse = unit_rows(h1[r, :])
            gain[5:6, :] += jnp.sum(t * unit, axis=0, keepdims=True)
            t = cot[r, :].astype(F32) + back_rows(t, gain[1:2, :], unit, inverse)
            h1[r, :] = t
            obuf[r, :] = t.astype(BF16)

    def mixed_back():
        @pl.loop(0, WIDE // 256)
        def _(k):
            at = pl.ds(pl.multiple_of(k * 256, 256), 256)
            t = lax.dot_general(
                obuf[...], W3[7, at, :], (((1,), (1,)), ((), ())), preferred_element_type=F32
            )
            dob[C:R, at] = t.astype(BF16)

    def input_back():
        @pl.loop(0, rows // 256)
        def _(k):
            r = pl.ds(pl.multiple_of(k * 256, 256), 256)
            ro = pl.ds(pl.multiple_of(k * 256 + C, 64), 256)
            t = None
            for u, src in enumerate((Q, K, V)):
                d = lax.dot_general(
                    src[ro, :], W3[4 + u], (((1,), (1,)), ((), ())), preferred_element_type=F32
                )
                t = d if t is None else t + d
            unit, inverse = unit_rows(x[r, :].astype(F32))
            gain[4:5, :] += jnp.sum(t * unit, axis=0, keepdims=True)
            t = h1[r, :] + back_rows(t, gain[0:1, :], unit, inverse)
            obuf[r, :] = t.astype(BF16)

    def local(k, src, dst):
        return pltpu.make_async_copy(src, dst, loc.at[k])

    def spill_copy(u):
        return local(u, W.at[u], spill.at[u])

    def reload_copy(u):
        return local(u, spill.at[u], W.at[4 + u])

    def grant(i):
        for q in p.peers():
            pl.semaphore_signal(credit.at[i], inc=1, device_id=q, device_id_type=MESH)

    for u in range(2):
        ga.first(u)
    mini.first(0)
    mini.second(0)
    for u in range(9):
        ga.second(u)
    place_own()
    mini.g1(0)
    mini.g2(0)
    tables()
    mini.g3(0)

    @pl.when(vis)
    def _():
        biases()

    mini.g4(0)
    gains()
    norm_one()

    def gather_step(s):
        if s + 2 < NU:
            ga.first(s + 2)
        if s + 9 < NU:
            ga.second(s + 9)
        if s < NU:
            ga.g1(s)
        if 0 <= s - 1 < NU:
            ga.g2(s - 1)
        if 0 <= s - 2 < NU:
            ga.g3(s - 2)
        if 0 <= s - 3 < NU:
            ga.g4(s - 3)

    for s in range(NU + 3):
        gather_step(s)
        u = s - 3
        if 0 <= u < 4:
            spill_copy(u).start()
        if 0 <= u < 3:
            project(u)
            to_visual(u, (Q, K, V)[u])
        if u == 2:
            for k, ref in enumerate((Q, K, V)):
                at_visual(k, ref)
            attend(0, 4)
        if u == 3:
            attend(4, 8)
            pad_forward()
            from_visual(3, ob)
            at_cond(3, ob)
            hidden()
        if u == 4:
            inner(0)
            grad2(0)
            for k in range(4):
                spill_copy(k).wait()
        if 5 <= u < 8:
            inner(u - 4)
            grad2(u - 4)
        if 8 <= u < 12:
            du(u - 8)
    ga.flush()
    mini.flush()
    for i in range(4):
        grant(i)

    def scatter_open(i):
        pl.semaphore_wait(credit.at[i], 6)
        sc.r0(i)

    def scatter_step(s):
        if s + 1 < NU:
            scatter_open(s + 1)
        if s < NU:
            sc.r1(s)
        if 0 <= s - 1 < NU:
            sc.r2(s - 1)
        if 0 <= s - 2 < NU:
            sc.r3(s - 2)
        if 0 <= s - 3 < NU:
            sc.r4(s - 3)
            sc.flush(s - 3)
            if s - 3 < 4:
                grant(s + 5)

    out_copy = local(4, obuf, out_hbm)
    xg_copy = local(5, obuf, xg_hbm)

    scatter_open(0)
    result()
    out_copy.start()
    for i in range(4, 8):
        grant(i)
    scatter_step(0)
    out_copy.wait()
    hidden_back()
    grad1(0)
    for u in range(4):
        reload_copy(u).start()
    scatter_step(1)
    grad1(1)
    for u in range(4):
        reload_copy(u).wait()
    mixed_back()
    sent_to_visual((0, Q), (1, K), (2, V))
    to_visual(4, dob)
    pad_back()
    scatter_step(2)
    at_visual(4, dob)
    attend_back(0, 2)
    scatter_step(3)
    grad1(2)
    attend_back(2, 4)
    scatter_step(4)
    grad1(3)
    attend_back(4, 6)
    scatter_step(5)
    weight_grad(8, lambda at: ob[pl.ds(C, rows), at], lambda: obuf[...])
    attend_back(6, 8)
    for k, ref in ((5, Q), (6, K), (7, V)):
        from_visual(k, ref)
        at_cond(k, ref)
    scatter_step(6)
    norm_one()
    weight_grad(9, lambda at: gp[0, :, at], lambda: Q[pl.ds(C, rows), :])
    scatter_step(7)
    weight_grad(10, lambda at: gp[0, :, at], lambda: K[pl.ds(C, rows), :])
    input_back()
    xg_copy.start()
    scatter_step(8)
    weight_grad(11, lambda at: gp[0, :, at], lambda: V[pl.ds(C, rows), :])
    for y in range(2):
        for z in range(4):
            for b in range(2):
                for c in range(2):
                    at = (y * 4 + z) * 128
                    ggp[0, y, z, b, c] = gain[:, at : at + 128]
    msc.r0(0)
    scatter_step(9)
    msc.r1(0)
    scatter_step(10)
    msc.r2(0)
    scatter_step(11)
    msc.r3(0)
    scatter_step(12)
    msc.r4(0)
    scatter_step(13)
    scatter_step(14)
    sc.flush()
    msc.flush()
    xflush()
    xg_copy.wait()


def head_order():
    side = (HD - RT) // 2
    first = list(range(RT // 2))
    first += [RT + k for k in range(side // 2)] + [RT + side + k for k in range(side // 2)]
    second = [RT // 2 + k for k in range(RT // 2)]
    second += [RT + side // 2 + k for k in range(side // 2)]
    second += [RT + side + side // 2 + k for k in range(side // 2)]
    return first, second


def pair_lanes(array):
    rows, width = array.shape
    first, second = head_order()
    heads = array.reshape(rows, width // 128, 2, 64)
    both = jnp.stack([heads[..., jnp.array(first)], heads[..., jnp.array(second)]], axis=2)
    return both.reshape(rows, width)


def unpair_lanes(array):
    rows, width = array.shape
    first, second = head_order()
    back = [0] * 64
    for k, (a, b) in enumerate(zip(first, second)):
        back[a] = k
        back[b] = 32 + k
    halves = array.reshape(rows, width // 128, 2, 2, 32)
    heads = jnp.swapaxes(halves, 2, 3).reshape(rows, width // 128, 2, 64)
    return heads[..., jnp.array(back)].reshape(rows, width)


def fast_body(
    tokens, w_qkv, w_proj, w_fc1, w_fc2, norm1_gain, norm2_gain, clip_index, frame_index, cotangent
):
    rows, width = tokens.shape
    frames = rows // FV
    C = frames * FA
    R = rows + C
    clip = lax.axis_index("clip")
    low = [w.astype(BF16) for w in (w_qkv, w_proj, w_fc1, w_fc2)]
    n = low[0].shape[0]
    fc1 = jnp.transpose(low[2].reshape(n, 32, 4, 32), (2, 0, 1, 3)).reshape(4, n, width)
    fc2 = low[3].reshape(4, n, width)
    own = jnp.concatenate(
        [
            jnp.stack(
                [
                    pair_lanes(low[0][:, :width]),
                    pair_lanes(low[0][:, width : 2 * width]),
                    low[0][:, 2 * width :],
                    low[1],
                ]
            ),
            fc1,
            fc2,
        ]
    )
    gains = jnp.stack([norm1_gain, norm2_gain]).astype(BF16).astype(F32)
    lane = (clip % 4) * n
    gown = lax.dynamic_update_slice(jnp.zeros((8, 128), F32), gains, (0, lane))[None]
    seen = clip_index.astype(F32)
    when = frame_index.astype(F32)

    def with_cond(v):
        return jnp.concatenate([jnp.repeat(v.reshape(frames, FV)[:, 0], FA), v])

    real = with_cond(seen) >= 0
    base = with_cond(seen) * 64.0
    code = base + with_cond(when)
    lo, hi = jnp.where(real, base, 1.0), jnp.where(real, code, 0.0)
    pad = -(-R // 128) * 128

    def wide(v):
        return jnp.pad(v, (0, pad - v.shape[0]))

    twice = lambda v: jnp.concatenate([v[:C], v[:C]])
    codes = jnp.stack(
        [wide(v) for v in (code, lo, hi, with_cond(when), twice(lo), twice(hi), code, code)]
    )
    any_spec = pl.BlockSpec(memory_space=pl.ANY)
    vmem = pl.BlockSpec(memory_space=pltpu.VMEM)
    unit = (2, 4, 2, 2, n, width)
    out, xg, gw, gg, _ = pl.pallas_call(
        layer_kernel,
        out_shape=[
            jax.ShapeDtypeStruct((rows, width), BF16),
            jax.ShapeDtypeStruct((rows, width), BF16),
            jax.ShapeDtypeStruct((NU, n, width), F32),
            jax.ShapeDtypeStruct((8, 128), F32),
            jax.ShapeDtypeStruct((4,) + unit, BF16),
        ],
        in_specs=[vmem] * 5,
        out_specs=[any_spec, any_spec, vmem, vmem, any_spec],
        scratch_shapes=[
            pltpu.VMEM((NU,) + unit, BF16),
            pltpu.VMEM((1, 2, 4, 2, 2, 8, 128), F32),
            pltpu.VMEM((R, width), BF16),
            pltpu.VMEM((R, width), BF16),
            pltpu.VMEM((R, width), BF16),
            pltpu.VMEM((R, width), BF16),
            pltpu.VMEM((R, width), BF16),
            pltpu.VMEM((rows, width), F32),
            pltpu.VMEM((rows, width), BF16),
            pltpu.VMEM((2,) + unit, BF16),
            pltpu.VMEM((4, rows, width), BF16),
            pltpu.VMEM((4,) + unit, BF16),
            pltpu.VMEM((rows, width), BF16),
            pltpu.VMEM((R, rows), F32),
            pltpu.VMEM((R, 128), F32),
            pltpu.VMEM((R, 128), F32),
            pltpu.VMEM((R, 128), F32),
            pltpu.VMEM((8, 8, 256), F32),
            pltpu.VMEM((R, 128), F32),
            pltpu.VMEM((R, 128), F32),
            pltpu.VMEM((8, width), F32),
            pltpu.VMEM((1, 2, 4, 2, 2, 8, 128), F32),
            pltpu.VMEM((32, 8, 128), F32),
            pltpu.SemaphoreType.DMA((NU, 17)),
            pltpu.SemaphoreType.DMA((NU, 17)),
            pltpu.SemaphoreType.DMA((1, 17)),
            pltpu.SemaphoreType.DMA((1, 17)),
            pltpu.SemaphoreType.DMA((NU, 12)),
            pltpu.SemaphoreType.DMA((NU, 12)),
            pltpu.SemaphoreType.DMA((1, 12)),
            pltpu.SemaphoreType.DMA((1, 12)),
            pltpu.SemaphoreType.DMA((8,)),
            pltpu.SemaphoreType.DMA((8,)),
            pltpu.SemaphoreType.DMA((6,)),
            pltpu.SemaphoreType.REGULAR((NU,)),
        ],
        compiler_params=pltpu.CompilerParams(
            collective_id=0, has_side_effects=True, vmem_limit_bytes=VMEM_LIMIT
        ),
    )(tokens, cotangent, own, gown, codes)
    grad_qkv = jnp.concatenate([unpair_lanes(gw[0]), unpair_lanes(gw[1]), gw[2]], axis=1)
    grad_fc1 = jnp.transpose(gw[4:8].reshape(4, n, 32, 32), (1, 2, 0, 3)).reshape(n, 4 * width)
    gains_out = lax.dynamic_slice(gg[4:6], (0, lane), (2, n))
    return (
        out,
        xg,
        grad_qkv,
        gw[3],
        grad_fc1,
        gw[8:].reshape(4 * n, width),
        gains_out[0],
        gains_out[1],
    )


def solution(mesh):
    placed = (
        P(("stream", "clip"), None),
        P(("stream", "clip"), None),
        P(("stream", "clip"), None),
        P(("stream", "clip"), None),
        P(("stream", "clip"), None),
        P(("stream", "clip")),
        P(("stream", "clip")),
        P(("stream", "clip")),
        P(("stream", "clip")),
        P(("stream", "clip"), None),
    )
    block = mesh.shape["stream"] == 2 and mesh.shape["clip"] == 16
    return jax.shard_map(
        fast_body if block else body,
        mesh=mesh,
        in_specs=placed,
        out_specs=(
            P(("stream", "clip"), None),
            P(("stream", "clip"), None),
            P(("stream", "clip"), None),
            P(("stream", "clip"), None),
            P(("stream", "clip"), None),
            P(("stream", "clip"), None),
            P(("stream", "clip")),
            P(("stream", "clip")),
        ),
        check_vma=False,
    )
```

```python
import jax
import jax.numpy as jnp
from jax import lax
from jax.experimental import pallas as pl
from jax.experimental.pallas import tpu as pltpu
from jax.sharding import PartitionSpec as P

HD = 64
RT = 16
GW = 4
FA = 2
FV = 16


EPSILON = 1e-06
THETA = 10000.0
MASKED = -1e30
LOG_THETA = 9.210340371976184
VMEM_LIMIT = 63 * 1024 * 1024


def shifted(value, axis, steps):
    count = lax.axis_size(axis)
    initial, last = (max(0, -steps), min(count, count - steps))
    return lax.ppermute(value, axis, [(source, source + steps) for source in range(initial, last)])


def frequencies(width):
    counter = jnp.arange(width // 2).astype(jnp.float32)
    return jnp.power(THETA, -2.0 * counter / width)


def angle_sets(frames, visual_flag, rows):
    place = jnp.arange(rows)
    inner = place % FV
    down_pos = inner // GW * visual_flag
    across_pos = inner % GW * visual_flag
    side = (HD - RT) // 2
    time_angles = frames.astype(jnp.float32)[:, None] * frequencies(RT)[None, :]
    down_angles = down_pos.astype(jnp.float32)[:, None] * frequencies(side)[None, :]
    across_angles = across_pos.astype(jnp.float32)[:, None] * frequencies(side)[None, :]
    return (time_angles, down_angles, across_angles)


def rotate(block, angles):
    half = block.shape[-1] // 2
    cosine = jnp.cos(angles)[:, None, :]
    sine = jnp.sin(angles)[:, None, :]
    first = block[..., :half]
    second = block[..., half:]
    return jnp.concatenate(
        [first * cosine - second * sine, first * sine + second * cosine], axis=-1
    )


def rotary(flat, sets, sign):
    rows = flat.shape[0]
    block = flat.reshape(rows, flat.shape[1] // HD, HD)
    side = (HD - RT) // 2
    pieces = (block[..., :RT], block[..., RT : RT + side], block[..., RT + side :])
    turned = [rotate(piece, sign * angles) for piece, angles in zip(pieces, sets)]
    return jnp.concatenate(turned, axis=-1).reshape(rows, -1)


def normalize(values, gain):
    centred = values - jnp.mean(values, axis=-1, keepdims=True)
    inverse = lax.rsqrt(jnp.mean(centred * centred, axis=-1, keepdims=True) + EPSILON)
    unit = centred * inverse
    return (unit * gain, unit, inverse)


def norm_back(grad_out, gain, unit, inverse):
    scaled = grad_out * gain
    centred = (
        scaled
        - jnp.mean(scaled, axis=-1, keepdims=True)
        - unit * jnp.mean(scaled * unit, axis=-1, keepdims=True)
    )
    return (inverse * centred, jnp.sum(grad_out * unit, axis=0))


def local_mask(clips, frames):
    rows = clips.shape[0]
    same = (
        (clips[:, None] == clips[None, :])
        & (clips[:, None] >= 0)
        & (frames[None, :] <= frames[:, None])
    )
    return same | (jnp.arange(rows)[:, None] == jnp.arange(rows)[None, :])


def cross_mask(clips, frames, far_clips, far_frames):
    return (
        (clips[:, None] == far_clips[None, :])
        & (clips[:, None] >= 0)
        & (far_frames[None, :] <= frames[:, None])
    )


def times_transpose(left, right):
    return lax.dot_general(
        left, right, (((1,), (1,)), ((), ())), preferred_element_type=jnp.float32
    )


def transpose_times(left, right):
    return lax.dot_general(
        left, right, (((0,), (0,)), ((), ())), preferred_element_type=jnp.float32
    )


def head_scores(query_part, key_part, allowed):
    query_heads = query_part.reshape(query_part.shape[0], 2, HD)
    key_heads = key_part.reshape(key_part.shape[0], 2, HD)
    scores = jnp.einsum(
        "qhd,khd->hqk", query_heads, key_heads, preferred_element_type=jnp.float32
    ) * HD ** (-0.5)
    return (jnp.where(allowed[None], scores, MASKED), query_heads, key_heads)


def attend_forward(query_part, key_part, value_part, allowed):
    rows = query_part.shape[0]
    scores, query_heads, key_heads = head_scores(query_part, key_part, allowed)
    peak = jnp.max(scores, axis=-1, keepdims=True)
    weights = jnp.exp(scores - peak)
    total = jnp.sum(weights, axis=-1, keepdims=True)
    probs = (weights / total).astype(jnp.bfloat16)
    value_heads = value_part.reshape(value_part.shape[0], 2, HD)
    mixed = jnp.einsum("hqk,khd->qhd", probs, value_heads, preferred_element_type=jnp.float32)
    return (mixed.reshape(rows, 2 * HD), (peak + jnp.log(total))[..., 0])


def attend_back(query_part, key_part, value_part, grad_part, allowed, log_total):
    rows = query_part.shape[0]
    scores, query_heads, key_heads = head_scores(query_part, key_part, allowed)
    probs = jnp.exp(scores - log_total[..., None])
    value_heads = value_part.reshape(value_part.shape[0], 2, HD)
    grad_heads = grad_part.reshape(rows, 2, HD)
    grad_probs = jnp.einsum(
        "qhd,khd->hqk", grad_heads, value_heads, preferred_element_type=jnp.float32
    )
    centre = jnp.sum(probs * grad_probs, axis=-1, keepdims=True)
    grad_scores = (probs * (grad_probs - centre)).astype(jnp.bfloat16)
    factor = HD ** (-0.5)
    grad_query = (
        jnp.einsum("hqk,khd->qhd", grad_scores, key_heads, preferred_element_type=jnp.float32)
        * factor
    )
    grad_key = (
        jnp.einsum("hqk,qhd->khd", grad_scores, query_heads, preferred_element_type=jnp.float32)
        * factor
    )
    grad_value = jnp.einsum(
        "hqk,qhd->khd", probs.astype(jnp.bfloat16), grad_heads, preferred_element_type=jnp.float32
    )
    key_count = key_part.shape[0]
    return (
        grad_query.reshape(rows, 2 * HD),
        grad_key.reshape(key_count, 2 * HD),
        grad_value.reshape(key_count, 2 * HD),
    )


def column_block(array, group_index):
    return lax.dynamic_slice_in_dim(array, group_index * 2 * HD, 2 * HD, 1)


def join_groups(stacked):
    return jnp.transpose(stacked, (1, 0, 2)).reshape(stacked.shape[1], -1)


def body(
    tokens, w_qkv, w_proj, w_fc1, w_fc2, norm1_gain, norm2_gain, clip_index, frame_index, cotangent
):
    rows = tokens.shape[0]
    width = tokens.shape[1]
    groups = width // (2 * HD)
    visual = lax.axis_index("stream") == 1
    visual_flag = visual.astype(jnp.int32)
    shards = (
        w_qkv.astype(jnp.bfloat16),
        w_proj.astype(jnp.bfloat16),
        w_fc1.astype(jnp.bfloat16),
        w_fc2.astype(jnp.bfloat16),
        norm1_gain.astype(jnp.bfloat16),
        norm2_gain.astype(jnp.bfloat16),
    )
    full_qkv, full_proj, full_fc1, full_fc2, gain_one, gain_two = (
        lax.all_gather(shards[0], ("stream", "clip"), axis=0, tiled=True),
        lax.all_gather(shards[1], ("stream", "clip"), axis=0, tiled=True),
        lax.all_gather(shards[2], ("stream", "clip"), axis=0, tiled=True),
        lax.all_gather(shards[3], ("stream", "clip"), axis=0, tiled=True),
        lax.all_gather(shards[4], ("stream", "clip"), axis=0, tiled=True),
        lax.all_gather(shards[5], ("stream", "clip"), axis=0, tiled=True),
    )
    gain_first = gain_one.astype(jnp.float32)
    gain_second = gain_two.astype(jnp.float32)
    values_in = tokens.astype(jnp.float32)
    normed, unit_one, inverse_one = normalize(values_in, gain_first)
    normed_b = normed.astype(jnp.bfloat16)
    projected = jnp.dot(normed_b, full_qkv, preferred_element_type=jnp.float32)
    sets = angle_sets(frame_index, visual_flag, rows)
    queries = rotary(projected[:, :width], sets, 1.0).astype(jnp.bfloat16)
    key_rows = rotary(projected[:, width : 2 * width], sets, 1.0).astype(jnp.bfloat16)
    values = projected[:, 2 * width :].astype(jnp.bfloat16)
    frames_row = rows // FV
    cond_rows = frames_row * FA
    near_keys, near_values = shifted((key_rows[:cond_rows], values[:cond_rows]), "stream", 1)
    far_keys, far_values = shifted((key_rows, values), "stream", -1)
    clip_seen = clip_index.reshape(frames_row, FV)[:, 0]
    clip_cond = clip_index[:cond_rows].reshape(frames_row, FA)[:, 0]
    frame_seen = frame_index.reshape(frames_row, FV)[:, 0]
    frame_cond = frame_index[:cond_rows].reshape(frames_row, FA)[:, 0]
    frame_clip = jnp.where(visual, clip_seen, clip_cond)
    frame_num = jnp.where(visual, frame_seen, frame_cond)
    partner_cond = (
        cross_mask(clip_index, frame_index, jnp.repeat(frame_clip, FA), jnp.repeat(frame_num, FA))
        & visual
    )
    partner_seen = cross_mask(
        clip_index, frame_index, jnp.repeat(frame_clip, FV), jnp.repeat(frame_num, FV)
    ) & jnp.logical_not(visual)
    allowed = jnp.concatenate(
        [partner_cond, partner_seen, local_mask(clip_index, frame_index)], axis=1
    )
    key_all = jnp.concatenate([near_keys, far_keys, key_rows], axis=0)
    value_all = jnp.concatenate([near_values, far_values, values], axis=0)

    def forward_group(group_index):
        return attend_forward(
            column_block(queries, group_index),
            column_block(key_all, group_index),
            column_block(value_all, group_index),
            allowed,
        )

    mixed_groups, log_totals = lax.map(forward_group, jnp.arange(groups))
    mixed_b = join_groups(mixed_groups).astype(jnp.bfloat16)
    hidden_one = values_in + jnp.dot(mixed_b, full_proj, preferred_element_type=jnp.float32)
    normed_two, unit_two, inverse_two = normalize(hidden_one, gain_second)
    normed_two_b = normed_two.astype(jnp.bfloat16)
    inner = jnp.dot(normed_two_b, full_fc1, preferred_element_type=jnp.float32)
    active, gelu_pull = jax.vjp(lambda given: jax.nn.gelu(given, approximate=False), inner)
    active_b = active.astype(jnp.bfloat16)
    result = hidden_one + jnp.dot(active_b, full_fc2, preferred_element_type=jnp.float32)
    full_qkv, full_proj, full_fc1, full_fc2, gain_one, gain_two = (
        lax.all_gather(shards[0], ("stream", "clip"), axis=0, tiled=True),
        lax.all_gather(shards[1], ("stream", "clip"), axis=0, tiled=True),
        lax.all_gather(shards[2], ("stream", "clip"), axis=0, tiled=True),
        lax.all_gather(shards[3], ("stream", "clip"), axis=0, tiled=True),
        lax.all_gather(shards[4], ("stream", "clip"), axis=0, tiled=True),
        lax.all_gather(shards[5], ("stream", "clip"), axis=0, tiled=True),
    )
    gain_first = gain_one.astype(jnp.float32)
    gain_second = gain_two.astype(jnp.float32)
    grad_out = cotangent.astype(jnp.float32)
    grad_fc2 = transpose_times(active_b, cotangent)
    grad_active = times_transpose(cotangent, full_fc2)
    grad_inner = gelu_pull(grad_active)[0].astype(jnp.bfloat16)
    grad_fc1 = transpose_times(normed_two_b, grad_inner)
    grad_normed_two = times_transpose(grad_inner, full_fc1)
    back_two, grad_gain2 = norm_back(grad_normed_two, gain_second, unit_two, inverse_two)
    grad_hidden = grad_out + back_two
    grad_attn = grad_hidden.astype(jnp.bfloat16)
    grad_proj = transpose_times(mixed_b, grad_attn)
    grad_mixed = times_transpose(grad_attn, full_proj).astype(jnp.bfloat16)

    def backward_group(inputs):
        group_index, log_total = inputs
        return attend_back(
            column_block(queries, group_index),
            column_block(key_all, group_index),
            column_block(value_all, group_index),
            column_block(grad_mixed, group_index),
            allowed,
            log_total,
        )

    grad_q_groups, grad_k_groups, grad_v_groups = lax.map(
        backward_group, (jnp.arange(groups), log_totals)
    )
    grad_queries = join_groups(grad_q_groups)
    grad_key_all = join_groups(grad_k_groups)
    grad_value_all = join_groups(grad_v_groups)
    outer = cond_rows + rows
    cond_keys_back, cond_values_back = (
        shifted(grad_key_all[:cond_rows].astype(jnp.bfloat16), "stream", -1).astype(jnp.float32),
        shifted(grad_value_all[:cond_rows].astype(jnp.bfloat16), "stream", -1).astype(jnp.float32),
    )
    seen_keys_back, seen_values_back = (
        shifted(grad_key_all[cond_rows:outer].astype(jnp.bfloat16), "stream", 1).astype(
            jnp.float32
        ),
        shifted(grad_value_all[cond_rows:outer].astype(jnp.bfloat16), "stream", 1).astype(
            jnp.float32
        ),
    )
    filler = jnp.zeros((rows - cond_rows, width), jnp.float32)
    grad_keys = (
        grad_key_all[outer:] + seen_keys_back + jnp.concatenate([cond_keys_back, filler], axis=0)
    )
    grad_values = (
        grad_value_all[outer:]
        + seen_values_back
        + jnp.concatenate([cond_values_back, filler], axis=0)
    )
    grad_projected = jnp.concatenate(
        [rotary(grad_queries, sets, -1.0), rotary(grad_keys, sets, -1.0), grad_values], axis=1
    ).astype(jnp.bfloat16)
    grad_qkv = transpose_times(normed_b, grad_projected)
    grad_normed = times_transpose(grad_projected, full_qkv)
    back_one, grad_gain1 = norm_back(grad_normed, gain_first, unit_one, inverse_one)
    input_grad = (grad_hidden + back_one).astype(jnp.bfloat16)
    sums = (
        lax.psum_scatter(grad_qkv, ("stream", "clip"), scatter_dimension=0, tiled=True),
        lax.psum_scatter(grad_proj, ("stream", "clip"), scatter_dimension=0, tiled=True),
        lax.psum_scatter(grad_fc1, ("stream", "clip"), scatter_dimension=0, tiled=True),
        lax.psum_scatter(grad_fc2, ("stream", "clip"), scatter_dimension=0, tiled=True),
        lax.psum_scatter(grad_gain1, ("stream", "clip"), scatter_dimension=0, tiled=True),
        lax.psum_scatter(grad_gain2, ("stream", "clip"), scatter_dimension=0, tiled=True),
    )
    return (
        result.astype(jnp.bfloat16),
        input_grad,
        sums[0],
        sums[1],
        sums[2],
        sums[3],
        sums[4],
        sums[5],
    )


MESH = pl.DeviceIdType.MESH
F32 = jnp.float32
BF16 = jnp.bfloat16
MB = 1 << 20
NU = 12
ORDER = (8, 9, 10, 11, 4, 5, 6, 7, 3, 0, 1, 2)
WIDE = 1024
NEG = -1e30


class Place:
    def __init__(self):
        self.y = lax.axis_index("stream")
        clip = lax.axis_index("clip")
        self.z, self.x, self.c = clip // 4, (clip // 2) % 2, clip % 2
        self.X = self.dev(self.y, self.z, 1 - self.x, self.c)
        self.Y = self.dev(1 - self.y, self.z, self.x, self.c)
        self.C = self.dev(self.y, self.z, self.x, 1 - self.c)

    def dev(self, y, z, x, c):
        return (y, z * 4 + x * 2 + c)

    def up(self, d):
        return lax.rem(self.z + d, 4)

    def above(self, d):
        return self.dev(self.y, self.up(d), self.x, self.c)

    def peers(self):
        return [self.X, self.Y, self.C] + [self.above(d) for d in (1, 2, 3)]


class Link:
    def __init__(self, place, sent, got):
        self.p, self.sent, self.got, self.open = place, sent, got, []

    def copy(self, u, slot, src, dst, to):
        return pltpu.make_async_remote_copy(
            src_ref=src,
            dst_ref=dst,
            send_sem=self.sent.at[u, slot],
            recv_sem=self.got.at[u, slot],
            device_id=to,
            device_id_type=MESH,
        )

    def send(self, u, slot, src, dst, to):
        c = self.copy(u, slot, src, dst, to)
        c.start()
        self.open.append((u, c))

    def recv(self, u, slot, dst):
        self.copy(u, slot, dst, dst, self.p.X).wait_recv()

    def flush(self, unit=None):
        rest = []
        for u, c in self.open:
            if unit is None or u == unit:
                c.wait_send()
            else:
                rest.append((u, c))
        self.open = rest


class Gather(Link):
    def __init__(self, place, whole, sent, got):
        super().__init__(place, sent, got)
        self.W = whole

    def first(self, u):
        p = self.p
        me = self.W.at[u, p.y, p.z, p.x, p.c]
        for d in (1, 2, 3):
            self.send(u, d - 1, me, me, p.above(d))

    def second(self, u):
        p = self.p
        me = self.W.at[u, p.y, p.z, p.x, p.c]
        self.send(u, 3, me, me, p.X)
        self.send(u, 7, me, me, p.Y)

    def g1(self, u):
        p, W = self.p, self.W
        for d in (1, 2, 3):
            b = W.at[u, p.y, p.up(4 - d), p.x, p.c]
            self.recv(u, d - 1, b)
            self.send(u, 3 + d, b, b, p.X)
            self.send(u, 7 + d, b, b, p.Y)
        b = W.at[u, p.y, :, p.x, p.c]
        self.send(u, 13, b, b, p.C)

    def g2(self, u):
        p, W = self.p, self.W
        for k in range(4):
            z = p.up(4 - k)
            self.recv(u, 3 + k, W.at[u, p.y, z, 1 - p.x, p.c])
            self.recv(u, 7 + k, W.at[u, 1 - p.y, z, p.x, p.c])
        b = W.at[u, p.y, pl.ds(0, 2), 1 - p.x, p.c]
        self.send(u, 11, b, b, p.Y)
        b = W.at[u, 1 - p.y, pl.ds(2, 2), p.x, p.c]
        self.send(u, 12, b, b, p.X)
        b = W.at[u, p.y, :, 1 - p.x, p.c]
        self.send(u, 14, b, b, p.C)
        b = W.at[u, 1 - p.y, :, p.x, p.c]
        self.send(u, 15, b, b, p.C)

    def g3(self, u):
        p, W = self.p, self.W
        self.recv(u, 11, W.at[u, 1 - p.y, pl.ds(0, 2), 1 - p.x, p.c])
        self.recv(u, 12, W.at[u, 1 - p.y, pl.ds(2, 2), 1 - p.x, p.c])
        b = W.at[u, 1 - p.y, :, 1 - p.x, p.c]
        self.send(u, 16, b, b, p.C)

    def g4(self, u):
        p, W = self.p, self.W
        o = 1 - p.c
        self.recv(u, 13, W.at[u, p.y, :, p.x, o])
        self.recv(u, 14, W.at[u, p.y, :, 1 - p.x, o])
        self.recv(u, 15, W.at[u, 1 - p.y, :, p.x, o])
        self.recv(u, 16, W.at[u, 1 - p.y, :, 1 - p.x, o])


class Scatter(Link):
    def __init__(self, place, part, land, out, sent, got):
        super().__init__(place, sent, got)
        self.part, self.land, self.out = part, land, out

    def col(self, i, a, b):
        return self.land(i, (a * 2 + b) * 4, 4)

    def blk(self, i, a, b, z):
        return self.land(i, (a * 2 + b) * 4 + z, 1).at[0]

    def add(self, n, dst, *srcs):
        @pl.loop(0, n)
        def _(k):
            t = srcs[0](k)[...].astype(F32)
            for r in srcs[1:]:
                t = t + r(k)[...].astype(F32)
            d = dst(k)
            d[...] = t.astype(d.dtype)

    def r0(self, i):
        p = self.p
        y, x, o, q = p.y, p.x, 1 - p.c, self.part(i)
        for k, (a, b) in enumerate(((1 - y, 1 - x), (1 - y, x), (y, 1 - x), (y, x))):
            self.send(i, k, q.at[a, :, b, o], self.col(i, a, b), p.C)

    def r1(self, i):
        p = self.p
        y, x, c, q = p.y, p.x, p.c, self.part(i)
        self.recv(i, 0, self.col(i, 1 - y, 1 - x))
        own = lambda k: q.at[1 - y, k, 1 - x, c]
        self.add(4, own, own, lambda k: self.blk(i, 1 - y, 1 - x, k))
        self.send(i, 4, q.at[1 - y, pl.ds(0, 2), 1 - x, c], self.land(i, 16, 2), p.X)
        self.send(i, 5, q.at[1 - y, pl.ds(2, 2), 1 - x, c], self.land(i, 18, 2), p.Y)

    def r2(self, i):
        p = self.p
        y, x, c, q = p.y, p.x, p.c, self.part(i)
        self.recv(i, 1, self.col(i, 1 - y, x))
        self.recv(i, 2, self.col(i, y, 1 - x))
        ny = lambda k: q.at[1 - y, k, x, c]
        my = lambda k: self.blk(i, 1 - y, x, k)
        nx = lambda k: q.at[y, k, 1 - x, c]
        mx = lambda k: self.blk(i, y, 1 - x, k)
        self.add(2, lambda k: ny(k + 2), lambda k: ny(k + 2), lambda k: my(k + 2))
        self.add(2, nx, nx, mx)
        self.recv(i, 4, self.land(i, 16, 2))
        self.add(2, ny, ny, my, lambda k: self.land(i, 16 + k, 1).at[0])
        self.send(i, 6, q.at[1 - y, :, x, c], self.land(i, 28, 4), p.Y)
        self.recv(i, 5, self.land(i, 18, 2))
        self.add(
            2,
            lambda k: nx(k + 2),
            lambda k: nx(k + 2),
            lambda k: mx(k + 2),
            lambda k: self.land(i, 18 + k, 1).at[0],
        )
        self.send(i, 7, q.at[y, :, 1 - x, c], self.land(i, 24, 4), p.X)

    def r3(self, i):
        p = self.p
        y, x, c, q = p.y, p.x, p.c, self.part(i)
        self.recv(i, 3, self.col(i, y, x))
        self.recv(i, 6, self.land(i, 28, 4))
        self.recv(i, 7, self.land(i, 24, 4))
        own = lambda k: q.at[y, k, x, c]
        self.add(
            4,
            own,
            own,
            lambda k: self.blk(i, y, x, k),
            lambda k: self.land(i, 28 + k, 1).at[0],
            lambda k: self.land(i, 24 + k, 1).at[0],
        )
        for d in (1, 2, 3):
            self.send(i, 8 + d, q.at[y, p.up(d), x, c], self.land(i, 19 + d, 1).at[0], p.above(d))

    def r4(self, i):
        p = self.p
        q = self.part(i)
        for d in (1, 2, 3):
            self.recv(i, 8 + d, self.land(i, 19 + d, 1).at[0])
        t = q[p.y, p.z, p.x, p.c].astype(F32)
        for d in (1, 2, 3):
            t = t + self.land(i, 19 + d, 1)[0].astype(F32)
        self.out(i, t)


def unit_rows(v):
    centred = v - jnp.mean(v, axis=-1, keepdims=True)
    inverse = lax.rsqrt(jnp.mean(centred * centred, axis=-1, keepdims=True) + EPSILON)
    return centred * inverse, inverse


def back_rows(d, gain, unit, inverse):
    e = d * gain
    return inverse * (
        e - jnp.mean(e, axis=-1, keepdims=True) - unit * jnp.mean(e * unit, axis=-1, keepdims=True)
    )


def dot(a, b):
    return jnp.dot(a, b, preferred_element_type=F32)


def head_moves():
    side = (HD - RT) // 2
    moves = []
    for head in range(2):
        src, dst = head * HD, head * 32
        for at, part in ((0, RT), (RT, side), (RT + side, side)):
            moves.append((src + at, dst, part // 2))
            moves.append((src + at + part // 2, dst + 64, part // 2))
            dst += part // 2
    return moves


def move_lanes(pieces, lane):
    out = None
    for v, a, b, n in pieces:
        t = v if a == b else pltpu.roll(v, (b - a) % 128, 1)
        out = t if out is None else jnp.where((lane >= b) & (lane < b + n), t, out)
    return out


def rope_lane(shape):
    lane = lax.broadcasted_iota(jnp.int32, shape, 1)
    return lane, lane % 32


def layer_kernel(
    x_hbm, cot_hbm, wq, wp, w1, w2, g1, g2, clips, frames,
    out_hbm, xg_hbm, gq, gpr, gf1, gf2, gg, spill,
    W, G, codes, x, cot, Q, K, V, ob, dob, h1, a2, gbuf, gp, PS, obuf,
    bias, cbias, ct, st, lse, dk, dv, gain, ggp, gland,
    ss, rs, gss, grs, sss, srs, mss, mrs, xss, xrs, loc, credit,
):
    p = Place()
    vis = p.y == 1
    rows = x_hbm.shape[0]
    R = x.shape[0]
    C = R - rows
    TILE = R // 2
    n_own = wq.shape[0]
    W3 = W.reshape(NU, WIDE, WIDE)
    Wf = W.reshape(NU, 32, 32, WIDE)
    gflat = gbuf.reshape(3 * WIDE, WIDE)
    P3 = PS.reshape(4, WIDE, WIDE)
    G3 = gbuf.reshape(3, WIDE, WIDE)

    def gbr(j):
        return gflat.at[pl.ds(j * R, R)]

    def slot(i):
        return (0, i) if i < 4 else (1, i - 4) if i < 6 else (0, i - 6) if i < 10 else (1, i - 10)

    def part(i):
        k, n = slot(i)
        return (PS, gbuf)[k].at[n]

    def part3(i):
        k, n = slot(i)
        return (P3, G3)[k].at[n]

    def land(i, at, n):
        u = i if i < 4 else i + 4 if i < 8 else i - 8
        return Wf.at[u, pl.ds(at, n)]

    def finish(i, t):
        u = ORDER[i]
        lane = lax.broadcasted_iota(jnp.int32, (n_own, 128), 1)
        if u < 2:
            for k in range(8):
                v = t[:, k * 128 : (k + 1) * 128]
                at = u * WIDE + k * 128
                gq[:, at : at + 128] = move_lanes([(v, b, a, n) for a, b, n in head_moves()], lane)
        elif u == 2:
            gq[:, 2 * WIDE :] = t
        elif u == 3:
            gpr[...] = t
        elif u < 8:
            for h in range(2):
                bias[pl.ds((2 * u - 8 + h) * n_own, n_own), :] = t[:, h * 512 : (h + 1) * 512]
            if u == 7:
                for g in range(8):
                    at = slice(g % 4 * 128, (g % 4 + 1) * 128)
                    vs = [
                        bias[pl.ds((2 * j + g // 4) * n_own, n_own), at] for j in range(4)
                    ]
                    for a in range(4):
                        at = g * 512 + a * 128
                        gf1[:, at : at + 128] = move_lanes(
                            [(vs[j], 32 * a, 32 * j, 32) for j in range(4)], lane
                        )
        else:
            gf2[(u - 8) * n_own : (u - 7) * n_own, :] = t

    def finish_gains(i, t):
        gg[...] = t

    ga = Gather(p, W, ss, rs)
    mini = Gather(p, G, gss, grs)
    sc = Scatter(p, part, land, finish, sss, srs)
    msc = Scatter(
        p, lambda i: ggp.at[0], lambda i, at, n: gland.at[pl.ds(at, n)], finish_gains, mss, mrs
    )

    bar = pltpu.get_barrier_semaphore()
    for q in p.peers():
        pl.semaphore_signal(bar, inc=1, device_id=q, device_id_type=MESH)

    def xcopy(k, src, dst):
        return pltpu.make_async_remote_copy(
            src_ref=src, dst_ref=dst, send_sem=xss.at[k], recv_sem=xrs.at[k],
            device_id=p.Y, device_id_type=MESH,
        )

    def load_rows(k, src, dst):
        @pl.when(vis)
        def _():
            local(k, src, dst.at[pl.ds(C, rows)]).start()

        @pl.when(p.y == 0)
        def _():
            xcopy(k, src.at[pl.ds(0, C)], dst.at[pl.ds(0, C)]).start()
            local(k, src.at[pl.ds(C, rows - C)], dst.at[pl.ds(2 * C, rows - C)]).start()
            dst[0 : 2 * C, :] = jnp.zeros((2 * C, WIDE), BF16)

    def wait_rows(k, src, dst):
        @pl.when(vis)
        def _():
            local(k, src, dst.at[pl.ds(C, rows)]).wait()
            xcopy(k, src.at[pl.ds(0, C)], dst.at[pl.ds(0, C)]).wait_recv()

        @pl.when(p.y == 0)
        def _():
            local(k, src.at[pl.ds(C, rows - C)], dst.at[pl.ds(2 * C, rows - C)]).wait()
            xcopy(k, src.at[pl.ds(0, C)], dst.at[pl.ds(0, C)]).wait_send()

    def store_rows(k, src, dst):
        @pl.when(vis)
        def _():
            xcopy(k, src.at[pl.ds(0, C)], dst.at[pl.ds(0, C)]).start()
            local(k, src.at[pl.ds(C, rows)], dst).start()

        @pl.when(p.y == 0)
        def _():
            local(k, src.at[pl.ds(2 * C, rows - C)], dst.at[pl.ds(C, rows - C)]).start()

    def stored_rows(k, src, dst):
        @pl.when(vis)
        def _():
            xcopy(k, src.at[pl.ds(0, C)], dst.at[pl.ds(0, C)]).wait_send()
            local(k, src.at[pl.ds(C, rows)], dst).wait()

        @pl.when(p.y == 0)
        def _():
            local(k, src.at[pl.ds(2 * C, rows - C)], dst.at[pl.ds(C, rows - C)]).wait()

    def came_back(k, src, dst):
        @pl.when(p.y == 0)
        def _():
            xcopy(k, src.at[pl.ds(0, C)], dst.at[pl.ds(0, C)]).wait_recv()

    def place_gains():
        lane = lax.broadcasted_iota(jnp.int32, (1, 128), 1)
        mine = lane // n_own == lax.rem(p.x * 2 + p.c, 4)
        pair = []
        for g in (g1, g2):
            v = g[...].astype(BF16).astype(F32)
            pair.append(jnp.where(mine, jnp.concatenate([v] * 4, axis=1), 0.0))
        G[0, p.y, p.z, p.x, p.c] = jnp.concatenate(pair + [jnp.zeros((6, 128), F32)], axis=0)

    def place_own(u):
        lane = lax.broadcasted_iota(jnp.int32, (n_own, 128), 1)
        for k in range(8):
            at = slice(k * 128, (k + 1) * 128)
            if u < 2:
                v = h1[u * n_own : (u + 1) * n_own, at]
                v = move_lanes([(v, a, b, n) for a, b, n in head_moves()], lane)
            elif u == 2:
                v = h1[2 * n_own : 3 * n_own, at]
            elif u == 3:
                v = h1[3 * n_own : 4 * n_own, at]
            elif u < 8:
                j = u - 4
                top = (4 + k // 2) * n_own
                left = k % 2 * 512
                v = move_lanes(
                    [
                        (h1[top : top + n_own, left + a * 128 : left + (a + 1) * 128], 32 * j, 32 * a, 32)
                        for a in range(4)
                    ],
                    lane,
                )
            else:
                v = h1[u * n_own : (u + 1) * n_own, at]
            W[u, p.y, p.z, p.x, p.c, :, at] = v.astype(BF16)

    def place_codes():
        pair = []
        for ref in (clips, frames):
            v = ref[...].astype(F32)
            pair.append(jnp.concatenate([v[k : k + 1] for k in range(rows // 128)], axis=1))
        both = jnp.concatenate(pair + [jnp.zeros((6, rows), F32)], axis=0)
        src = lax.broadcasted_iota(jnp.int32, (rows, 128), 0)
        lane = lax.broadcasted_iota(jnp.int32, (rows, 128), 1)
        pick = jnp.where((src == lane // FA * FV) & (lane < C), 1.0, 0.0).astype(BF16)
        cond = dot(both.astype(BF16), pick)
        full = jnp.concatenate([cond[:, :C], both], axis=1)
        clip, when = full[0:1], full[1:2]
        base = clip * 64.0
        code = base + when
        lo = jnp.where(clip >= 0, base, 1.0)
        hi = jnp.where(clip >= 0, code, 0.0)
        twice = lambda v: jnp.concatenate([v[:, :C], v[:, :C], v[:, 2 * C :]], axis=1)
        for k, v in enumerate((code, lo, hi, when, twice(lo), twice(hi))):
            codes[k : k + 1, 0:R] = v

    def gains():
        for y in range(2):
            for z in range(4):
                t = G[0, y, z, 0, 0] + G[0, y, z, 0, 1] + G[0, y, z, 1, 0] + G[0, y, z, 1, 1]
                gain[:, (y * 4 + z) * 128 : (y * 4 + z + 1) * 128] = t

    def column(row, at):
        return jnp.transpose(jnp.broadcast_to(codes[row : row + 1, at : at + 128], (128, 128)))

    def tables():
        side = (HD - RT) // 2
        for at in range(0, R, 128):
            n = min(128, R - at)
            shape = (n, 128)
            lane, i = rope_lane(shape)
            t = column(3, at)[:n]
            place = lax.broadcasted_iota(jnp.int32, shape, 0) + (at - C)
            inner = place % FV
            own_row = (place >= 0) & vis
            down = jnp.where(own_row, inner // GW, 0).astype(F32)
            across = jnp.where(own_row, inner % GW, 0).astype(F32)
            first, second = RT // 2, RT // 2 + side // 2
            k = jnp.where(i < first, i, jnp.where(i < second, i - first, i - second)).astype(F32)
            n_at = jnp.where(i < first, t, jnp.where(i < second, down, across))
            width = jnp.where(i < first, float(RT), float(side))
            angle = n_at * jnp.exp(k / width * (-2.0 * LOG_THETA))
            ct[at : at + n, :] = jnp.cos(angle)
            sine = jnp.sin(angle)
            st[at : at + n, :] = jnp.where(lane < 64, -sine, sine)

    def biases():
        for at in range(0, R, 128):
            n = min(128, R - at)
            kc = column(0, at)[:n]
            key = lax.broadcasted_iota(jnp.int32, (n, 128), 0) + at
            lane = lax.broadcasted_iota(jnp.int32, (n, 128), 1)
            for qa in range(0, rows, 128):
                lo = codes[1:2, C + qa : C + qa + 128]
                hi = codes[2:3, C + qa : C + qa + 128]
                ok = ((kc >= lo) & (kc <= hi)) | (key == lane + (qa + C))
                bias[at : at + n, qa : qa + 128] = jnp.where(ok, 0.0, NEG)
            lo, hi = codes[4:5, 0:128], codes[5:6, 0:128]
            ok = ((kc >= lo) & (kc <= hi)) | (key == lane % 64)
            cbias[at : at + n, :] = jnp.where(ok, 0.0, NEG)

    def norm_one():
        @pl.loop(0, R // 64)
        def _(k):
            r = pl.ds(pl.multiple_of(k * 64, 64), 64)
            unit, _ = unit_rows(x[r, :].astype(F32))
            gp[0, r, :] = (unit * gain[0:1, :]).astype(BF16)

    def turned(v, rowset, sign):
        return v * ct[rowset, :] + pltpu.roll(v, 64, 1) * (st[rowset, :] * sign)

    def project(u):
        dst = (Q, K, V)[u]

        @pl.loop(0, WIDE // 256)
        def _(k):
            at = pl.multiple_of(k * 256, 256)
            v = dot(gp[0], W3[u, :, pl.ds(at, 256)])
            for h in range(2):
                part_v = v[:, h * 128 : (h + 1) * 128]
                if u < 2:
                    part_v = turned(part_v, slice(0, R), 1.0)
                dst[:, pl.ds(pl.multiple_of(at + h * 128, 128), 128)] = part_v.astype(BF16)

    blocks = [(0, C, R)] + [(C + 128 * b, 128, C + 128 * (b + 1)) for b in range(rows // 128)]

    def masks():
        lane, _ = rope_lane((1, 128))
        even = (lane % 64) < 32
        first = lane < 64
        return even, first

    def stack(v, m, scale):
        zero = jnp.zeros_like(v)
        both = jnp.concatenate([jnp.where(m, v, zero), jnp.where(m, zero, v)], axis=0)
        return both * jnp.asarray(scale, BF16) if scale != 1.0 else both

    def scores(b, q0, nq, n, k, rq):
        s = lax.dot_general(k[:n], rq, (((1,), (1,)), ((), ())), preferred_element_type=F32)
        if b == 0:
            return s + cbias[0:n, :]
        t = bias[0:n, q0 - C : q0 - C + nq]
        return s + jnp.concatenate([t, t], axis=1)

    def attend(lo, hi):
        @pl.when(vis)
        def _():
            even, first = masks()

            @pl.loop(lo, hi)
            def _(pair):
                cols = pl.ds(pl.multiple_of(pair * 128, 128), 128)
                k, v = K[:, cols], V[:, cols]
                for b, (q0, nq, n) in enumerate(blocks):
                    rq = stack(Q[q0 : q0 + nq, cols], even, HD ** -0.5)
                    s = scores(b, q0, nq, n, k, rq)
                    top = jnp.max(s, axis=0, keepdims=True)
                    e = jnp.exp(s - top)
                    total = jnp.sum(e, axis=0, keepdims=True)
                    prob = (e * (1.0 / total)).astype(BF16)
                    lse[pair, b : b + 1, 0 : 2 * nq] = top + jnp.log(total)
                    o = lax.dot_general(
                        v[:n], prob, (((0,), (0,)), ((), ())), preferred_element_type=F32
                    )
                    o = jnp.transpose(o)
                    ob[q0 : q0 + nq, cols] = jnp.where(first, o[:nq], o[nq:]).astype(BF16)

    def attend_back(lo, hi):
        @pl.when(vis)
        def _():
            even, first = masks()

            @pl.loop(lo, hi)
            def _(pair):
                cols = pl.ds(pl.multiple_of(pair * 128, 128), 128)
                k, v = K[:, cols], V[:, cols]
                for b, (q0, nq, n) in enumerate(blocks):
                    rq = stack(Q[q0 : q0 + nq, cols], even, HD ** -0.5)
                    rd = stack(dob[q0 : q0 + nq, cols], first, 1.0)
                    s = scores(b, q0, nq, n, k, rq)
                    prob = jnp.exp(s - lse[pair, b : b + 1, 0 : 2 * nq])
                    dp = lax.dot_general(
                        v[:n], rd, (((1,), (1,)), ((), ())), preferred_element_type=F32
                    )
                    centre = jnp.sum(prob * dp, axis=0, keepdims=True)
                    ds = (prob * (dp - centre)).astype(BF16)
                    dvn = dot(prob.astype(BF16), rd)
                    dkn = dot(ds, rq)
                    if b == 0:
                        dv[...] = dvn
                        dk[...] = dkn
                    else:
                        dv[0:n, :] += dvn
                        dk[0:n, :] += dkn
                    t = lax.dot_general(
                        k[:n], ds, (((0,), (0,)), ((), ())), preferred_element_type=F32
                    )
                    t = jnp.transpose(t)
                    dq = jnp.where(even, t[:nq], t[nq:]) * HD ** -0.5
                    Q[q0 : q0 + nq, cols] = turned(dq, slice(q0, q0 + nq), -1.0).astype(BF16)
                K[:, cols] = turned(dk[...], slice(0, R), -1.0).astype(BF16)
                V[:, cols] = dv[...].astype(BF16)

    def pad_forward():
        @pl.when(p.y == 0)
        def _():
            ob[...] = V[...]

    def pad_back():
        @pl.when(p.y == 0)
        def _():
            Q[...] = jnp.zeros((R, WIDE), BF16)
            K[...] = jnp.zeros((R, WIDE), BF16)
            V[...] = dob[...]

    def hidden():
        @pl.loop(0, R // TILE)
        def _(k):
            r = pl.ds(pl.multiple_of(k * TILE, 32), TILE)
            h1[r, :] = x[r, :].astype(F32) + dot(ob[r, :], W3[3])

        @pl.loop(0, R // 64)
        def _(k):
            r = pl.ds(pl.multiple_of(k * 64, 64), 64)
            unit, _ = unit_rows(h1[r, :])
            a2[r, :] = (unit * gain[1:2, :]).astype(BF16)

    def inner(j):
        @pl.loop(0, WIDE // 256)
        def _(k):
            at = pl.ds(pl.multiple_of(k * 256, 256), 256)
            u = dot(a2[...], W3[4 + j, :, at])
            phi = 0.5 + 0.5 * lax.erf(u * 0.7071067811865476)
            gbr(j)[:, at] = (u * phi).astype(BF16)
            gp[j, :, at] = (phi + u * (jnp.exp(u * u * -0.5) * 0.3989422804014327)).astype(BF16)

    def weight_grad(i, left, right):
        dst = part3(i)

        @pl.loop(0, WIDE // 256)
        def _(k):
            at = pl.ds(pl.multiple_of(k * 256, 256), 256)
            t = lax.dot_general(
                left(at), right(), (((0,), (0,)), ((), ())), preferred_element_type=F32
            )
            dst[at, :] = t.astype(BF16)

    def grad2(j):
        weight_grad(j, lambda at: gbr(j)[:, at], lambda: cot[...])

    def grad1(j):
        weight_grad(4 + j, lambda at: a2[:, at], lambda: gp[j])

    def du(j):
        @pl.loop(0, WIDE // 256)
        def _(k):
            at = pl.ds(pl.multiple_of(k * 256, 256), 256)
            d = lax.dot_general(
                cot[...], W3[8 + j, at, :], (((1,), (1,)), ((), ())), preferred_element_type=F32
            )
            gp[j, :, at] = (d * gp[j, :, at].astype(F32)).astype(BF16)

    def result():
        @pl.loop(0, WIDE // 256)
        def _(k):
            at = pl.ds(pl.multiple_of(k * 256, 256), 256)
            t = h1[:, at]
            for j in range(4):
                t = t + dot(gbr(j)[...], W3[8 + j, :, at])
            obuf[:, at] = t.astype(BF16)

    def hidden_back():
        gain[4:6, :] = jnp.zeros((2, WIDE), F32)

        @pl.loop(0, R // TILE)
        def _(k):
            r = pl.ds(pl.multiple_of(k * TILE, 32), TILE)
            t = lax.dot_general(
                gp[0, r, :], W3[4], (((1,), (1,)), ((), ())), preferred_element_type=F32
            )
            for j in range(1, 4):
                t = t + lax.dot_general(
                    gp[j, r, :], W3[4 + j], (((1,), (1,)), ((), ())), preferred_element_type=F32
                )
            unit, inverse = unit_rows(h1[r, :])
            gain[5:6, :] += jnp.sum(t * unit, axis=0, keepdims=True)
            t = cot[r, :].astype(F32) + back_rows(t, gain[1:2, :], unit, inverse)
            h1[r, :] = t
            obuf[r, :] = t.astype(BF16)

    def mixed_back():
        @pl.loop(0, WIDE // 256)
        def _(k):
            at = pl.ds(pl.multiple_of(k * 256, 256), 256)
            t = lax.dot_general(
                obuf[...], W3[7, at, :], (((1,), (1,)), ((), ())), preferred_element_type=F32
            )
            dob[:, at] = t.astype(BF16)

    def input_back():
        @pl.loop(0, R // TILE)
        def _(k):
            r = pl.ds(pl.multiple_of(k * TILE, 32), TILE)
            t = None
            for u, src in enumerate((Q, K, V)):
                d = lax.dot_general(
                    src[r, :], W3[4 + u], (((1,), (1,)), ((), ())), preferred_element_type=F32
                )
                t = d if t is None else t + d
            unit, inverse = unit_rows(x[r, :].astype(F32))
            gain[4:5, :] += jnp.sum(t * unit, axis=0, keepdims=True)
            t = h1[r, :] + back_rows(t, gain[0:1, :], unit, inverse)
            obuf[r, :] = t.astype(BF16)

    def local(k, src, dst):
        return pltpu.make_async_copy(src, dst, loc.at[k])

    def own_copies():
        pieces = [wq.at[:, pl.ds(k * WIDE, WIDE)] for k in range(3)] + [wp]
        pieces += [w1.at[:, pl.ds(k * WIDE, WIDE)] for k in range(4)]
        pieces += [w2.at[pl.ds(k * n_own, n_own)] for k in range(4)]
        return [
            local(8 + k, piece, h1.at[pl.ds(k * n_own, n_own)]) for k, piece in enumerate(pieces)
        ]

    def spill_copy(u):
        return local(4 + u, W.at[u], spill.at[u])

    def reload_copy(u):
        return local(4 + u, spill.at[u], W.at[4 + u])

    def grant(i):
        for q in p.peers():
            pl.semaphore_signal(credit.at[i], inc=1, device_id=q, device_id_type=MESH)

    shards = own_copies()
    for c in shards:
        c.start()
    place_gains()
    for c in shards[:2]:
        c.wait()
    place_own(0)
    place_own(1)
    pl.semaphore_wait(bar, 6)
    mini.first(0)
    mini.second(0)
    for u in range(2):
        ga.first(u)
        ga.second(u)
    load_rows(0, x_hbm, x)
    load_rows(1, cot_hbm, cot)
    for c in shards[2:]:
        c.wait()
    for u in range(2, NU):
        place_own(u)
        if u < 9:
            ga.second(u)
    mini.g1(0)
    place_codes()
    mini.g2(0)
    tables()
    mini.g3(0)

    @pl.when(vis)
    def _():
        biases()

    mini.g4(0)
    gains()
    wait_rows(0, x_hbm, x)
    wait_rows(1, cot_hbm, cot)
    norm_one()

    def gather_step(s):
        if s + 2 < NU:
            ga.first(s + 2)
        if s + 9 < NU:
            ga.second(s + 9)
        if s < NU:
            ga.g1(s)
        if 0 <= s - 1 < NU:
            ga.g2(s - 1)
        if 0 <= s - 2 < NU:
            ga.g3(s - 2)
        if 0 <= s - 3 < NU:
            ga.g4(s - 3)

    for s in range(NU + 3):
        gather_step(s)
        u = s - 3
        if 0 <= u < 4:
            spill_copy(u).start()
        if 0 <= u < 3:
            project(u)
        if u == 2:
            attend(0, 2)
        if u == 3:
            attend(2, 8)
            pad_forward()
            hidden()
            for k in range(4):
                spill_copy(k).wait()
        if 4 <= u < 8:
            inner(u - 4)
            grad2(u - 4)
        if 8 <= u < 12:
            du(u - 8)
    ga.flush()
    mini.flush()
    for i in range(4):
        grant(i)

    def scatter_open(i):
        pl.semaphore_wait(credit.at[i], 6)
        sc.r0(i)

    def scatter_step(s):
        if s + 1 < NU:
            scatter_open(s + 1)
        if s < NU:
            sc.r1(s)
        if 0 <= s - 1 < NU:
            sc.r2(s - 1)
        if 0 <= s - 2 < NU:
            sc.r3(s - 2)
        if 0 <= s - 3 < NU:
            sc.r4(s - 3)
            sc.flush(s - 3)
            if s - 3 < 4:
                grant(s + 5)

    scatter_open(0)
    result()
    store_rows(2, obuf, out_hbm)
    for i in range(4, 8):
        grant(i)
    scatter_step(0)
    stored_rows(2, obuf, out_hbm)
    hidden_back()
    grad1(0)
    for u in range(4):
        reload_copy(u).start()
    scatter_step(1)
    grad1(1)
    for u in range(4):
        reload_copy(u).wait()
    mixed_back()
    pad_back()
    scatter_step(2)
    attend_back(0, 2)
    scatter_step(3)
    grad1(2)
    attend_back(2, 4)
    scatter_step(4)
    grad1(3)
    attend_back(4, 6)
    scatter_step(5)
    weight_grad(8, lambda at: ob[:, at], lambda: obuf[...])
    attend_back(6, 8)
    scatter_step(6)
    norm_one()
    weight_grad(9, lambda at: gp[0, :, at], lambda: Q[...])
    scatter_step(7)
    weight_grad(10, lambda at: gp[0, :, at], lambda: K[...])
    input_back()
    store_rows(3, obuf, xg_hbm)
    scatter_step(8)
    weight_grad(11, lambda at: gp[0, :, at], lambda: V[...])
    for y in range(2):
        for z in range(4):
            for b in range(2):
                for c in range(2):
                    at = (y * 4 + z) * 128
                    ggp[0, y, z, b, c] = gain[:, at : at + 128]
    msc.r0(0)
    scatter_step(9)
    msc.r1(0)
    scatter_step(10)
    msc.r2(0)
    scatter_step(11)
    msc.r3(0)
    scatter_step(12)
    msc.r4(0)
    scatter_step(13)
    scatter_step(14)
    sc.flush()
    msc.flush()
    stored_rows(3, obuf, xg_hbm)
    came_back(2, obuf, out_hbm)
    came_back(3, obuf, xg_hbm)


def fast_body(
    tokens, w_qkv, w_proj, w_fc1, w_fc2, norm1_gain, norm2_gain, clip_index, frame_index, cotangent
):
    rows, width = tokens.shape
    n = w_qkv.shape[0]
    R = rows + rows // FV * FA
    unit = (2, 4, 2, 2, n, width)
    hbm = pl.BlockSpec(memory_space=pl.ANY)
    vmem = pl.BlockSpec(memory_space=pltpu.VMEM)
    rows_low = pltpu.VMEM((R, width), BF16)
    lanes = pltpu.VMEM((R, 128), F32)
    out, xg, gq, gpr, gf1, gf2, gg, _ = pl.pallas_call(
        layer_kernel,
        out_shape=[
            jax.ShapeDtypeStruct((rows, width), BF16),
            jax.ShapeDtypeStruct((rows, width), BF16),
            jax.ShapeDtypeStruct(w_qkv.shape, F32),
            jax.ShapeDtypeStruct(w_proj.shape, F32),
            jax.ShapeDtypeStruct(w_fc1.shape, F32),
            jax.ShapeDtypeStruct(w_fc2.shape, F32),
            jax.ShapeDtypeStruct((8, 128), F32),
            jax.ShapeDtypeStruct((4,) + unit, BF16),
        ],
        in_specs=[hbm] * 6 + [vmem] * 4,
        out_specs=[hbm, hbm] + [vmem] * 5 + [hbm],
        scratch_shapes=[
            pltpu.VMEM((NU,) + unit, BF16),
            pltpu.VMEM((1, 2, 4, 2, 2, 8, 128), F32),
            pltpu.VMEM((8, -(-R // 128) * 128), F32),
            rows_low,
            rows_low,
            rows_low,
            rows_low,
            rows_low,
            rows_low,
            rows_low,
            pltpu.VMEM((R, width), F32),
            rows_low,
            pltpu.VMEM((3,) + unit, BF16),
            pltpu.VMEM((4, R, width), BF16),
            pltpu.VMEM((4,) + unit, BF16),
            rows_low,
            pltpu.VMEM((R, rows), F32),
            lanes,
            lanes,
            lanes,
            pltpu.VMEM((8, 8, 256), F32),
            lanes,
            lanes,
            pltpu.VMEM((8, width), F32),
            pltpu.VMEM((1, 2, 4, 2, 2, 8, 128), F32),
            pltpu.VMEM((32, 8, 128), F32),
            pltpu.SemaphoreType.DMA((NU, 17)),
            pltpu.SemaphoreType.DMA((NU, 17)),
            pltpu.SemaphoreType.DMA((1, 17)),
            pltpu.SemaphoreType.DMA((1, 17)),
            pltpu.SemaphoreType.DMA((NU, 12)),
            pltpu.SemaphoreType.DMA((NU, 12)),
            pltpu.SemaphoreType.DMA((1, 12)),
            pltpu.SemaphoreType.DMA((1, 12)),
            pltpu.SemaphoreType.DMA((4,)),
            pltpu.SemaphoreType.DMA((4,)),
            pltpu.SemaphoreType.DMA((20,)),
            pltpu.SemaphoreType.REGULAR((NU,)),
        ],
        compiler_params=pltpu.CompilerParams(
            collective_id=0, has_side_effects=True, vmem_limit_bytes=VMEM_LIMIT
        ),
    )(
        tokens,
        cotangent,
        w_qkv,
        w_proj,
        w_fc1,
        w_fc2,
        norm1_gain.reshape(1, n),
        norm2_gain.reshape(1, n),
        clip_index.reshape(rows // 128, 128),
        frame_index.reshape(rows // 128, 128),
    )
    gains = lax.dynamic_slice(gg[4:6], (0, lax.axis_index("clip") % 4 * n), (2, n))
    return out, xg, gq, gpr, gf1, gf2, gains[0], gains[1]


def solution(mesh):
    placed = (
        P(("stream", "clip"), None),
        P(("stream", "clip"), None),
        P(("stream", "clip"), None),
        P(("stream", "clip"), None),
        P(("stream", "clip"), None),
        P(("stream", "clip")),
        P(("stream", "clip")),
        P(("stream", "clip")),
        P(("stream", "clip")),
        P(("stream", "clip"), None),
    )
    block = mesh.shape["stream"] == 2 and mesh.shape["clip"] == 16
    return jax.shard_map(
        fast_body if block else body,
        mesh=mesh,
        in_specs=placed,
        out_specs=(
            P(("stream", "clip"), None),
            P(("stream", "clip"), None),
            P(("stream", "clip"), None),
            P(("stream", "clip"), None),
            P(("stream", "clip"), None),
            P(("stream", "clip"), None),
            P(("stream", "clip")),
            P(("stream", "clip")),
        ),
        check_vma=False,
    )
```

```python
import jax
import jax.numpy as jnp
from jax import lax
from jax.experimental import pallas as pl
from jax.experimental.pallas import tpu as pltpu
from jax.sharding import PartitionSpec as P

HD = 64
RT = 16
GW = 4
FA = 2
FV = 16


EPSILON = 1e-06
THETA = 10000.0
MASKED = -1e30
LOG_THETA = 9.210340371976184
VMEM_LIMIT = 63 * 1024 * 1024


def shifted(value, axis, steps):
    count = lax.axis_size(axis)
    initial, last = (max(0, -steps), min(count, count - steps))
    return lax.ppermute(value, axis, [(source, source + steps) for source in range(initial, last)])


def frequencies(width):
    counter = jnp.arange(width // 2).astype(jnp.float32)
    return jnp.power(THETA, -2.0 * counter / width)


def angle_sets(frames, visual_flag, rows):
    place = jnp.arange(rows)
    inner = place % FV
    down_pos = inner // GW * visual_flag
    across_pos = inner % GW * visual_flag
    side = (HD - RT) // 2
    time_angles = frames.astype(jnp.float32)[:, None] * frequencies(RT)[None, :]
    down_angles = down_pos.astype(jnp.float32)[:, None] * frequencies(side)[None, :]
    across_angles = across_pos.astype(jnp.float32)[:, None] * frequencies(side)[None, :]
    return (time_angles, down_angles, across_angles)


def rotate(block, angles):
    half = block.shape[-1] // 2
    cosine = jnp.cos(angles)[:, None, :]
    sine = jnp.sin(angles)[:, None, :]
    first = block[..., :half]
    second = block[..., half:]
    return jnp.concatenate(
        [first * cosine - second * sine, first * sine + second * cosine], axis=-1
    )


def rotary(flat, sets, sign):
    rows = flat.shape[0]
    block = flat.reshape(rows, flat.shape[1] // HD, HD)
    side = (HD - RT) // 2
    pieces = (block[..., :RT], block[..., RT : RT + side], block[..., RT + side :])
    turned = [rotate(piece, sign * angles) for piece, angles in zip(pieces, sets)]
    return jnp.concatenate(turned, axis=-1).reshape(rows, -1)


def normalize(values, gain):
    centred = values - jnp.mean(values, axis=-1, keepdims=True)
    inverse = lax.rsqrt(jnp.mean(centred * centred, axis=-1, keepdims=True) + EPSILON)
    unit = centred * inverse
    return (unit * gain, unit, inverse)


def norm_back(grad_out, gain, unit, inverse):
    scaled = grad_out * gain
    centred = (
        scaled
        - jnp.mean(scaled, axis=-1, keepdims=True)
        - unit * jnp.mean(scaled * unit, axis=-1, keepdims=True)
    )
    return (inverse * centred, jnp.sum(grad_out * unit, axis=0))


def local_mask(clips, frames):
    rows = clips.shape[0]
    same = (
        (clips[:, None] == clips[None, :])
        & (clips[:, None] >= 0)
        & (frames[None, :] <= frames[:, None])
    )
    return same | (jnp.arange(rows)[:, None] == jnp.arange(rows)[None, :])


def cross_mask(clips, frames, far_clips, far_frames):
    return (
        (clips[:, None] == far_clips[None, :])
        & (clips[:, None] >= 0)
        & (far_frames[None, :] <= frames[:, None])
    )


def times_transpose(left, right):
    return lax.dot_general(
        left, right, (((1,), (1,)), ((), ())), preferred_element_type=jnp.float32
    )


def transpose_times(left, right):
    return lax.dot_general(
        left, right, (((0,), (0,)), ((), ())), preferred_element_type=jnp.float32
    )


def head_scores(query_part, key_part, allowed):
    query_heads = query_part.reshape(query_part.shape[0], 2, HD)
    key_heads = key_part.reshape(key_part.shape[0], 2, HD)
    scores = jnp.einsum(
        "qhd,khd->hqk", query_heads, key_heads, preferred_element_type=jnp.float32
    ) * HD ** (-0.5)
    return (jnp.where(allowed[None], scores, MASKED), query_heads, key_heads)


def attend_forward(query_part, key_part, value_part, allowed):
    rows = query_part.shape[0]
    scores, query_heads, key_heads = head_scores(query_part, key_part, allowed)
    peak = jnp.max(scores, axis=-1, keepdims=True)
    weights = jnp.exp(scores - peak)
    total = jnp.sum(weights, axis=-1, keepdims=True)
    probs = (weights / total).astype(jnp.bfloat16)
    value_heads = value_part.reshape(value_part.shape[0], 2, HD)
    mixed = jnp.einsum("hqk,khd->qhd", probs, value_heads, preferred_element_type=jnp.float32)
    return (mixed.reshape(rows, 2 * HD), (peak + jnp.log(total))[..., 0])


def attend_back(query_part, key_part, value_part, grad_part, allowed, log_total):
    rows = query_part.shape[0]
    scores, query_heads, key_heads = head_scores(query_part, key_part, allowed)
    probs = jnp.exp(scores - log_total[..., None])
    value_heads = value_part.reshape(value_part.shape[0], 2, HD)
    grad_heads = grad_part.reshape(rows, 2, HD)
    grad_probs = jnp.einsum(
        "qhd,khd->hqk", grad_heads, value_heads, preferred_element_type=jnp.float32
    )
    centre = jnp.sum(probs * grad_probs, axis=-1, keepdims=True)
    grad_scores = (probs * (grad_probs - centre)).astype(jnp.bfloat16)
    factor = HD ** (-0.5)
    grad_query = (
        jnp.einsum("hqk,khd->qhd", grad_scores, key_heads, preferred_element_type=jnp.float32)
        * factor
    )
    grad_key = (
        jnp.einsum("hqk,qhd->khd", grad_scores, query_heads, preferred_element_type=jnp.float32)
        * factor
    )
    grad_value = jnp.einsum(
        "hqk,qhd->khd", probs.astype(jnp.bfloat16), grad_heads, preferred_element_type=jnp.float32
    )
    key_count = key_part.shape[0]
    return (
        grad_query.reshape(rows, 2 * HD),
        grad_key.reshape(key_count, 2 * HD),
        grad_value.reshape(key_count, 2 * HD),
    )


def column_block(array, group_index):
    return lax.dynamic_slice_in_dim(array, group_index * 2 * HD, 2 * HD, 1)


def join_groups(stacked):
    return jnp.transpose(stacked, (1, 0, 2)).reshape(stacked.shape[1], -1)


def body(
    tokens, w_qkv, w_proj, w_fc1, w_fc2, norm1_gain, norm2_gain, clip_index, frame_index, cotangent
):
    rows = tokens.shape[0]
    width = tokens.shape[1]
    groups = width // (2 * HD)
    visual = lax.axis_index("stream") == 1
    visual_flag = visual.astype(jnp.int32)
    shards = (
        w_qkv.astype(jnp.bfloat16),
        w_proj.astype(jnp.bfloat16),
        w_fc1.astype(jnp.bfloat16),
        w_fc2.astype(jnp.bfloat16),
        norm1_gain.astype(jnp.bfloat16),
        norm2_gain.astype(jnp.bfloat16),
    )
    full_qkv, full_proj, full_fc1, full_fc2, gain_one, gain_two = (
        lax.all_gather(shards[0], ("stream", "clip"), axis=0, tiled=True),
        lax.all_gather(shards[1], ("stream", "clip"), axis=0, tiled=True),
        lax.all_gather(shards[2], ("stream", "clip"), axis=0, tiled=True),
        lax.all_gather(shards[3], ("stream", "clip"), axis=0, tiled=True),
        lax.all_gather(shards[4], ("stream", "clip"), axis=0, tiled=True),
        lax.all_gather(shards[5], ("stream", "clip"), axis=0, tiled=True),
    )
    gain_first = gain_one.astype(jnp.float32)
    gain_second = gain_two.astype(jnp.float32)
    values_in = tokens.astype(jnp.float32)
    normed, unit_one, inverse_one = normalize(values_in, gain_first)
    normed_b = normed.astype(jnp.bfloat16)
    projected = jnp.dot(normed_b, full_qkv, preferred_element_type=jnp.float32)
    sets = angle_sets(frame_index, visual_flag, rows)
    queries = rotary(projected[:, :width], sets, 1.0).astype(jnp.bfloat16)
    key_rows = rotary(projected[:, width : 2 * width], sets, 1.0).astype(jnp.bfloat16)
    values = projected[:, 2 * width :].astype(jnp.bfloat16)
    frames_row = rows // FV
    cond_rows = frames_row * FA
    near_keys, near_values = shifted((key_rows[:cond_rows], values[:cond_rows]), "stream", 1)
    far_keys, far_values = shifted((key_rows, values), "stream", -1)
    clip_seen = clip_index.reshape(frames_row, FV)[:, 0]
    clip_cond = clip_index[:cond_rows].reshape(frames_row, FA)[:, 0]
    frame_seen = frame_index.reshape(frames_row, FV)[:, 0]
    frame_cond = frame_index[:cond_rows].reshape(frames_row, FA)[:, 0]
    frame_clip = jnp.where(visual, clip_seen, clip_cond)
    frame_num = jnp.where(visual, frame_seen, frame_cond)
    partner_cond = (
        cross_mask(clip_index, frame_index, jnp.repeat(frame_clip, FA), jnp.repeat(frame_num, FA))
        & visual
    )
    partner_seen = cross_mask(
        clip_index, frame_index, jnp.repeat(frame_clip, FV), jnp.repeat(frame_num, FV)
    ) & jnp.logical_not(visual)
    allowed = jnp.concatenate(
        [partner_cond, partner_seen, local_mask(clip_index, frame_index)], axis=1
    )
    key_all = jnp.concatenate([near_keys, far_keys, key_rows], axis=0)
    value_all = jnp.concatenate([near_values, far_values, values], axis=0)

    def forward_group(group_index):
        return attend_forward(
            column_block(queries, group_index),
            column_block(key_all, group_index),
            column_block(value_all, group_index),
            allowed,
        )

    mixed_groups, log_totals = lax.map(forward_group, jnp.arange(groups))
    mixed_b = join_groups(mixed_groups).astype(jnp.bfloat16)
    hidden_one = values_in + jnp.dot(mixed_b, full_proj, preferred_element_type=jnp.float32)
    normed_two, unit_two, inverse_two = normalize(hidden_one, gain_second)
    normed_two_b = normed_two.astype(jnp.bfloat16)
    inner = jnp.dot(normed_two_b, full_fc1, preferred_element_type=jnp.float32)
    active, gelu_pull = jax.vjp(lambda given: jax.nn.gelu(given, approximate=False), inner)
    active_b = active.astype(jnp.bfloat16)
    result = hidden_one + jnp.dot(active_b, full_fc2, preferred_element_type=jnp.float32)
    full_qkv, full_proj, full_fc1, full_fc2, gain_one, gain_two = (
        lax.all_gather(shards[0], ("stream", "clip"), axis=0, tiled=True),
        lax.all_gather(shards[1], ("stream", "clip"), axis=0, tiled=True),
        lax.all_gather(shards[2], ("stream", "clip"), axis=0, tiled=True),
        lax.all_gather(shards[3], ("stream", "clip"), axis=0, tiled=True),
        lax.all_gather(shards[4], ("stream", "clip"), axis=0, tiled=True),
        lax.all_gather(shards[5], ("stream", "clip"), axis=0, tiled=True),
    )
    gain_first = gain_one.astype(jnp.float32)
    gain_second = gain_two.astype(jnp.float32)
    grad_out = cotangent.astype(jnp.float32)
    grad_fc2 = transpose_times(active_b, cotangent)
    grad_active = times_transpose(cotangent, full_fc2)
    grad_inner = gelu_pull(grad_active)[0].astype(jnp.bfloat16)
    grad_fc1 = transpose_times(normed_two_b, grad_inner)
    grad_normed_two = times_transpose(grad_inner, full_fc1)
    back_two, grad_gain2 = norm_back(grad_normed_two, gain_second, unit_two, inverse_two)
    grad_hidden = grad_out + back_two
    grad_attn = grad_hidden.astype(jnp.bfloat16)
    grad_proj = transpose_times(mixed_b, grad_attn)
    grad_mixed = times_transpose(grad_attn, full_proj).astype(jnp.bfloat16)

    def backward_group(inputs):
        group_index, log_total = inputs
        return attend_back(
            column_block(queries, group_index),
            column_block(key_all, group_index),
            column_block(value_all, group_index),
            column_block(grad_mixed, group_index),
            allowed,
            log_total,
        )

    grad_q_groups, grad_k_groups, grad_v_groups = lax.map(
        backward_group, (jnp.arange(groups), log_totals)
    )
    grad_queries = join_groups(grad_q_groups)
    grad_key_all = join_groups(grad_k_groups)
    grad_value_all = join_groups(grad_v_groups)
    outer = cond_rows + rows
    cond_keys_back, cond_values_back = (
        shifted(grad_key_all[:cond_rows].astype(jnp.bfloat16), "stream", -1).astype(jnp.float32),
        shifted(grad_value_all[:cond_rows].astype(jnp.bfloat16), "stream", -1).astype(jnp.float32),
    )
    seen_keys_back, seen_values_back = (
        shifted(grad_key_all[cond_rows:outer].astype(jnp.bfloat16), "stream", 1).astype(
            jnp.float32
        ),
        shifted(grad_value_all[cond_rows:outer].astype(jnp.bfloat16), "stream", 1).astype(
            jnp.float32
        ),
    )
    filler = jnp.zeros((rows - cond_rows, width), jnp.float32)
    grad_keys = (
        grad_key_all[outer:] + seen_keys_back + jnp.concatenate([cond_keys_back, filler], axis=0)
    )
    grad_values = (
        grad_value_all[outer:]
        + seen_values_back
        + jnp.concatenate([cond_values_back, filler], axis=0)
    )
    grad_projected = jnp.concatenate(
        [rotary(grad_queries, sets, -1.0), rotary(grad_keys, sets, -1.0), grad_values], axis=1
    ).astype(jnp.bfloat16)
    grad_qkv = transpose_times(normed_b, grad_projected)
    grad_normed = times_transpose(grad_projected, full_qkv)
    back_one, grad_gain1 = norm_back(grad_normed, gain_first, unit_one, inverse_one)
    input_grad = (grad_hidden + back_one).astype(jnp.bfloat16)
    sums = (
        lax.psum_scatter(grad_qkv, ("stream", "clip"), scatter_dimension=0, tiled=True),
        lax.psum_scatter(grad_proj, ("stream", "clip"), scatter_dimension=0, tiled=True),
        lax.psum_scatter(grad_fc1, ("stream", "clip"), scatter_dimension=0, tiled=True),
        lax.psum_scatter(grad_fc2, ("stream", "clip"), scatter_dimension=0, tiled=True),
        lax.psum_scatter(grad_gain1, ("stream", "clip"), scatter_dimension=0, tiled=True),
        lax.psum_scatter(grad_gain2, ("stream", "clip"), scatter_dimension=0, tiled=True),
    )
    return (
        result.astype(jnp.bfloat16),
        input_grad,
        sums[0],
        sums[1],
        sums[2],
        sums[3],
        sums[4],
        sums[5],
    )


MESH = pl.DeviceIdType.MESH
F32 = jnp.float32
BF16 = jnp.bfloat16
MB = 1 << 20
NU = 12
ORDER = (8, 9, 10, 11, 4, 5, 6, 7, 3, 0, 1, 2)
WIDE = 1024
NEG = -1e30


class Place:
    def __init__(self):
        self.y = lax.axis_index("stream")
        clip = lax.axis_index("clip")
        self.z, self.x, self.c = clip // 4, (clip // 2) % 2, clip % 2
        self.X = self.dev(self.y, self.z, 1 - self.x, self.c)
        self.Y = self.dev(1 - self.y, self.z, self.x, self.c)
        self.C = self.dev(self.y, self.z, self.x, 1 - self.c)

    def dev(self, y, z, x, c):
        return (y, z * 4 + x * 2 + c)

    def up(self, d):
        return lax.rem(self.z + d, 4)

    def above(self, d):
        return self.dev(self.y, self.up(d), self.x, self.c)

    def peers(self):
        return [self.X, self.Y, self.C] + [self.above(d) for d in (1, 2, 3)]


class Link:
    def __init__(self, place, sent, got):
        self.p, self.sent, self.got, self.open = place, sent, got, []

    def copy(self, u, slot, src, dst, to):
        return pltpu.make_async_remote_copy(
            src_ref=src,
            dst_ref=dst,
            send_sem=self.sent.at[u, slot],
            recv_sem=self.got.at[u, slot],
            device_id=to,
            device_id_type=MESH,
        )

    def send(self, u, slot, src, dst, to):
        c = self.copy(u, slot, src, dst, to)
        c.start()
        self.open.append((u, c))

    def recv(self, u, slot, dst):
        self.copy(u, slot, dst, dst, self.p.X).wait_recv()

    def flush(self, unit=None):
        rest = []
        for u, c in self.open:
            if unit is None or u == unit:
                c.wait_send()
            else:
                rest.append((u, c))
        self.open = rest


class Gather(Link):
    def __init__(self, place, whole, sent, got):
        super().__init__(place, sent, got)
        self.W = whole

    def first(self, u):
        p = self.p
        me = self.W.at[u, p.y, p.z, p.x, p.c]
        for d in (1, 2, 3):
            self.send(u, d - 1, me, me, p.above(d))

    def second(self, u):
        p = self.p
        me = self.W.at[u, p.y, p.z, p.x, p.c]
        self.send(u, 3, me, me, p.X)
        self.send(u, 7, me, me, p.Y)

    def g1(self, u):
        p, W = self.p, self.W
        for d in (1, 2, 3):
            b = W.at[u, p.y, p.up(4 - d), p.x, p.c]
            self.recv(u, d - 1, b)
            self.send(u, 3 + d, b, b, p.X)
            self.send(u, 7 + d, b, b, p.Y)
        b = W.at[u, p.y, :, p.x, p.c]
        self.send(u, 13, b, b, p.C)

    def g2(self, u):
        p, W = self.p, self.W
        for k in range(4):
            z = p.up(4 - k)
            self.recv(u, 3 + k, W.at[u, p.y, z, 1 - p.x, p.c])
            self.recv(u, 7 + k, W.at[u, 1 - p.y, z, p.x, p.c])
        b = W.at[u, p.y, pl.ds(0, 2), 1 - p.x, p.c]
        self.send(u, 11, b, b, p.Y)
        b = W.at[u, 1 - p.y, pl.ds(2, 2), p.x, p.c]
        self.send(u, 12, b, b, p.X)
        b = W.at[u, p.y, :, 1 - p.x, p.c]
        self.send(u, 14, b, b, p.C)
        b = W.at[u, 1 - p.y, :, p.x, p.c]
        self.send(u, 15, b, b, p.C)

    def g3(self, u):
        p, W = self.p, self.W
        self.recv(u, 11, W.at[u, 1 - p.y, pl.ds(0, 2), 1 - p.x, p.c])
        self.recv(u, 12, W.at[u, 1 - p.y, pl.ds(2, 2), 1 - p.x, p.c])
        b = W.at[u, 1 - p.y, :, 1 - p.x, p.c]
        self.send(u, 16, b, b, p.C)

    def g4(self, u):
        p, W = self.p, self.W
        o = 1 - p.c
        self.recv(u, 13, W.at[u, p.y, :, p.x, o])
        self.recv(u, 14, W.at[u, p.y, :, 1 - p.x, o])
        self.recv(u, 15, W.at[u, 1 - p.y, :, p.x, o])
        self.recv(u, 16, W.at[u, 1 - p.y, :, 1 - p.x, o])


    def plane(self, u, z, c):
        return self.W.at[u, :, z, :, c]

    def line0(self, u):
        p = self.p
        me = self.W.at[u, p.y, p.z, p.x, p.c]
        self.send(u, 0, me, me, p.X)
        self.send(u, 1, me, me, p.Y)

    def line1(self, u):
        p, W = self.p, self.W
        h = W.shape[-2] // 2
        bx = W.at[u, p.y, p.z, 1 - p.x, p.c]
        by = W.at[u, 1 - p.y, p.z, p.x, p.c]
        self.recv(u, 0, bx)
        self.send(u, 2, bx.at[pl.ds(0, h)], bx.at[pl.ds(0, h)], p.Y)
        self.recv(u, 1, by)
        self.send(u, 3, by.at[pl.ds(h, h)], by.at[pl.ds(h, h)], p.X)

    def line2(self, u):
        p = self.p
        h = self.W.shape[-2] // 2
        bd = self.W.at[u, 1 - p.y, p.z, 1 - p.x, p.c]
        self.recv(u, 2, bd.at[pl.ds(0, h)])
        self.recv(u, 3, bd.at[pl.ds(h, h)])
        self.pass_on(u, 0)
        b = self.plane(u, p.z, p.c)
        self.send(u, 10, b, b, p.C)

    def ways(self, k):
        p = self.p
        return (
            (4 + k, 10 + k, p.z - k, p.z - k >= 0, p.z < 3, p.dev(p.y, p.z + 1, p.x, p.c)),
            (7 + k, 13 + k, p.z + k, p.z + k <= 3, p.z > 0, p.dev(p.y, p.z - 1, p.x, p.c)),
        )

    def pass_on(self, u, k):
        for slot, _, z, there, more, to in self.ways(k):
            @pl.when(there & more)
            def _():
                b = self.plane(u, z, self.p.c)
                self.copy(u, slot, b, b, to).start()

    def line3(self, u, k):
        for slot, core, z, there, _, _ in self.ways(k):
            @pl.when(there)
            def _():
                b = self.plane(u, z, self.p.c)
                self.recv(u, slot - 1, b)
                self.copy(u, core, b, b, self.p.C).start()
        if k < 3:
            self.pass_on(u, k)

    def line4(self, u):
        p = self.p
        self.recv(u, 10, self.plane(u, p.z, 1 - p.c))
        for k in (1, 2, 3):
            for _, core, z, there, _, _ in self.ways(k):
                @pl.when(there)
                def _():
                    self.recv(u, core, self.plane(u, z, 1 - p.c))

    def line_flush(self, u):
        for k in range(4):
            for slot, core, z, there, more, to in self.ways(k):
                b = self.plane(u, 0, 0)
                if k < 3:
                    @pl.when(there & more)
                    def _():
                        self.copy(u, slot, b, b, to).wait_send()
                if k > 0:
                    @pl.when(there)
                    def _():
                        self.copy(u, core, b, b, self.p.C).wait_send()


class Scatter(Link):
    def __init__(self, place, part, land, out, sent, got):
        super().__init__(place, sent, got)
        self.part, self.land, self.out = part, land, out

    def halves(self):
        p = self.p
        return (
            (pl.ds(0, 512), p.y, p.x, p.Y, p.X, lambda a, b: (a, b)),
            (pl.ds(512, 512), p.x, p.y, p.X, p.Y, lambda a, b: (b, a)),
        )

    def h1(self, i):
        p, q, c = self.p, self.part(i), self.p.c
        for k, (a, b) in enumerate(((1 - p.y, 1 - p.x), (1 - p.y, p.x), (p.y, 1 - p.x))):
            self.recv(i, k, self.col(i, a, b))
        for n, (half, mine, other, A, B, order) in enumerate(self.halves()):
            for bb in range(2):
                y, x = order(1 - mine, bb)
                own = lambda k: q.at[y, k, x, c, :, half]
                self.add(4, own, own, lambda k: self.blk(i, y, x, k).at[:, half])
                self.send(
                    i,
                    4 + 2 * n + bb,
                    q.at[y, :, x, c, :, half],
                    self.land(i, 16 + 4 * bb, 4).at[:, :, half],
                    A,
                )

    def h2(self, i):
        p, q, c = self.p, self.part(i), self.p.c
        self.recv(i, 3, self.col(i, p.y, p.x))
        for n, (half, mine, other, A, B, order) in enumerate(self.halves()):
            for bb in range(2):
                self.recv(i, 4 + 2 * n + bb, self.land(i, 16 + 4 * bb, 4).at[:, :, half])
                y, x = order(mine, bb)
                own = lambda k: q.at[y, k, x, c, :, half]
                self.add(
                    4,
                    own,
                    own,
                    lambda k: self.blk(i, y, x, k).at[:, half],
                    lambda k: self.land(i, 16 + 4 * bb + k, 1).at[0, :, half],
                )
            for d in (1, 2, 3):
                z = p.up(d)
                src = q.at[p.y, z, :, c, :, half] if n == 0 else q.at[:, z, p.x, c, :, half]
                self.send(
                    i, 7 + 3 * n + d, src, self.land(i, 22 + 2 * d, 2).at[:, :, half], p.above(d)
                )

    def h3(self, i):
        p, q, c = self.p, self.part(i), self.p.c
        for n, (half, mine, other, A, B, order) in enumerate(self.halves()):
            for d in (1, 2, 3):
                self.recv(i, 7 + 3 * n + d, self.land(i, 22 + 2 * d, 2).at[:, :, half])
            for bb in (1 - other, other):
                y, x = order(mine, bb)
                d = q.at[y, p.z, x, c, :, half]
                t = d[...].astype(F32)
                for k in (1, 2, 3):
                    t = t + self.land(i, 22 + 2 * k + bb, 1)[0, :, half].astype(F32)
                d[...] = t.astype(d.dtype)
            y, x = order(mine, 1 - other)
            self.send(
                i, 14 + n, q.at[y, p.z, x, c, :, half], self.land(i, 30, 1).at[0, :, half], B
            )

    def h4(self, i):
        p = self.p
        for n, (half, *_) in enumerate(self.halves()):
            self.recv(i, 14 + n, self.land(i, 30, 1).at[0, :, half])
        t = self.part(i)[p.y, p.z, p.x, p.c].astype(F32) + self.land(i, 30, 1)[0].astype(F32)
        self.out(i, t)

    def col(self, i, a, b):
        return self.land(i, (a * 2 + b) * 4, 4)

    def blk(self, i, a, b, z):
        return self.land(i, (a * 2 + b) * 4 + z, 1).at[0]

    def add(self, n, dst, *srcs):
        @pl.loop(0, n)
        def _(k):
            t = srcs[0](k)[...].astype(F32)
            for r in srcs[1:]:
                t = t + r(k)[...].astype(F32)
            d = dst(k)
            d[...] = t.astype(d.dtype)

    def r0(self, i):
        p = self.p
        y, x, o, q = p.y, p.x, 1 - p.c, self.part(i)
        for k, (a, b) in enumerate(((1 - y, 1 - x), (1 - y, x), (y, 1 - x), (y, x))):
            self.send(i, k, q.at[a, :, b, o], self.col(i, a, b), p.C)

    def r1(self, i):
        p = self.p
        y, x, c, q = p.y, p.x, p.c, self.part(i)
        self.recv(i, 0, self.col(i, 1 - y, 1 - x))
        own = lambda k: q.at[1 - y, k, 1 - x, c]
        self.add(4, own, own, lambda k: self.blk(i, 1 - y, 1 - x, k))
        self.send(i, 4, q.at[1 - y, pl.ds(0, 2), 1 - x, c], self.land(i, 16, 2), p.X)
        self.send(i, 5, q.at[1 - y, pl.ds(2, 2), 1 - x, c], self.land(i, 18, 2), p.Y)

    def r2(self, i):
        p = self.p
        y, x, c, q = p.y, p.x, p.c, self.part(i)
        self.recv(i, 1, self.col(i, 1 - y, x))
        self.recv(i, 2, self.col(i, y, 1 - x))
        ny = lambda k: q.at[1 - y, k, x, c]
        my = lambda k: self.blk(i, 1 - y, x, k)
        nx = lambda k: q.at[y, k, 1 - x, c]
        mx = lambda k: self.blk(i, y, 1 - x, k)
        self.add(2, lambda k: ny(k + 2), lambda k: ny(k + 2), lambda k: my(k + 2))
        self.add(2, nx, nx, mx)
        self.recv(i, 4, self.land(i, 16, 2))
        self.add(2, ny, ny, my, lambda k: self.land(i, 16 + k, 1).at[0])
        self.send(i, 6, q.at[1 - y, :, x, c], self.land(i, 28, 4), p.Y)
        self.recv(i, 5, self.land(i, 18, 2))
        self.add(
            2,
            lambda k: nx(k + 2),
            lambda k: nx(k + 2),
            lambda k: mx(k + 2),
            lambda k: self.land(i, 18 + k, 1).at[0],
        )
        self.send(i, 7, q.at[y, :, 1 - x, c], self.land(i, 24, 4), p.X)

    def r3(self, i):
        p = self.p
        y, x, c, q = p.y, p.x, p.c, self.part(i)
        self.recv(i, 3, self.col(i, y, x))
        self.recv(i, 6, self.land(i, 28, 4))
        self.recv(i, 7, self.land(i, 24, 4))
        own = lambda k: q.at[y, k, x, c]
        self.add(
            4,
            own,
            own,
            lambda k: self.blk(i, y, x, k),
            lambda k: self.land(i, 28 + k, 1).at[0],
            lambda k: self.land(i, 24 + k, 1).at[0],
        )
        for d in (1, 2, 3):
            self.send(i, 8 + d, q.at[y, p.up(d), x, c], self.land(i, 19 + d, 1).at[0], p.above(d))

    def r4(self, i):
        p = self.p
        q = self.part(i)
        for d in (1, 2, 3):
            self.recv(i, 8 + d, self.land(i, 19 + d, 1).at[0])
        t = q[p.y, p.z, p.x, p.c].astype(F32)
        for d in (1, 2, 3):
            t = t + self.land(i, 19 + d, 1)[0].astype(F32)
        self.out(i, t)


def unit_rows(v):
    centred = v - jnp.mean(v, axis=-1, keepdims=True)
    inverse = lax.rsqrt(jnp.mean(centred * centred, axis=-1, keepdims=True) + EPSILON)
    return centred * inverse, inverse


def back_rows(d, gain, unit, inverse):
    e = d * gain
    return inverse * (
        e - jnp.mean(e, axis=-1, keepdims=True) - unit * jnp.mean(e * unit, axis=-1, keepdims=True)
    )


def dot(a, b):
    return jnp.dot(a, b, preferred_element_type=F32)


def head_moves():
    side = (HD - RT) // 2
    moves = []
    for head in range(2):
        src, dst = head * HD, head * 32
        for at, part in ((0, RT), (RT, side), (RT + side, side)):
            moves.append((src + at, dst, part // 2))
            moves.append((src + at + part // 2, dst + 64, part // 2))
            dst += part // 2
    return moves


def move_lanes(pieces, lane):
    out = None
    for v, a, b, n in pieces:
        t = v if a == b else pltpu.roll(v, (b - a) % 128, 1)
        out = t if out is None else jnp.where((lane >= b) & (lane < b + n), t, out)
    return out


def rope_lane(shape):
    lane = lax.broadcasted_iota(jnp.int32, shape, 1)
    return lane, lane % 32


def layer_kernel(
    x_hbm, cot_hbm, wq, wp, w1, w2, g1, g2, clips, frames,
    out_hbm, xg_hbm, gq, gpr, gf1, gf2, gg, spill,
    W, G, codes, x, cot, Q, K, V, ob, dob, h1, a2, gbuf, gp, PS, obuf,
    bias, cbias, ct, st, lse, dk, dv, gain, ggp, gland,
    ss, rs, gss, grs, sss, srs, mss, mrs, xss, xrs, loc, credit,
):
    p = Place()
    vis = p.y == 1
    rows = x_hbm.shape[0]
    R = x.shape[0]
    C = R - rows
    TILE = R // 2
    n_own = wq.shape[0]
    W3 = W.reshape(NU, WIDE, WIDE)
    Wf = W.reshape(NU, 32, 32, WIDE)
    gflat = gbuf.reshape(2 * WIDE, WIDE)
    P3 = PS.reshape(4, WIDE, WIDE)
    H3 = gbuf.reshape(2, WIDE, WIDE)

    pflat = gp.reshape(3 * WIDE, WIDE)
    D3 = gp.reshape(3, WIDE, WIDE)

    def dur(j):
        return pflat.at[pl.ds(j * R, R)]

    def gbr(j):
        return gflat.at[pl.ds(j * R, R)] if j < 3 else dob

    def slot(i):
        return (0, i) if i < 4 else (1, i - 4) if i < 6 else (0, i - 6) if i < 10 else (2, i - 9)

    def part(i):
        k, n = slot(i)
        return (PS, gbuf, gp)[k].at[n]

    def part3(i):
        k, n = slot(i)
        return (P3, H3, D3)[k].at[n]

    def land(i, at, n):
        u = i if i < 4 else i + 4 if i < 8 else i - 8
        return Wf.at[u, pl.ds(at, n)]

    def finish(i, t):
        u = ORDER[i]
        lane = lax.broadcasted_iota(jnp.int32, (n_own, 128), 1)
        if u < 2:
            for k in range(8):
                v = t[:, k * 128 : (k + 1) * 128]
                at = u * WIDE + k * 128
                gq[:, at : at + 128] = move_lanes([(v, b, a, n) for a, b, n in head_moves()], lane)
        elif u == 2:
            gq[:, 2 * WIDE :] = t
        elif u == 3:
            gpr[...] = t
        elif u < 8:
            for h in range(2):
                bias[pl.ds((2 * u - 8 + h) * n_own, n_own), :] = t[:, h * 512 : (h + 1) * 512]
            if u == 7:
                for g in range(8):
                    at = slice(g % 4 * 128, (g % 4 + 1) * 128)
                    vs = [
                        bias[pl.ds((2 * j + g // 4) * n_own, n_own), at] for j in range(4)
                    ]
                    for a in range(4):
                        at = g * 512 + a * 128
                        gf1[:, at : at + 128] = move_lanes(
                            [(vs[j], 32 * a, 32 * j, 32) for j in range(4)], lane
                        )
        else:
            gf2[(u - 8) * n_own : (u - 7) * n_own, :] = t

    def finish_gains(i, t):
        gg[...] = t

    ga = Gather(p, W, ss, rs)
    mini = Gather(p, G, gss, grs)
    sc = Scatter(p, part, land, finish, sss, srs)
    msc = Scatter(
        p, lambda i: ggp.at[0], lambda i, at, n: gland.at[pl.ds(at, n)], finish_gains, mss, mrs
    )

    bar = pltpu.get_barrier_semaphore()
    for q in p.peers():
        pl.semaphore_signal(bar, inc=1, device_id=q, device_id_type=MESH)

    def xcopy(k, src, dst):
        return pltpu.make_async_remote_copy(
            src_ref=src, dst_ref=dst, send_sem=xss.at[k], recv_sem=xrs.at[k],
            device_id=p.Y, device_id_type=MESH,
        )

    def load_rows(k, src, dst):
        @pl.when(vis)
        def _():
            local(k, src, dst.at[pl.ds(C, rows)]).start()

        @pl.when(p.y == 0)
        def _():
            xcopy(k, src.at[pl.ds(0, C)], dst.at[pl.ds(0, C)]).start()
            local(k, src.at[pl.ds(C, rows - C)], dst.at[pl.ds(2 * C, rows - C)]).start()
            dst[0 : 2 * C, :] = jnp.zeros((2 * C, WIDE), BF16)

    def wait_rows(k, src, dst):
        @pl.when(vis)
        def _():
            local(k, src, dst.at[pl.ds(C, rows)]).wait()
            xcopy(k, src.at[pl.ds(0, C)], dst.at[pl.ds(0, C)]).wait_recv()

        @pl.when(p.y == 0)
        def _():
            local(k, src.at[pl.ds(C, rows - C)], dst.at[pl.ds(2 * C, rows - C)]).wait()
            xcopy(k, src.at[pl.ds(0, C)], dst.at[pl.ds(0, C)]).wait_send()

    def store_rows(k, src, dst):
        @pl.when(vis)
        def _():
            xcopy(k, src.at[pl.ds(0, C)], dst.at[pl.ds(0, C)]).start()
            local(k, src.at[pl.ds(C, rows)], dst).start()

        @pl.when(p.y == 0)
        def _():
            local(k, src.at[pl.ds(2 * C, rows - C)], dst.at[pl.ds(C, rows - C)]).start()

    def stored_rows(k, src, dst):
        @pl.when(vis)
        def _():
            xcopy(k, src.at[pl.ds(0, C)], dst.at[pl.ds(0, C)]).wait_send()
            local(k, src.at[pl.ds(C, rows)], dst).wait()

        @pl.when(p.y == 0)
        def _():
            local(k, src.at[pl.ds(2 * C, rows - C)], dst.at[pl.ds(C, rows - C)]).wait()

    def came_back(k, src, dst):
        @pl.when(p.y == 0)
        def _():
            xcopy(k, src.at[pl.ds(0, C)], dst.at[pl.ds(0, C)]).wait_recv()

    def place_gains():
        lane = lax.broadcasted_iota(jnp.int32, (1, 128), 1)
        mine = lane // n_own == lax.rem(p.x * 2 + p.c, 4)
        pair = []
        for g in (g1, g2):
            v = g[...].astype(BF16).astype(F32)
            pair.append(jnp.where(mine, jnp.concatenate([v] * 4, axis=1), 0.0))
        G[0, p.y, p.z, p.x, p.c] = jnp.concatenate(pair + [jnp.zeros((6, 128), F32)], axis=0)

    def place_own(u):
        lane = lax.broadcasted_iota(jnp.int32, (n_own, 128), 1)
        for k in range(8):
            at = slice(k * 128, (k + 1) * 128)
            if u < 2:
                v = h1[u * n_own : (u + 1) * n_own, at]
                v = move_lanes([(v, a, b, n) for a, b, n in head_moves()], lane)
            elif u == 2:
                v = h1[2 * n_own : 3 * n_own, at]
            elif u == 3:
                v = h1[3 * n_own : 4 * n_own, at]
            elif u < 8:
                j = u - 4
                top = (4 + k // 2) * n_own
                left = k % 2 * 512
                v = move_lanes(
                    [
                        (h1[top : top + n_own, left + a * 128 : left + (a + 1) * 128], 32 * j, 32 * a, 32)
                        for a in range(4)
                    ],
                    lane,
                )
            else:
                v = h1[u * n_own : (u + 1) * n_own, at]
            W[u, p.y, p.z, p.x, p.c, :, at] = v.astype(BF16)

    def place_codes():
        pair = []
        for ref in (clips, frames):
            v = ref[...].astype(F32)
            pair.append(jnp.concatenate([v[k : k + 1] for k in range(rows // 128)], axis=1))
        both = jnp.concatenate(pair + [jnp.zeros((6, rows), F32)], axis=0)
        src = lax.broadcasted_iota(jnp.int32, (rows, 128), 0)
        lane = lax.broadcasted_iota(jnp.int32, (rows, 128), 1)
        pick = jnp.where((src == lane // FA * FV) & (lane < C), 1.0, 0.0).astype(BF16)
        cond = dot(both.astype(BF16), pick)
        full = jnp.concatenate([cond[:, :C], both], axis=1)
        clip, when = full[0:1], full[1:2]
        base = clip * 64.0
        code = base + when
        lo = jnp.where(clip >= 0, base, 1.0)
        hi = jnp.where(clip >= 0, code, 0.0)
        twice = lambda v: jnp.concatenate([v[:, :C], v[:, :C], v[:, 2 * C :]], axis=1)
        for k, v in enumerate((code, lo, hi, when, twice(lo), twice(hi))):
            codes[k : k + 1, 0:R] = v

    def gains():
        for y in range(2):
            for z in range(4):
                t = G[0, y, z, 0, 0] + G[0, y, z, 0, 1] + G[0, y, z, 1, 0] + G[0, y, z, 1, 1]
                gain[:, (y * 4 + z) * 128 : (y * 4 + z + 1) * 128] = t
        gain[4:6, :] = jnp.zeros((2, WIDE), F32)

    def column(row, at):
        return jnp.transpose(jnp.broadcast_to(codes[row : row + 1, at : at + 128], (128, 128)))

    def tables():
        side = (HD - RT) // 2
        for at in range(0, R, 128):
            n = min(128, R - at)
            shape = (n, 128)
            lane, i = rope_lane(shape)
            t = column(3, at)[:n]
            place = lax.broadcasted_iota(jnp.int32, shape, 0) + (at - C)
            inner = place % FV
            own_row = (place >= 0) & vis
            down = jnp.where(own_row, inner // GW, 0).astype(F32)
            across = jnp.where(own_row, inner % GW, 0).astype(F32)
            first, second = RT // 2, RT // 2 + side // 2
            k = jnp.where(i < first, i, jnp.where(i < second, i - first, i - second)).astype(F32)
            n_at = jnp.where(i < first, t, jnp.where(i < second, down, across))
            width = jnp.where(i < first, float(RT), float(side))
            angle = n_at * jnp.exp(k / width * (-2.0 * LOG_THETA))
            ct[at : at + n, :] = jnp.cos(angle)
            sine = jnp.sin(angle)
            st[at : at + n, :] = jnp.where(lane < 64, -sine, sine)

    def biases():
        for at in range(0, R, 128):
            n = min(128, R - at)
            kc = column(0, at)[:n]
            key = lax.broadcasted_iota(jnp.int32, (n, 128), 0) + at
            lane = lax.broadcasted_iota(jnp.int32, (n, 128), 1)
            for qa in range(0, rows, 128):
                lo = codes[1:2, C + qa : C + qa + 128]
                hi = codes[2:3, C + qa : C + qa + 128]
                ok = ((kc >= lo) & (kc <= hi)) | (key == lane + (qa + C))
                bias[at : at + n, qa : qa + 128] = jnp.where(ok, 0.0, NEG)
            lo, hi = codes[4:5, 0:128], codes[5:6, 0:128]
            ok = ((kc >= lo) & (kc <= hi)) | (key == lane % 64)
            cbias[at : at + n, :] = jnp.where(ok, 0.0, NEG)

    def norm_one():
        @pl.loop(0, R // 64)
        def _(k):
            r = pl.ds(pl.multiple_of(k * 64, 64), 64)
            unit, _ = unit_rows(x[r, :].astype(F32))
            dur(0)[r, :] = (unit * gain[0:1, :]).astype(BF16)

    def turned(v, rowset, sign):
        return v * ct[rowset, :] + pltpu.roll(v, 64, 1) * (st[rowset, :] * sign)

    def project(u):
        dst = (Q, K, V)[u]

        @pl.loop(0, WIDE // 256)
        def _(k):
            at = pl.multiple_of(k * 256, 256)
            v = dot(dur(0)[...], W3[u, :, pl.ds(at, 256)])
            for h in range(2):
                part_v = v[:, h * 128 : (h + 1) * 128]
                if u < 2:
                    part_v = turned(part_v, slice(0, R), 1.0)
                dst[:, pl.ds(pl.multiple_of(at + h * 128, 128), 128)] = part_v.astype(BF16)

    blocks = [(0, C, R)] + [(C + 128 * b, 128, C + 128 * (b + 1)) for b in range(rows // 128)]

    def masks():
        lane, _ = rope_lane((1, 128))
        even = (lane % 64) < 32
        first = lane < 64
        return even, first

    def stack(v, m, scale):
        zero = jnp.zeros_like(v)
        both = jnp.concatenate([jnp.where(m, v, zero), jnp.where(m, zero, v)], axis=0)
        return both * jnp.asarray(scale, BF16) if scale != 1.0 else both

    def scores(b, q0, nq, n, k, rq):
        s = lax.dot_general(k[:n], rq, (((1,), (1,)), ((), ())), preferred_element_type=F32)
        if b == 0:
            return s + cbias[0:n, :]
        t = bias[0:n, q0 - C : q0 - C + nq]
        return s + jnp.concatenate([t, t], axis=1)

    def attend(lo, hi):
        @pl.when(vis)
        def _():
            even, first = masks()

            @pl.loop(lo, hi)
            def _(pair):
                cols = pl.ds(pl.multiple_of(pair * 128, 128), 128)
                k, v = K[:, cols], V[:, cols]
                for b, (q0, nq, n) in enumerate(blocks):
                    rq = stack(Q[q0 : q0 + nq, cols], even, HD ** -0.5)
                    s = scores(b, q0, nq, n, k, rq)
                    top = jnp.max(s, axis=0, keepdims=True)
                    e = jnp.exp(s - top)
                    total = jnp.sum(e, axis=0, keepdims=True)
                    prob = (e * (1.0 / total)).astype(BF16)
                    lse[pair, b : b + 1, 0 : 2 * nq] = top + jnp.log(total)
                    o = lax.dot_general(
                        v[:n], prob, (((0,), (0,)), ((), ())), preferred_element_type=F32
                    )
                    o = jnp.transpose(o)
                    ob[q0 : q0 + nq, cols] = jnp.where(first, o[:nq], o[nq:]).astype(BF16)

    def attend_back(lo, hi):
        @pl.when(vis)
        def _():
            even, first = masks()

            @pl.loop(lo, hi)
            def _(pair):
                cols = pl.ds(pl.multiple_of(pair * 128, 128), 128)
                k, v = K[:, cols], V[:, cols]
                for b, (q0, nq, n) in enumerate(blocks):
                    rq = stack(Q[q0 : q0 + nq, cols], even, HD ** -0.5)
                    rd = stack(dob[q0 : q0 + nq, cols], first, 1.0)
                    s = scores(b, q0, nq, n, k, rq)
                    prob = jnp.exp(s - lse[pair, b : b + 1, 0 : 2 * nq])
                    dp = lax.dot_general(
                        v[:n], rd, (((1,), (1,)), ((), ())), preferred_element_type=F32
                    )
                    centre = jnp.sum(prob * dp, axis=0, keepdims=True)
                    ds = (prob * (dp - centre)).astype(BF16)
                    dvn = dot(prob.astype(BF16), rd)
                    dkn = dot(ds, rq)
                    if b == 0:
                        dv[...] = dvn
                        dk[...] = dkn
                    else:
                        dv[0:n, :] += dvn
                        dk[0:n, :] += dkn
                    t = lax.dot_general(
                        k[:n], ds, (((0,), (0,)), ((), ())), preferred_element_type=F32
                    )
                    t = jnp.transpose(t)
                    dq = jnp.where(even, t[:nq], t[nq:]) * HD ** -0.5
                    Q[q0 : q0 + nq, cols] = turned(dq, slice(q0, q0 + nq), -1.0).astype(BF16)
                K[:, cols] = turned(dk[...], slice(0, R), -1.0).astype(BF16)
                V[:, cols] = dv[...].astype(BF16)

    def pad_forward():
        @pl.when(p.y == 0)
        def _():
            ob[...] = V[...]

    def pad_back():
        @pl.when(p.y == 0)
        def _():
            Q[...] = jnp.zeros((R, WIDE), BF16)
            K[...] = jnp.zeros((R, WIDE), BF16)
            V[...] = dob[...]

    def hidden():
        @pl.loop(0, R // TILE)
        def _(k):
            r = pl.ds(pl.multiple_of(k * TILE, 32), TILE)
            h1[r, :] = x[r, :].astype(F32) + dot(ob[r, :], W3[3])

        @pl.loop(0, R // 64)
        def _(k):
            r = pl.ds(pl.multiple_of(k * 64, 64), 64)
            unit, _ = unit_rows(h1[r, :])
            a2[r, :] = (unit * gain[1:2, :]).astype(BF16)

    def inner(j):
        @pl.loop(0, WIDE // 256)
        def _(k):
            at = pl.ds(pl.multiple_of(k * 256, 256), 256)
            u = dot(a2[...], W3[4 + j, :, at])
            phi = 0.5 + 0.5 * lax.erf(u * 0.7071067811865476)
            gbr(j)[:, at] = (u * phi).astype(BF16)
            dur(j)[:, at] = (phi + u * (jnp.exp(u * u * -0.5) * 0.3989422804014327)).astype(BF16)

    def weight_grad(i, left, right):
        dst = part3(i)

        @pl.loop(0, WIDE // 256)
        def _(k):
            at = pl.ds(pl.multiple_of(k * 256, 256), 256)
            t = lax.dot_general(
                left(at), right(), (((0,), (0,)), ((), ())), preferred_element_type=F32
            )
            dst[at, :] = t.astype(BF16)

    def grad2(j):
        weight_grad(j, lambda at: gbr(j)[:, at], lambda: cot[...])

    def grad1(j):
        weight_grad(4 + j, lambda at: a2[:, at], lambda: dur(j)[...])

    def du(j):
        @pl.loop(0, WIDE // 256)
        def _(k):
            at = pl.ds(pl.multiple_of(k * 256, 256), 256)
            d = lax.dot_general(
                cot[...], W3[8 + j, at, :], (((1,), (1,)), ((), ())), preferred_element_type=F32
            )
            dur(j)[:, at] = (d * dur(j)[:, at].astype(F32)).astype(BF16)

    def result(lo, hi):
        @pl.loop(lo, hi)
        def _(k):
            at = pl.ds(pl.multiple_of(k * 256, 256), 256)
            t = h1[:, at]
            for j in range(4):
                t = t + dot(gbr(j)[...], W3[8 + j, :, at])
            obuf[:, at] = t.astype(BF16)

    def hidden_back(lo, hi):
        @pl.loop(lo, hi)
        def _(k):
            r = pl.ds(pl.multiple_of(k * TILE, 32), TILE)
            t = lax.dot_general(
                dur(0)[r, :], W3[4], (((1,), (1,)), ((), ())), preferred_element_type=F32
            )
            for j in range(1, 4):
                t = t + lax.dot_general(
                    dur(j)[r, :], W3[4 + j], (((1,), (1,)), ((), ())), preferred_element_type=F32
                )
            unit, inverse = unit_rows(h1[r, :])
            gain[5:6, :] += jnp.sum(t * unit, axis=0, keepdims=True)
            t = cot[r, :].astype(F32) + back_rows(t, gain[1:2, :], unit, inverse)
            h1[r, :] = t
            obuf[r, :] = t.astype(BF16)

    def mixed_back():
        @pl.loop(0, WIDE // 256)
        def _(k):
            at = pl.ds(pl.multiple_of(k * 256, 256), 256)
            t = lax.dot_general(
                obuf[...], W3[7, at, :], (((1,), (1,)), ((), ())), preferred_element_type=F32
            )
            dob[:, at] = t.astype(BF16)

    def input_back(lo, hi):
        @pl.loop(lo, hi)
        def _(k):
            r = pl.ds(pl.multiple_of(k * TILE, 32), TILE)
            t = None
            for u, src in enumerate((Q, K, V)):
                d = lax.dot_general(
                    src[r, :], W3[4 + u], (((1,), (1,)), ((), ())), preferred_element_type=F32
                )
                t = d if t is None else t + d
            unit, inverse = unit_rows(x[r, :].astype(F32))
            gain[4:5, :] += jnp.sum(t * unit, axis=0, keepdims=True)
            t = h1[r, :] + back_rows(t, gain[0:1, :], unit, inverse)
            obuf[r, :] = t.astype(BF16)

    def local(k, src, dst):
        return pltpu.make_async_copy(src, dst, loc.at[k])

    def own_copies():
        pieces = [wq.at[:, pl.ds(k * WIDE, WIDE)] for k in range(3)] + [wp]
        pieces += [w1.at[:, pl.ds(k * WIDE, WIDE)] for k in range(4)]
        pieces += [w2.at[pl.ds(k * n_own, n_own)] for k in range(4)]
        return [
            local(8 + k, piece, h1.at[pl.ds(k * n_own, n_own)]) for k, piece in enumerate(pieces)
        ]

    def spill_copy(u):
        return local(4 + u, W.at[u], spill.at[u])

    def reload_copy(u):
        return local(4 + u, spill.at[u], W.at[4 + u])

    def grant(i):
        for q in p.peers():
            pl.semaphore_signal(credit.at[i], inc=1, device_id=q, device_id_type=MESH)

    shards = own_copies()
    for c in shards:
        c.start()
    place_gains()
    for c in shards[:2]:
        c.wait()
    place_own(0)
    place_own(1)
    pl.semaphore_wait(bar, 6)
    mini.first(0)
    mini.second(0)
    early = [u for u in range(NU) if u not in LINE_UNITS]
    ga.first(0)
    ga.second(0)
    ga.first(1)
    ga.second(1)
    load_rows(0, x_hbm, x)
    load_rows(1, cot_hbm, cot)
    for c in shards[2:]:
        c.wait()
    for u in range(2, NU):
        place_own(u)
        if u in LINE_UNITS[:1] and LINE_START[0] == 0:
            ga.line0(u)
        if u in early[2:FIRST_AHEAD]:
            ga.first(u)
        if u in early[2:SECOND_AHEAD]:
            ga.second(u)
    mini.g1(0)
    place_codes()
    mini.g2(0)
    tables()
    mini.g3(0)

    @pl.when(vis)
    def _():
        biases()

    mini.g4(0)
    gains()
    wait_rows(0, x_hbm, x)
    wait_rows(1, cot_hbm, cot)
    norm_one()

    def scatter_open(i):
        pl.semaphore_wait(credit.at[i], 6)
        sc.r0(i)

    def scatter_close(i):
        (sc.h4 if i in HALF_UNITS else sc.r4)(i)
        sc.flush(i)
        if i < 4:
            grant(i + 8)

    def row_gains():
        for y in range(2):
            for z in range(4):
                at = (y * 4 + z) * 128
                for b in range(2):
                    for c in range(2):
                        ggp[0, y, z, b, c] = gain[:, at : at + 128]

    def gather_close():
        ga.flush()
        for u in LINE_UNITS:
            ga.line_flush(u)

    def grants(lo, hi):
        for i in range(lo, hi):
            grant(i)

    def all_of(f, *args):
        for a in args:
            f(a)

    def spills(start):
        for u in range(4):
            if start:
                spill_copy(u).start()
            else:
                spill_copy(u).wait()

    def reloads(start):
        for u in range(4):
            if start:
                reload_copy(u).start()
            else:
                reload_copy(u).wait()

    def run_part(i):
        if i < 4:
            grad2(i)
        elif i < 8:
            grad1(i - 4)
        elif i == 8:
            weight_grad(8, lambda at: ob[:, at], lambda: obuf[...])
        else:
            src = (Q, K, V)[i - 9]
            weight_grad(i, lambda at: dur(0)[:, at], lambda: src[...])

    def run_hback(k):
        if k == 0:
            stored_rows(2, obuf, out_hbm)
        hidden_back(k, k + 1)

    def early_close():
        for u in range(4):
            ga.flush(u)

    actions = {
        FIRST: ga.first,
        SECOND: ga.second,
        G1: ga.g1,
        G2: ga.g2,
        G3: ga.g3,
        G4: ga.g4,
        LINE0: ga.line0,
        LINE1: ga.line1,
        LINE2: ga.line2,
        LINE31: lambda u: ga.line3(u, 1),
        LINE32: lambda u: ga.line3(u, 2),
        LINE33: lambda u: ga.line3(u, 3),
        LINE4: ga.line4,
        CLOSE0: early_close,
        CLOSE: gather_close,
        OPEN: scatter_open,
        R1: lambda i: (sc.h1 if i in HALF_UNITS else sc.r1)(i),
        R2: lambda i: (sc.h2 if i in HALF_UNITS else sc.r2)(i),
        R3: lambda i: (sc.h3 if i in HALF_UNITS else sc.r3)(i),
        R4: scatter_close,
        MINI: lambda k: (msc.r0, msc.r1, msc.r2, msc.r3, msc.r4)[k](0),
        PROJ: project,
        ATTEND: lambda k: attend(k * PAIRS, (k + 1) * PAIRS),
        HIDDEN: lambda: (pad_forward(), hidden(), spills(True)),
        INNER: inner,
        PART: run_part,
        GRANT0: lambda: (spills(False), grants(0, 4)),
        DU: du,
        RESULT: lambda k: result(2 * k, 2 * k + 2),
        GRANT4: lambda: (store_rows(2, obuf, out_hbm), grants(4, 8)),
        HBACK: run_hback,
        RELOAD: lambda: reloads(True),
        MIXED: lambda: (reloads(False), mixed_back(), pad_back()),
        ABACK: lambda k: attend_back(k * PAIRS, (k + 1) * PAIRS),
        AGAIN: norm_one,
        IBACK: lambda k: input_back(k, k + 1),
        ROWS: lambda: (store_rows(3, obuf, xg_hbm), row_gains()),
    }
    for name in full_order():
        actions[name[0]](*name[1:])
    sc.flush()
    msc.flush()
    mini.flush()
    stored_rows(3, obuf, xg_hbm)
    came_back(2, obuf, out_hbm)
    came_back(3, obuf, xg_hbm)


(
    FIRST, SECOND, G1, G2, G3, G4, LINE0, LINE1, LINE2, LINE31, LINE32, LINE33, LINE4, CLOSE0, CLOSE,
    OPEN, R1, R2, R3, R4, MINI, PROJ, ATTEND, HIDDEN, INNER, PART, GRANT0, DU, RESULT, GRANT4, HBACK,
    RELOAD, MIXED, ABACK, AGAIN, IBACK, ROWS,
) = range(37)
PAIRS = 2


LINE_UNITS = (10, 11)
LINE_START = (0, 3)
HALF_UNITS = ()
FIRST_AHEAD = 2
SECOND_AHEAD = 2


PLAN = (
    2, 18, 32, 3, 19, 33, 48, 122, 4, 20, 34, 49, 64, 107, 138, 5, 21, 35, 50, 80,
    336, 65, 6, 22, 36, 51, 81, 337, 66, 154, 123, 7, 23, 37, 52, 82, 338, 67, 352, 139,
    8, 24, 38, 353, 53, 83, 208, 68, 354, 170, 9, 25, 39, 355, 54, 84, 69, 368, 155, 384,
    40, 55, 400, 85, 385, 70, 186, 401, 41, 416, 56, 86, 386, 71, 402, 202, 171, 434, 57, 87,
    387, 72, 403, 240, 241, 256, 88, 432, 73, 187, 242, 257, 272, 89, 433, 203, 435, 224, 243, 258,
    448, 273, 449, 464, 404, 244, 259, 274, 480, 288, 405, 245, 260, 481, 275, 289, 496, 512, 304, 406,
    246, 261, 276, 528, 290, 305, 407, 247, 262, 529, 277, 291, 306, 408, 248, 263, 530, 278, 292, 307,
    531, 544, 409, 249, 264, 279, 293, 410, 308, 411, 250, 265, 560, 280, 294, 561, 309, 576, 251, 266,
    281, 295, 310, 267, 282, 296, 311, 320, 283, 297, 312, 321, 298, 313, 322, 299, 314, 323, 315, 324,
)
BARE = (CLOSE0, CLOSE, HIDDEN, GRANT0, GRANT4, RELOAD, MIXED, AGAIN, ROWS)


def full_order():
    return [(v // 16,) if v // 16 in BARE else (v // 16, v % 16) for v in PLAN]


def hand_over_kernel(*refs):
    n = 6
    arrays, gg, outs, g1, g2 = refs[:n], refs[n], refs[n + 1 : 2 * n + 1], refs[2 * n + 1], refs[2 * n + 2]
    held, sems = refs[2 * n + 3 : 3 * n + 3], refs[3 * n + 3]
    into = [pltpu.make_async_copy(a, h, sems.at[k]) for k, (a, h) in enumerate(zip(arrays, held))]
    back = [pltpu.make_async_copy(h, o, sems.at[n + k]) for k, (h, o) in enumerate(zip(held, outs))]
    for c in into:
        c.start()
    lane = lax.rem(lax.axis_index("clip"), 4)
    for row, g in ((4, g1), (5, g2)):
        v = gg[row : row + 1, :]
        t = v[:, 0:32]
        for k in range(1, 4):
            t = jnp.where(lane == k, v[:, 32 * k : 32 * k + 32], t)
        g[...] = t
    for a, b in zip(into, back):
        a.wait()
        b.start()
    for b in back:
        b.wait()


def hand_over(arrays, gg, n):
    hbm = pl.BlockSpec(memory_space=pl.ANY)
    vmem = pl.BlockSpec(memory_space=pltpu.VMEM)
    shapes = [jax.ShapeDtypeStruct(a.shape, a.dtype) for a in arrays]
    return pl.pallas_call(
        hand_over_kernel,
        out_shape=shapes + [jax.ShapeDtypeStruct((1, n), F32)] * 2,
        in_specs=[hbm] * len(arrays) + [vmem],
        out_specs=[hbm] * len(arrays) + [vmem] * 2,
        scratch_shapes=[pltpu.VMEM(a.shape, a.dtype) for a in arrays]
        + [pltpu.SemaphoreType.DMA((2 * len(arrays),))],
    )(*arrays, gg)


def fast_body(
    tokens, w_qkv, w_proj, w_fc1, w_fc2, norm1_gain, norm2_gain, clip_index, frame_index, cotangent
):
    rows, width = tokens.shape
    n = w_qkv.shape[0]
    R = rows + rows // FV * FA
    unit = (2, 4, 2, 2, n, width)
    hbm = pl.BlockSpec(memory_space=pl.ANY)
    vmem = pl.BlockSpec(memory_space=pltpu.VMEM)
    rows_low = pltpu.VMEM((R, width), BF16)
    lanes = pltpu.VMEM((R, 128), F32)
    out, xg, gq, gpr, gf1, gf2, gg, _ = pl.pallas_call(
        layer_kernel,
        out_shape=[
            jax.ShapeDtypeStruct((rows, width), BF16),
            jax.ShapeDtypeStruct((rows, width), BF16),
            jax.ShapeDtypeStruct(w_qkv.shape, F32),
            jax.ShapeDtypeStruct(w_proj.shape, F32),
            jax.ShapeDtypeStruct(w_fc1.shape, F32),
            jax.ShapeDtypeStruct(w_fc2.shape, F32),
            jax.ShapeDtypeStruct((8, 128), F32),
            jax.ShapeDtypeStruct((4,) + unit, BF16),
        ],
        in_specs=[hbm] * 6 + [vmem] * 4,
        out_specs=[hbm, hbm] + [vmem] * 5 + [hbm],
        scratch_shapes=[
            pltpu.VMEM((NU,) + unit, BF16),
            pltpu.VMEM((1, 2, 4, 2, 2, 8, 128), F32),
            pltpu.VMEM((8, -(-R // 128) * 128), F32),
            rows_low,
            rows_low,
            rows_low,
            rows_low,
            rows_low,
            rows_low,
            rows_low,
            pltpu.VMEM((R, width), F32),
            rows_low,
            pltpu.VMEM((2,) + unit, BF16),
            pltpu.VMEM((3,) + unit, BF16),
            pltpu.VMEM((4,) + unit, BF16),
            rows_low,
            pltpu.VMEM((R, rows), F32),
            lanes,
            lanes,
            lanes,
            pltpu.VMEM((8, 8, 256), F32),
            lanes,
            lanes,
            pltpu.VMEM((8, width), F32),
            pltpu.VMEM((1, 2, 4, 2, 2, 8, 128), F32),
            pltpu.VMEM((32, 8, 128), F32),
            pltpu.SemaphoreType.DMA((NU, 17)),
            pltpu.SemaphoreType.DMA((NU, 17)),
            pltpu.SemaphoreType.DMA((1, 17)),
            pltpu.SemaphoreType.DMA((1, 17)),
            pltpu.SemaphoreType.DMA((NU, 16)),
            pltpu.SemaphoreType.DMA((NU, 16)),
            pltpu.SemaphoreType.DMA((1, 12)),
            pltpu.SemaphoreType.DMA((1, 12)),
            pltpu.SemaphoreType.DMA((4,)),
            pltpu.SemaphoreType.DMA((4,)),
            pltpu.SemaphoreType.DMA((20,)),
            pltpu.SemaphoreType.REGULAR((NU,)),
        ],
        compiler_params=pltpu.CompilerParams(
            collective_id=0, has_side_effects=True, vmem_limit_bytes=VMEM_LIMIT
        ),
    )(
        tokens,
        cotangent,
        w_qkv,
        w_proj,
        w_fc1,
        w_fc2,
        norm1_gain.reshape(1, n),
        norm2_gain.reshape(1, n),
        clip_index.reshape(rows // 128, 128),
        frame_index.reshape(rows // 128, 128),
    )
    *arrays, gain1, gain2 = hand_over((out, xg, gq, gpr, gf1, gf2), gg, n)
    return *arrays, gain1.reshape(n), gain2.reshape(n)


def solution(mesh):
    placed = (
        P(("stream", "clip"), None),
        P(("stream", "clip"), None),
        P(("stream", "clip"), None),
        P(("stream", "clip"), None),
        P(("stream", "clip"), None),
        P(("stream", "clip")),
        P(("stream", "clip")),
        P(("stream", "clip")),
        P(("stream", "clip")),
        P(("stream", "clip"), None),
    )
    block = mesh.shape["stream"] == 2 and mesh.shape["clip"] == 16
    return jax.shard_map(
        fast_body if block else body,
        mesh=mesh,
        in_specs=placed,
        out_specs=(
            P(("stream", "clip"), None),
            P(("stream", "clip"), None),
            P(("stream", "clip"), None),
            P(("stream", "clip"), None),
            P(("stream", "clip"), None),
            P(("stream", "clip"), None),
            P(("stream", "clip")),
            P(("stream", "clip")),
        ),
        check_vma=False,
    )
```

```python
import jax
import jax.numpy as jnp
from jax import lax
from jax.experimental import pallas as pl
from jax.experimental.pallas import tpu as pltpu
from jax.sharding import PartitionSpec as P

HD = 64
RT = 16
GW = 4
FA = 2
FV = 16


EPSILON = 1e-06
THETA = 10000.0
MASKED = -1e30
LOG_THETA = 9.210340371976184
VMEM_LIMIT = 63 * 1024 * 1024


def shifted(value, axis, steps):
    count = lax.axis_size(axis)
    initial, last = (max(0, -steps), min(count, count - steps))
    return lax.ppermute(value, axis, [(source, source + steps) for source in range(initial, last)])


def frequencies(width):
    counter = jnp.arange(width // 2).astype(jnp.float32)
    return jnp.power(THETA, -2.0 * counter / width)


def angle_sets(frames, visual_flag, rows):
    place = jnp.arange(rows)
    inner = place % FV
    down_pos = inner // GW * visual_flag
    across_pos = inner % GW * visual_flag
    side = (HD - RT) // 2
    time_angles = frames.astype(jnp.float32)[:, None] * frequencies(RT)[None, :]
    down_angles = down_pos.astype(jnp.float32)[:, None] * frequencies(side)[None, :]
    across_angles = across_pos.astype(jnp.float32)[:, None] * frequencies(side)[None, :]
    return (time_angles, down_angles, across_angles)


def rotate(block, angles):
    half = block.shape[-1] // 2
    cosine = jnp.cos(angles)[:, None, :]
    sine = jnp.sin(angles)[:, None, :]
    first = block[..., :half]
    second = block[..., half:]
    return jnp.concatenate(
        [first * cosine - second * sine, first * sine + second * cosine], axis=-1
    )


def rotary(flat, sets, sign):
    rows = flat.shape[0]
    block = flat.reshape(rows, flat.shape[1] // HD, HD)
    side = (HD - RT) // 2
    pieces = (block[..., :RT], block[..., RT : RT + side], block[..., RT + side :])
    turned = [rotate(piece, sign * angles) for piece, angles in zip(pieces, sets)]
    return jnp.concatenate(turned, axis=-1).reshape(rows, -1)


def normalize(values, gain):
    centred = values - jnp.mean(values, axis=-1, keepdims=True)
    inverse = lax.rsqrt(jnp.mean(centred * centred, axis=-1, keepdims=True) + EPSILON)
    unit = centred * inverse
    return (unit * gain, unit, inverse)


def norm_back(grad_out, gain, unit, inverse):
    scaled = grad_out * gain
    centred = (
        scaled
        - jnp.mean(scaled, axis=-1, keepdims=True)
        - unit * jnp.mean(scaled * unit, axis=-1, keepdims=True)
    )
    return (inverse * centred, jnp.sum(grad_out * unit, axis=0))


def local_mask(clips, frames):
    rows = clips.shape[0]
    same = (
        (clips[:, None] == clips[None, :])
        & (clips[:, None] >= 0)
        & (frames[None, :] <= frames[:, None])
    )
    return same | (jnp.arange(rows)[:, None] == jnp.arange(rows)[None, :])


def cross_mask(clips, frames, far_clips, far_frames):
    return (
        (clips[:, None] == far_clips[None, :])
        & (clips[:, None] >= 0)
        & (far_frames[None, :] <= frames[:, None])
    )


def times_transpose(left, right):
    return lax.dot_general(
        left, right, (((1,), (1,)), ((), ())), preferred_element_type=jnp.float32
    )


def transpose_times(left, right):
    return lax.dot_general(
        left, right, (((0,), (0,)), ((), ())), preferred_element_type=jnp.float32
    )


def head_scores(query_part, key_part, allowed):
    query_heads = query_part.reshape(query_part.shape[0], 2, HD)
    key_heads = key_part.reshape(key_part.shape[0], 2, HD)
    scores = jnp.einsum(
        "qhd,khd->hqk", query_heads, key_heads, preferred_element_type=jnp.float32
    ) * HD ** (-0.5)
    return (jnp.where(allowed[None], scores, MASKED), query_heads, key_heads)


def attend_forward(query_part, key_part, value_part, allowed):
    rows = query_part.shape[0]
    scores, query_heads, key_heads = head_scores(query_part, key_part, allowed)
    peak = jnp.max(scores, axis=-1, keepdims=True)
    weights = jnp.exp(scores - peak)
    total = jnp.sum(weights, axis=-1, keepdims=True)
    probs = (weights / total).astype(jnp.bfloat16)
    value_heads = value_part.reshape(value_part.shape[0], 2, HD)
    mixed = jnp.einsum("hqk,khd->qhd", probs, value_heads, preferred_element_type=jnp.float32)
    return (mixed.reshape(rows, 2 * HD), (peak + jnp.log(total))[..., 0])


def attend_back(query_part, key_part, value_part, grad_part, allowed, log_total):
    rows = query_part.shape[0]
    scores, query_heads, key_heads = head_scores(query_part, key_part, allowed)
    probs = jnp.exp(scores - log_total[..., None])
    value_heads = value_part.reshape(value_part.shape[0], 2, HD)
    grad_heads = grad_part.reshape(rows, 2, HD)
    grad_probs = jnp.einsum(
        "qhd,khd->hqk", grad_heads, value_heads, preferred_element_type=jnp.float32
    )
    centre = jnp.sum(probs * grad_probs, axis=-1, keepdims=True)
    grad_scores = (probs * (grad_probs - centre)).astype(jnp.bfloat16)
    factor = HD ** (-0.5)
    grad_query = (
        jnp.einsum("hqk,khd->qhd", grad_scores, key_heads, preferred_element_type=jnp.float32)
        * factor
    )
    grad_key = (
        jnp.einsum("hqk,qhd->khd", grad_scores, query_heads, preferred_element_type=jnp.float32)
        * factor
    )
    grad_value = jnp.einsum(
        "hqk,qhd->khd", probs.astype(jnp.bfloat16), grad_heads, preferred_element_type=jnp.float32
    )
    key_count = key_part.shape[0]
    return (
        grad_query.reshape(rows, 2 * HD),
        grad_key.reshape(key_count, 2 * HD),
        grad_value.reshape(key_count, 2 * HD),
    )


def column_block(array, group_index):
    return lax.dynamic_slice_in_dim(array, group_index * 2 * HD, 2 * HD, 1)


def join_groups(stacked):
    return jnp.transpose(stacked, (1, 0, 2)).reshape(stacked.shape[1], -1)


def body(
    tokens, w_qkv, w_proj, w_fc1, w_fc2, norm1_gain, norm2_gain, clip_index, frame_index, cotangent
):
    rows = tokens.shape[0]
    width = tokens.shape[1]
    groups = width // (2 * HD)
    visual = lax.axis_index("stream") == 1
    visual_flag = visual.astype(jnp.int32)
    shards = (
        w_qkv.astype(jnp.bfloat16),
        w_proj.astype(jnp.bfloat16),
        w_fc1.astype(jnp.bfloat16),
        w_fc2.astype(jnp.bfloat16),
        norm1_gain.astype(jnp.bfloat16),
        norm2_gain.astype(jnp.bfloat16),
    )
    full_qkv, full_proj, full_fc1, full_fc2, gain_one, gain_two = (
        lax.all_gather(shards[0], ("stream", "clip"), axis=0, tiled=True),
        lax.all_gather(shards[1], ("stream", "clip"), axis=0, tiled=True),
        lax.all_gather(shards[2], ("stream", "clip"), axis=0, tiled=True),
        lax.all_gather(shards[3], ("stream", "clip"), axis=0, tiled=True),
        lax.all_gather(shards[4], ("stream", "clip"), axis=0, tiled=True),
        lax.all_gather(shards[5], ("stream", "clip"), axis=0, tiled=True),
    )
    gain_first = gain_one.astype(jnp.float32)
    gain_second = gain_two.astype(jnp.float32)
    values_in = tokens.astype(jnp.float32)
    normed, unit_one, inverse_one = normalize(values_in, gain_first)
    normed_b = normed.astype(jnp.bfloat16)
    projected = jnp.dot(normed_b, full_qkv, preferred_element_type=jnp.float32)
    sets = angle_sets(frame_index, visual_flag, rows)
    queries = rotary(projected[:, :width], sets, 1.0).astype(jnp.bfloat16)
    key_rows = rotary(projected[:, width : 2 * width], sets, 1.0).astype(jnp.bfloat16)
    values = projected[:, 2 * width :].astype(jnp.bfloat16)
    frames_row = rows // FV
    cond_rows = frames_row * FA
    near_keys, near_values = shifted((key_rows[:cond_rows], values[:cond_rows]), "stream", 1)
    far_keys, far_values = shifted((key_rows, values), "stream", -1)
    clip_seen = clip_index.reshape(frames_row, FV)[:, 0]
    clip_cond = clip_index[:cond_rows].reshape(frames_row, FA)[:, 0]
    frame_seen = frame_index.reshape(frames_row, FV)[:, 0]
    frame_cond = frame_index[:cond_rows].reshape(frames_row, FA)[:, 0]
    frame_clip = jnp.where(visual, clip_seen, clip_cond)
    frame_num = jnp.where(visual, frame_seen, frame_cond)
    partner_cond = (
        cross_mask(clip_index, frame_index, jnp.repeat(frame_clip, FA), jnp.repeat(frame_num, FA))
        & visual
    )
    partner_seen = cross_mask(
        clip_index, frame_index, jnp.repeat(frame_clip, FV), jnp.repeat(frame_num, FV)
    ) & jnp.logical_not(visual)
    allowed = jnp.concatenate(
        [partner_cond, partner_seen, local_mask(clip_index, frame_index)], axis=1
    )
    key_all = jnp.concatenate([near_keys, far_keys, key_rows], axis=0)
    value_all = jnp.concatenate([near_values, far_values, values], axis=0)

    def forward_group(group_index):
        return attend_forward(
            column_block(queries, group_index),
            column_block(key_all, group_index),
            column_block(value_all, group_index),
            allowed,
        )

    mixed_groups, log_totals = lax.map(forward_group, jnp.arange(groups))
    mixed_b = join_groups(mixed_groups).astype(jnp.bfloat16)
    hidden_one = values_in + jnp.dot(mixed_b, full_proj, preferred_element_type=jnp.float32)
    normed_two, unit_two, inverse_two = normalize(hidden_one, gain_second)
    normed_two_b = normed_two.astype(jnp.bfloat16)
    inner = jnp.dot(normed_two_b, full_fc1, preferred_element_type=jnp.float32)
    active, gelu_pull = jax.vjp(lambda given: jax.nn.gelu(given, approximate=False), inner)
    active_b = active.astype(jnp.bfloat16)
    result = hidden_one + jnp.dot(active_b, full_fc2, preferred_element_type=jnp.float32)
    full_qkv, full_proj, full_fc1, full_fc2, gain_one, gain_two = (
        lax.all_gather(shards[0], ("stream", "clip"), axis=0, tiled=True),
        lax.all_gather(shards[1], ("stream", "clip"), axis=0, tiled=True),
        lax.all_gather(shards[2], ("stream", "clip"), axis=0, tiled=True),
        lax.all_gather(shards[3], ("stream", "clip"), axis=0, tiled=True),
        lax.all_gather(shards[4], ("stream", "clip"), axis=0, tiled=True),
        lax.all_gather(shards[5], ("stream", "clip"), axis=0, tiled=True),
    )
    gain_first = gain_one.astype(jnp.float32)
    gain_second = gain_two.astype(jnp.float32)
    grad_out = cotangent.astype(jnp.float32)
    grad_fc2 = transpose_times(active_b, cotangent)
    grad_active = times_transpose(cotangent, full_fc2)
    grad_inner = gelu_pull(grad_active)[0].astype(jnp.bfloat16)
    grad_fc1 = transpose_times(normed_two_b, grad_inner)
    grad_normed_two = times_transpose(grad_inner, full_fc1)
    back_two, grad_gain2 = norm_back(grad_normed_two, gain_second, unit_two, inverse_two)
    grad_hidden = grad_out + back_two
    grad_attn = grad_hidden.astype(jnp.bfloat16)
    grad_proj = transpose_times(mixed_b, grad_attn)
    grad_mixed = times_transpose(grad_attn, full_proj).astype(jnp.bfloat16)

    def backward_group(inputs):
        group_index, log_total = inputs
        return attend_back(
            column_block(queries, group_index),
            column_block(key_all, group_index),
            column_block(value_all, group_index),
            column_block(grad_mixed, group_index),
            allowed,
            log_total,
        )

    grad_q_groups, grad_k_groups, grad_v_groups = lax.map(
        backward_group, (jnp.arange(groups), log_totals)
    )
    grad_queries = join_groups(grad_q_groups)
    grad_key_all = join_groups(grad_k_groups)
    grad_value_all = join_groups(grad_v_groups)
    outer = cond_rows + rows
    cond_keys_back, cond_values_back = (
        shifted(grad_key_all[:cond_rows].astype(jnp.bfloat16), "stream", -1).astype(jnp.float32),
        shifted(grad_value_all[:cond_rows].astype(jnp.bfloat16), "stream", -1).astype(jnp.float32),
    )
    seen_keys_back, seen_values_back = (
        shifted(grad_key_all[cond_rows:outer].astype(jnp.bfloat16), "stream", 1).astype(
            jnp.float32
        ),
        shifted(grad_value_all[cond_rows:outer].astype(jnp.bfloat16), "stream", 1).astype(
            jnp.float32
        ),
    )
    filler = jnp.zeros((rows - cond_rows, width), jnp.float32)
    grad_keys = (
        grad_key_all[outer:] + seen_keys_back + jnp.concatenate([cond_keys_back, filler], axis=0)
    )
    grad_values = (
        grad_value_all[outer:]
        + seen_values_back
        + jnp.concatenate([cond_values_back, filler], axis=0)
    )
    grad_projected = jnp.concatenate(
        [rotary(grad_queries, sets, -1.0), rotary(grad_keys, sets, -1.0), grad_values], axis=1
    ).astype(jnp.bfloat16)
    grad_qkv = transpose_times(normed_b, grad_projected)
    grad_normed = times_transpose(grad_projected, full_qkv)
    back_one, grad_gain1 = norm_back(grad_normed, gain_first, unit_one, inverse_one)
    input_grad = (grad_hidden + back_one).astype(jnp.bfloat16)
    sums = (
        lax.psum_scatter(grad_qkv, ("stream", "clip"), scatter_dimension=0, tiled=True),
        lax.psum_scatter(grad_proj, ("stream", "clip"), scatter_dimension=0, tiled=True),
        lax.psum_scatter(grad_fc1, ("stream", "clip"), scatter_dimension=0, tiled=True),
        lax.psum_scatter(grad_fc2, ("stream", "clip"), scatter_dimension=0, tiled=True),
        lax.psum_scatter(grad_gain1, ("stream", "clip"), scatter_dimension=0, tiled=True),
        lax.psum_scatter(grad_gain2, ("stream", "clip"), scatter_dimension=0, tiled=True),
    )
    return (
        result.astype(jnp.bfloat16),
        input_grad,
        sums[0],
        sums[1],
        sums[2],
        sums[3],
        sums[4],
        sums[5],
    )


MESH = pl.DeviceIdType.MESH
F32 = jnp.float32
BF16 = jnp.bfloat16
MB = 1 << 20
NU = 12
ORDER = (8, 9, 10, 11, 4, 5, 6, 7, 3, 0, 1, 2)
WIDE = 1024
NEG = -1e30


class Place:
    def __init__(self):
        self.y = lax.axis_index("stream")
        clip = lax.axis_index("clip")
        self.z, self.x, self.c = clip // 4, (clip // 2) % 2, clip % 2
        self.X = self.dev(self.y, self.z, 1 - self.x, self.c)
        self.Y = self.dev(1 - self.y, self.z, self.x, self.c)
        self.C = self.dev(self.y, self.z, self.x, 1 - self.c)

    def dev(self, y, z, x, c):
        return (y, z * 4 + x * 2 + c)

    def up(self, d):
        return lax.rem(self.z + d, 4)

    def above(self, d):
        return self.dev(self.y, self.up(d), self.x, self.c)

    def peers(self):
        return [self.X, self.Y, self.C] + [self.above(d) for d in (1, 2, 3)]


class Link:
    def __init__(self, place, sent, got):
        self.p, self.sent, self.got, self.open = place, sent, got, []

    def copy(self, u, slot, src, dst, to):
        return pltpu.make_async_remote_copy(
            src_ref=src,
            dst_ref=dst,
            send_sem=self.sent.at[u, slot],
            recv_sem=self.got.at[u, slot],
            device_id=to,
            device_id_type=MESH,
        )

    def send(self, u, slot, src, dst, to):
        c = self.copy(u, slot, src, dst, to)
        c.start()
        self.open.append((u, c))

    def recv(self, u, slot, dst):
        self.copy(u, slot, dst, dst, self.p.X).wait_recv()

    def flush(self, unit=None):
        rest = []
        for u, c in self.open:
            if unit is None or u == unit:
                c.wait_send()
            else:
                rest.append((u, c))
        self.open = rest


class Gather(Link):
    def __init__(self, place, whole, sent, got):
        super().__init__(place, sent, got)
        self.W = whole

    def first(self, u):
        p = self.p
        me = self.W.at[u, p.y, p.z, p.x, p.c]
        for d in (1, 2, 3):
            self.send(u, d - 1, me, me, p.above(d))

    def second(self, u):
        p = self.p
        me = self.W.at[u, p.y, p.z, p.x, p.c]
        self.send(u, 3, me, me, p.X)
        self.send(u, 7, me, me, p.Y)

    def g1(self, u):
        p, W = self.p, self.W
        for d in (1, 2, 3):
            b = W.at[u, p.y, p.up(4 - d), p.x, p.c]
            self.recv(u, d - 1, b)
            self.send(u, 3 + d, b, b, p.X)
            self.send(u, 7 + d, b, b, p.Y)
        b = W.at[u, p.y, :, p.x, p.c]
        self.send(u, 13, b, b, p.C)

    def g2(self, u):
        p, W = self.p, self.W
        for k in range(4):
            z = p.up(4 - k)
            self.recv(u, 3 + k, W.at[u, p.y, z, 1 - p.x, p.c])
            self.recv(u, 7 + k, W.at[u, 1 - p.y, z, p.x, p.c])
        b = W.at[u, p.y, pl.ds(0, 2), 1 - p.x, p.c]
        self.send(u, 11, b, b, p.Y)
        b = W.at[u, 1 - p.y, pl.ds(2, 2), p.x, p.c]
        self.send(u, 12, b, b, p.X)
        b = W.at[u, p.y, :, 1 - p.x, p.c]
        self.send(u, 14, b, b, p.C)
        b = W.at[u, 1 - p.y, :, p.x, p.c]
        self.send(u, 15, b, b, p.C)

    def g3(self, u):
        p, W = self.p, self.W
        self.recv(u, 11, W.at[u, 1 - p.y, pl.ds(0, 2), 1 - p.x, p.c])
        self.recv(u, 12, W.at[u, 1 - p.y, pl.ds(2, 2), 1 - p.x, p.c])
        b = W.at[u, 1 - p.y, :, 1 - p.x, p.c]
        self.send(u, 16, b, b, p.C)

    def g4(self, u):
        p, W = self.p, self.W
        o = 1 - p.c
        self.recv(u, 13, W.at[u, p.y, :, p.x, o])
        self.recv(u, 14, W.at[u, p.y, :, 1 - p.x, o])
        self.recv(u, 15, W.at[u, 1 - p.y, :, p.x, o])
        self.recv(u, 16, W.at[u, 1 - p.y, :, 1 - p.x, o])


    def plane(self, u, z, c):
        return self.W.at[u, :, z, :, c]

    def line0(self, u):
        p = self.p
        me = self.W.at[u, p.y, p.z, p.x, p.c]
        self.send(u, 0, me, me, p.X)
        self.send(u, 1, me, me, p.Y)

    def line1(self, u):
        p, W = self.p, self.W
        h = W.shape[-2] // 2
        bx = W.at[u, p.y, p.z, 1 - p.x, p.c]
        by = W.at[u, 1 - p.y, p.z, p.x, p.c]
        self.recv(u, 0, bx)
        self.send(u, 2, bx.at[pl.ds(0, h)], bx.at[pl.ds(0, h)], p.Y)
        self.recv(u, 1, by)
        self.send(u, 3, by.at[pl.ds(h, h)], by.at[pl.ds(h, h)], p.X)

    def line2(self, u):
        p = self.p
        h = self.W.shape[-2] // 2
        bd = self.W.at[u, 1 - p.y, p.z, 1 - p.x, p.c]
        self.recv(u, 2, bd.at[pl.ds(0, h)])
        self.recv(u, 3, bd.at[pl.ds(h, h)])
        self.pass_on(u, 0)
        b = self.plane(u, p.z, p.c)
        self.send(u, 10, b, b, p.C)

    def ways(self, k):
        p = self.p
        return (
            (4 + k, 10 + k, p.z - k, p.z - k >= 0, p.z < 3, p.dev(p.y, p.z + 1, p.x, p.c)),
            (7 + k, 13 + k, p.z + k, p.z + k <= 3, p.z > 0, p.dev(p.y, p.z - 1, p.x, p.c)),
        )

    def pass_on(self, u, k):
        for slot, _, z, there, more, to in self.ways(k):
            @pl.when(there & more)
            def _():
                b = self.plane(u, z, self.p.c)
                self.copy(u, slot, b, b, to).start()

    def line3(self, u, k):
        for slot, core, z, there, _, _ in self.ways(k):
            @pl.when(there)
            def _():
                b = self.plane(u, z, self.p.c)
                self.recv(u, slot - 1, b)
                self.copy(u, core, b, b, self.p.C).start()
        if k < 3:
            self.pass_on(u, k)

    def line4(self, u):
        p = self.p
        self.recv(u, 10, self.plane(u, p.z, 1 - p.c))
        for k in (1, 2, 3):
            for _, core, z, there, _, _ in self.ways(k):
                @pl.when(there)
                def _():
                    self.recv(u, core, self.plane(u, z, 1 - p.c))

    def line_flush(self, u):
        for k in range(4):
            for slot, core, z, there, more, to in self.ways(k):
                b = self.plane(u, 0, 0)
                if k < 3:
                    @pl.when(there & more)
                    def _():
                        self.copy(u, slot, b, b, to).wait_send()
                if k > 0:
                    @pl.when(there)
                    def _():
                        self.copy(u, core, b, b, self.p.C).wait_send()


class Scatter(Link):
    def __init__(self, place, part, land, out, sent, got):
        super().__init__(place, sent, got)
        self.part, self.land, self.out = part, land, out

    def halves(self):
        p = self.p
        return (
            (pl.ds(0, 512), p.y, p.x, p.Y, p.X, lambda a, b: (a, b)),
            (pl.ds(512, 512), p.x, p.y, p.X, p.Y, lambda a, b: (b, a)),
        )

    def h1(self, i):
        p, q, c = self.p, self.part(i), self.p.c
        for k, (a, b) in enumerate(((1 - p.y, 1 - p.x), (1 - p.y, p.x), (p.y, 1 - p.x))):
            self.recv(i, k, self.col(i, a, b))
        for n, (half, mine, other, A, B, order) in enumerate(self.halves()):
            for bb in range(2):
                y, x = order(1 - mine, bb)
                own = lambda k: q.at[y, k, x, c, :, half]
                self.add(4, own, own, lambda k: self.blk(i, y, x, k).at[:, half])
                self.send(
                    i,
                    4 + 2 * n + bb,
                    q.at[y, :, x, c, :, half],
                    self.land(i, 16 + 4 * bb, 4).at[:, :, half],
                    A,
                )

    def h2(self, i):
        p, q, c = self.p, self.part(i), self.p.c
        self.recv(i, 3, self.col(i, p.y, p.x))
        for n, (half, mine, other, A, B, order) in enumerate(self.halves()):
            for bb in range(2):
                self.recv(i, 4 + 2 * n + bb, self.land(i, 16 + 4 * bb, 4).at[:, :, half])
                y, x = order(mine, bb)
                own = lambda k: q.at[y, k, x, c, :, half]
                self.add(
                    4,
                    own,
                    own,
                    lambda k: self.blk(i, y, x, k).at[:, half],
                    lambda k: self.land(i, 16 + 4 * bb + k, 1).at[0, :, half],
                )
            for d in (1, 2, 3):
                z = p.up(d)
                src = q.at[p.y, z, :, c, :, half] if n == 0 else q.at[:, z, p.x, c, :, half]
                self.send(
                    i, 7 + 3 * n + d, src, self.land(i, 22 + 2 * d, 2).at[:, :, half], p.above(d)
                )

    def h3(self, i):
        p, q, c = self.p, self.part(i), self.p.c
        for n, (half, mine, other, A, B, order) in enumerate(self.halves()):
            for d in (1, 2, 3):
                self.recv(i, 7 + 3 * n + d, self.land(i, 22 + 2 * d, 2).at[:, :, half])
            for bb in (1 - other, other):
                y, x = order(mine, bb)
                d = q.at[y, p.z, x, c, :, half]
                t = d[...].astype(F32)
                for k in (1, 2, 3):
                    t = t + self.land(i, 22 + 2 * k + bb, 1)[0, :, half].astype(F32)
                d[...] = t.astype(d.dtype)
            y, x = order(mine, 1 - other)
            self.send(
                i, 14 + n, q.at[y, p.z, x, c, :, half], self.land(i, 30, 1).at[0, :, half], B
            )

    def h4(self, i):
        p = self.p
        for n, (half, *_) in enumerate(self.halves()):
            self.recv(i, 14 + n, self.land(i, 30, 1).at[0, :, half])
        t = self.part(i)[p.y, p.z, p.x, p.c].astype(F32) + self.land(i, 30, 1)[0].astype(F32)
        self.out(i, t)

    def col(self, i, a, b):
        return self.land(i, (a * 2 + b) * 4, 4)

    def blk(self, i, a, b, z):
        return self.land(i, (a * 2 + b) * 4 + z, 1).at[0]

    def add(self, n, dst, *srcs):
        @pl.loop(0, n)
        def _(k):
            t = srcs[0](k)[...].astype(F32)
            for r in srcs[1:]:
                t = t + r(k)[...].astype(F32)
            d = dst(k)
            d[...] = t.astype(d.dtype)

    def r0(self, i):
        p = self.p
        y, x, o, q = p.y, p.x, 1 - p.c, self.part(i)
        for k, (a, b) in enumerate(((1 - y, 1 - x), (1 - y, x), (y, 1 - x), (y, x))):
            self.send(i, k, q.at[a, :, b, o], self.col(i, a, b), p.C)

    def r1(self, i):
        p = self.p
        y, x, c, q = p.y, p.x, p.c, self.part(i)
        self.recv(i, 0, self.col(i, 1 - y, 1 - x))
        own = lambda k: q.at[1 - y, k, 1 - x, c]
        self.add(4, own, own, lambda k: self.blk(i, 1 - y, 1 - x, k))
        self.send(i, 4, q.at[1 - y, pl.ds(0, 2), 1 - x, c], self.land(i, 16, 2), p.X)
        self.send(i, 5, q.at[1 - y, pl.ds(2, 2), 1 - x, c], self.land(i, 18, 2), p.Y)

    def r2(self, i):
        p = self.p
        y, x, c, q = p.y, p.x, p.c, self.part(i)
        self.recv(i, 1, self.col(i, 1 - y, x))
        self.recv(i, 2, self.col(i, y, 1 - x))
        ny = lambda k: q.at[1 - y, k, x, c]
        my = lambda k: self.blk(i, 1 - y, x, k)
        nx = lambda k: q.at[y, k, 1 - x, c]
        mx = lambda k: self.blk(i, y, 1 - x, k)
        self.add(2, lambda k: ny(k + 2), lambda k: ny(k + 2), lambda k: my(k + 2))
        self.add(2, nx, nx, mx)
        self.recv(i, 4, self.land(i, 16, 2))
        self.add(2, ny, ny, my, lambda k: self.land(i, 16 + k, 1).at[0])
        self.send(i, 6, q.at[1 - y, :, x, c], self.land(i, 28, 4), p.Y)
        self.recv(i, 5, self.land(i, 18, 2))
        self.add(
            2,
            lambda k: nx(k + 2),
            lambda k: nx(k + 2),
            lambda k: mx(k + 2),
            lambda k: self.land(i, 18 + k, 1).at[0],
        )
        self.send(i, 7, q.at[y, :, 1 - x, c], self.land(i, 24, 4), p.X)

    def r3(self, i):
        p = self.p
        y, x, c, q = p.y, p.x, p.c, self.part(i)
        self.recv(i, 3, self.col(i, y, x))
        self.recv(i, 6, self.land(i, 28, 4))
        self.recv(i, 7, self.land(i, 24, 4))
        own = lambda k: q.at[y, k, x, c]
        self.add(
            4,
            own,
            own,
            lambda k: self.blk(i, y, x, k),
            lambda k: self.land(i, 28 + k, 1).at[0],
            lambda k: self.land(i, 24 + k, 1).at[0],
        )
        for d in (1, 2, 3):
            self.send(i, 8 + d, q.at[y, p.up(d), x, c], self.land(i, 19 + d, 1).at[0], p.above(d))

    def r4(self, i):
        p = self.p
        q = self.part(i)
        for d in (1, 2, 3):
            self.recv(i, 8 + d, self.land(i, 19 + d, 1).at[0])
        t = q[p.y, p.z, p.x, p.c].astype(F32)
        for d in (1, 2, 3):
            t = t + self.land(i, 19 + d, 1)[0].astype(F32)
        self.out(i, t)


def unit_rows(v):
    centred = v - jnp.mean(v, axis=-1, keepdims=True)
    inverse = lax.rsqrt(jnp.mean(centred * centred, axis=-1, keepdims=True) + EPSILON)
    return centred * inverse, inverse


def back_rows(d, gain, unit, inverse):
    e = d * gain
    return inverse * (
        e - jnp.mean(e, axis=-1, keepdims=True) - unit * jnp.mean(e * unit, axis=-1, keepdims=True)
    )


def dot(a, b):
    return jnp.dot(a, b, preferred_element_type=F32)


def head_moves():
    side = (HD - RT) // 2
    moves = []
    for head in range(2):
        src, dst = head * HD, head * 32
        for at, part in ((0, RT), (RT, side), (RT + side, side)):
            moves.append((src + at, dst, part // 2))
            moves.append((src + at + part // 2, dst + 64, part // 2))
            dst += part // 2
    return moves


def move_lanes(pieces, lane):
    out = None
    for v, a, b, n in pieces:
        t = v if a == b else pltpu.roll(v, (b - a) % 128, 1)
        out = t if out is None else jnp.where((lane >= b) & (lane < b + n), t, out)
    return out


def rope_lane(shape):
    lane = lax.broadcasted_iota(jnp.int32, shape, 1)
    return lane, lane % 32


def layer_kernel(
    x_hbm, cot_hbm, wq, wp, w1, w2, g1, g2, clips, frames,
    out_hbm, xg_hbm, gq, gpr, gf1, gf2, gg, spill,
    W, G, codes, x, cot, Q, K, V, ob, dob, h1, a2, gbuf, gp, PS, obuf,
    bias, cbias, ct, st, lse, dk, dv, gain, ggp, gland,
    ss, rs, gss, grs, sss, srs, mss, mrs, xss, xrs, loc, credit,
):
    p = Place()
    vis = p.y == 1
    rows = x_hbm.shape[0]
    R = x.shape[0]
    C = R - rows
    TILE = R // 2
    n_own = wq.shape[0]
    W3 = W.reshape(NU, WIDE, WIDE)
    Wf = W.reshape(NU, 32, 32, WIDE)
    gflat = gbuf.reshape(2 * WIDE, WIDE)
    P3 = PS.reshape(4, WIDE, WIDE)
    H3 = gbuf.reshape(2, WIDE, WIDE)

    pflat = gp.reshape(3 * WIDE, WIDE)
    D3 = gp.reshape(3, WIDE, WIDE)

    def dur(j):
        return pflat.at[pl.ds(j * R, R)]

    def gbr(j):
        return gflat.at[pl.ds(j * R, R)] if j < 3 else dob

    def slot(i):
        return (0, i) if i < 4 else (1, i - 4) if i < 6 else (0, i - 6) if i < 10 else (2, i - 9)

    def part(i):
        k, n = slot(i)
        return (PS, gbuf, gp)[k].at[n]

    def part3(i):
        k, n = slot(i)
        return (P3, H3, D3)[k].at[n]

    def land(i, at, n):
        u = i if i < 4 else i + 4 if i < 8 else i - 8
        return Wf.at[u, pl.ds(at, n)]

    def finish(i, t):
        u = ORDER[i]
        lane = lax.broadcasted_iota(jnp.int32, (n_own, 128), 1)
        if u < 2:
            for k in range(8):
                v = t[:, k * 128 : (k + 1) * 128]
                at = u * WIDE + k * 128
                gq[:, at : at + 128] = move_lanes([(v, b, a, n) for a, b, n in head_moves()], lane)
        elif u == 2:
            gq[:, 2 * WIDE :] = t
        elif u == 3:
            gpr[...] = t
        elif u < 8:
            for h in range(2):
                bias[pl.ds((2 * u - 8 + h) * n_own, n_own), :] = t[:, h * 512 : (h + 1) * 512]
            if u == 7:
                for g in range(8):
                    at = slice(g % 4 * 128, (g % 4 + 1) * 128)
                    vs = [
                        bias[pl.ds((2 * j + g // 4) * n_own, n_own), at] for j in range(4)
                    ]
                    for a in range(4):
                        at = g * 512 + a * 128
                        gf1[:, at : at + 128] = move_lanes(
                            [(vs[j], 32 * a, 32 * j, 32) for j in range(4)], lane
                        )
        else:
            gf2[(u - 8) * n_own : (u - 7) * n_own, :] = t

    def finish_gains(i, t):
        gg[...] = t

    ga = Gather(p, W, ss, rs)
    mini = Gather(p, G, gss, grs)
    sc = Scatter(p, part, land, finish, sss, srs)
    msc = Scatter(
        p, lambda i: ggp.at[0], lambda i, at, n: gland.at[pl.ds(at, n)], finish_gains, mss, mrs
    )

    bar = pltpu.get_barrier_semaphore()
    for q in p.peers():
        pl.semaphore_signal(bar, inc=1, device_id=q, device_id_type=MESH)

    def xcopy(k, src, dst):
        return pltpu.make_async_remote_copy(
            src_ref=src, dst_ref=dst, send_sem=xss.at[k], recv_sem=xrs.at[k],
            device_id=p.Y, device_id_type=MESH,
        )

    def load_rows(k, src, dst):
        @pl.when(vis)
        def _():
            local(k, src, dst.at[pl.ds(C, rows)]).start()

        @pl.when(p.y == 0)
        def _():
            xcopy(k, src.at[pl.ds(0, C)], dst.at[pl.ds(0, C)]).start()
            local(k, src.at[pl.ds(C, rows - C)], dst.at[pl.ds(2 * C, rows - C)]).start()
            dst[0 : 2 * C, :] = jnp.zeros((2 * C, WIDE), BF16)

    def wait_rows(k, src, dst):
        @pl.when(vis)
        def _():
            local(k, src, dst.at[pl.ds(C, rows)]).wait()
            xcopy(k, src.at[pl.ds(0, C)], dst.at[pl.ds(0, C)]).wait_recv()

        @pl.when(p.y == 0)
        def _():
            local(k, src.at[pl.ds(C, rows - C)], dst.at[pl.ds(2 * C, rows - C)]).wait()
            xcopy(k, src.at[pl.ds(0, C)], dst.at[pl.ds(0, C)]).wait_send()

    def store_rows(k, src, dst):
        @pl.when(vis)
        def _():
            xcopy(k, src.at[pl.ds(0, C)], dst.at[pl.ds(0, C)]).start()
            local(k, src.at[pl.ds(C, rows)], dst).start()

        @pl.when(p.y == 0)
        def _():
            local(k, src.at[pl.ds(2 * C, rows - C)], dst.at[pl.ds(C, rows - C)]).start()

    def stored_rows(k, src, dst):
        @pl.when(vis)
        def _():
            xcopy(k, src.at[pl.ds(0, C)], dst.at[pl.ds(0, C)]).wait_send()
            local(k, src.at[pl.ds(C, rows)], dst).wait()

        @pl.when(p.y == 0)
        def _():
            local(k, src.at[pl.ds(2 * C, rows - C)], dst.at[pl.ds(C, rows - C)]).wait()

    def came_back(k, src, dst):
        @pl.when(p.y == 0)
        def _():
            xcopy(k, src.at[pl.ds(0, C)], dst.at[pl.ds(0, C)]).wait_recv()

    def place_gains():
        lane = lax.broadcasted_iota(jnp.int32, (1, 128), 1)
        mine = lane // n_own == lax.rem(p.x * 2 + p.c, 4)
        pair = []
        for g in (g1, g2):
            v = g[...].astype(BF16).astype(F32)
            pair.append(jnp.where(mine, jnp.concatenate([v] * 4, axis=1), 0.0))
        G[0, p.y, p.z, p.x, p.c] = jnp.concatenate(pair + [jnp.zeros((6, 128), F32)], axis=0)

    def place_own(u):
        lane = lax.broadcasted_iota(jnp.int32, (n_own, 128), 1)
        for k in range(8):
            at = slice(k * 128, (k + 1) * 128)
            if u < 2:
                v = h1[u * n_own : (u + 1) * n_own, at]
                v = move_lanes([(v, a, b, n) for a, b, n in head_moves()], lane)
            elif u == 2:
                v = h1[2 * n_own : 3 * n_own, at]
            elif u == 3:
                v = h1[3 * n_own : 4 * n_own, at]
            elif u < 8:
                j = u - 4
                top = (4 + k // 2) * n_own
                left = k % 2 * 512
                v = move_lanes(
                    [
                        (h1[top : top + n_own, left + a * 128 : left + (a + 1) * 128], 32 * j, 32 * a, 32)
                        for a in range(4)
                    ],
                    lane,
                )
            else:
                v = h1[u * n_own : (u + 1) * n_own, at]
            W[u, p.y, p.z, p.x, p.c, :, at] = v.astype(BF16)

    def place_codes():
        pair = []
        for ref in (clips, frames):
            v = ref[...].astype(F32)
            pair.append(jnp.concatenate([v[k : k + 1] for k in range(rows // 128)], axis=1))
        both = jnp.concatenate(pair + [jnp.zeros((6, rows), F32)], axis=0)
        src = lax.broadcasted_iota(jnp.int32, (rows, 128), 0)
        lane = lax.broadcasted_iota(jnp.int32, (rows, 128), 1)
        pick = jnp.where((src == lane // FA * FV) & (lane < C), 1.0, 0.0).astype(BF16)
        cond = dot(both.astype(BF16), pick)
        full = jnp.concatenate([cond[:, :C], both], axis=1)
        clip, when = full[0:1], full[1:2]
        base = clip * 64.0
        code = base + when
        lo = jnp.where(clip >= 0, base, 1.0)
        hi = jnp.where(clip >= 0, code, 0.0)
        twice = lambda v: jnp.concatenate([v[:, :C], v[:, :C], v[:, 2 * C :]], axis=1)
        for k, v in enumerate((code, lo, hi, when, twice(lo), twice(hi))):
            codes[k : k + 1, 0:R] = v

    def gains():
        for y in range(2):
            for z in range(4):
                t = G[0, y, z, 0, 0] + G[0, y, z, 0, 1] + G[0, y, z, 1, 0] + G[0, y, z, 1, 1]
                gain[:, (y * 4 + z) * 128 : (y * 4 + z + 1) * 128] = t
        gain[4:6, :] = jnp.zeros((2, WIDE), F32)

    def column(row, at):
        return jnp.transpose(jnp.broadcast_to(codes[row : row + 1, at : at + 128], (128, 128)))

    def tables():
        side = (HD - RT) // 2
        for at in range(0, R, 128):
            n = min(128, R - at)
            shape = (n, 128)
            lane, i = rope_lane(shape)
            t = column(3, at)[:n]
            place = lax.broadcasted_iota(jnp.int32, shape, 0) + (at - C)
            inner = place % FV
            own_row = (place >= 0) & vis
            down = jnp.where(own_row, inner // GW, 0).astype(F32)
            across = jnp.where(own_row, inner % GW, 0).astype(F32)
            first, second = RT // 2, RT // 2 + side // 2
            k = jnp.where(i < first, i, jnp.where(i < second, i - first, i - second)).astype(F32)
            n_at = jnp.where(i < first, t, jnp.where(i < second, down, across))
            width = jnp.where(i < first, float(RT), float(side))
            angle = n_at * jnp.exp(k / width * (-2.0 * LOG_THETA))
            ct[at : at + n, :] = jnp.cos(angle)
            sine = jnp.sin(angle)
            st[at : at + n, :] = jnp.where(lane < 64, -sine, sine)

    def biases():
        for at in range(0, R, 128):
            n = min(128, R - at)
            kc = column(0, at)[:n]
            key = lax.broadcasted_iota(jnp.int32, (n, 128), 0) + at
            lane = lax.broadcasted_iota(jnp.int32, (n, 128), 1)
            for qa in range(0, rows, 128):
                lo = codes[1:2, C + qa : C + qa + 128]
                hi = codes[2:3, C + qa : C + qa + 128]
                ok = ((kc >= lo) & (kc <= hi)) | (key == lane + (qa + C))
                bias[at : at + n, qa : qa + 128] = jnp.where(ok, 0.0, NEG)
            lo, hi = codes[4:5, 0:128], codes[5:6, 0:128]
            ok = ((kc >= lo) & (kc <= hi)) | (key == lane % 64)
            cbias[at : at + n, :] = jnp.where(ok, 0.0, NEG)

    def norm_one():
        @pl.loop(0, R // 64)
        def _(k):
            r = pl.ds(pl.multiple_of(k * 64, 64), 64)
            unit, _ = unit_rows(x[r, :].astype(F32))
            dur(0)[r, :] = (unit * gain[0:1, :]).astype(BF16)

    def turned(v, rowset, sign):
        return v * ct[rowset, :] + pltpu.roll(v, 64, 1) * (st[rowset, :] * sign)

    def project(u):
        dst = (Q, K, V)[u]

        @pl.loop(0, WIDE // 256)
        def _(k):
            at = pl.multiple_of(k * 256, 256)
            v = dot(dur(0)[...], W3[u, :, pl.ds(at, 256)])
            for h in range(2):
                part_v = v[:, h * 128 : (h + 1) * 128]
                if u < 2:
                    part_v = turned(part_v, slice(0, R), 1.0)
                dst[:, pl.ds(pl.multiple_of(at + h * 128, 128), 128)] = part_v.astype(BF16)

    blocks = [(0, C, R)] + [(C + 128 * b, 128, C + 128 * (b + 1)) for b in range(rows // 128)]

    def masks():
        lane, _ = rope_lane((1, 128))
        even = (lane % 64) < 32
        first = lane < 64
        return even, first

    def stack(v, m, scale):
        zero = jnp.zeros_like(v)
        both = jnp.concatenate([jnp.where(m, v, zero), jnp.where(m, zero, v)], axis=0)
        return both * jnp.asarray(scale, BF16) if scale != 1.0 else both

    def scores(b, q0, nq, n, k, rq):
        s = lax.dot_general(k[:n], rq, (((1,), (1,)), ((), ())), preferred_element_type=F32)
        if b == 0:
            return s + cbias[0:n, :]
        t = bias[0:n, q0 - C : q0 - C + nq]
        return s + jnp.concatenate([t, t], axis=1)

    def attend(lo, hi):
        @pl.when(vis)
        def _():
            even, first = masks()

            @pl.loop(lo, hi)
            def _(pair):
                cols = pl.ds(pl.multiple_of(pair * 128, 128), 128)
                k, v = K[:, cols], V[:, cols]
                for b, (q0, nq, n) in enumerate(blocks):
                    rq = stack(Q[q0 : q0 + nq, cols], even, HD ** -0.5)
                    s = scores(b, q0, nq, n, k, rq)
                    top = jnp.max(s, axis=0, keepdims=True)
                    e = jnp.exp(s - top)
                    total = jnp.sum(e, axis=0, keepdims=True)
                    prob = (e * (1.0 / total)).astype(BF16)
                    lse[pair, b : b + 1, 0 : 2 * nq] = top + jnp.log(total)
                    o = lax.dot_general(
                        v[:n], prob, (((0,), (0,)), ((), ())), preferred_element_type=F32
                    )
                    o = jnp.transpose(o)
                    ob[q0 : q0 + nq, cols] = jnp.where(first, o[:nq], o[nq:]).astype(BF16)

    def attend_back(lo, hi):
        @pl.when(vis)
        def _():
            even, first = masks()

            @pl.loop(lo, hi)
            def _(pair):
                cols = pl.ds(pl.multiple_of(pair * 128, 128), 128)
                k, v = K[:, cols], V[:, cols]
                for b, (q0, nq, n) in enumerate(blocks):
                    rq = stack(Q[q0 : q0 + nq, cols], even, HD ** -0.5)
                    rd = stack(dob[q0 : q0 + nq, cols], first, 1.0)
                    s = scores(b, q0, nq, n, k, rq)
                    prob = jnp.exp(s - lse[pair, b : b + 1, 0 : 2 * nq])
                    dp = lax.dot_general(
                        v[:n], rd, (((1,), (1,)), ((), ())), preferred_element_type=F32
                    )
                    centre = jnp.sum(prob * dp, axis=0, keepdims=True)
                    ds = (prob * (dp - centre)).astype(BF16)
                    dvn = dot(prob.astype(BF16), rd)
                    dkn = dot(ds, rq)
                    if b == 0:
                        dv[...] = dvn
                        dk[...] = dkn
                    else:
                        dv[0:n, :] += dvn
                        dk[0:n, :] += dkn
                    t = lax.dot_general(
                        k[:n], ds, (((0,), (0,)), ((), ())), preferred_element_type=F32
                    )
                    t = jnp.transpose(t)
                    dq = jnp.where(even, t[:nq], t[nq:]) * HD ** -0.5
                    Q[q0 : q0 + nq, cols] = turned(dq, slice(q0, q0 + nq), -1.0).astype(BF16)
                K[:, cols] = turned(dk[...], slice(0, R), -1.0).astype(BF16)
                V[:, cols] = dv[...].astype(BF16)

    def pad_forward():
        @pl.when(p.y == 0)
        def _():
            ob[...] = V[...]

    def pad_back():
        @pl.when(p.y == 0)
        def _():
            Q[...] = jnp.zeros((R, WIDE), BF16)
            K[...] = jnp.zeros((R, WIDE), BF16)
            V[...] = dob[...]

    def hidden():
        @pl.loop(0, R // TILE)
        def _(k):
            r = pl.ds(pl.multiple_of(k * TILE, 32), TILE)
            h1[r, :] = x[r, :].astype(F32) + dot(ob[r, :], W3[3])

        @pl.loop(0, R // 64)
        def _(k):
            r = pl.ds(pl.multiple_of(k * 64, 64), 64)
            unit, _ = unit_rows(h1[r, :])
            a2[r, :] = (unit * gain[1:2, :]).astype(BF16)

    def inner(j):
        @pl.loop(0, WIDE // 256)
        def _(k):
            at = pl.ds(pl.multiple_of(k * 256, 256), 256)
            u = dot(a2[...], W3[4 + j, :, at])
            phi = 0.5 + 0.5 * lax.erf(u * 0.7071067811865476)
            gbr(j)[:, at] = (u * phi).astype(BF16)
            dur(j)[:, at] = (phi + u * (jnp.exp(u * u * -0.5) * 0.3989422804014327)).astype(BF16)

    def weight_grad(i, left, right):
        dst = part3(i)

        @pl.loop(0, WIDE // 256)
        def _(k):
            at = pl.ds(pl.multiple_of(k * 256, 256), 256)
            t = lax.dot_general(
                left(at), right(), (((0,), (0,)), ((), ())), preferred_element_type=F32
            )
            dst[at, :] = t.astype(BF16)

    def grad2(j):
        weight_grad(j, lambda at: gbr(j)[:, at], lambda: cot[...])

    def grad1(j):
        weight_grad(4 + j, lambda at: a2[:, at], lambda: dur(j)[...])

    def du(j):
        @pl.loop(0, WIDE // 256)
        def _(k):
            at = pl.ds(pl.multiple_of(k * 256, 256), 256)
            d = lax.dot_general(
                cot[...], W3[8 + j, at, :], (((1,), (1,)), ((), ())), preferred_element_type=F32
            )
            dur(j)[:, at] = (d * dur(j)[:, at].astype(F32)).astype(BF16)

    def result(lo, hi):
        @pl.loop(lo, hi)
        def _(k):
            at = pl.ds(pl.multiple_of(k * 256, 256), 256)
            t = h1[:, at]
            for j in range(4):
                t = t + dot(gbr(j)[...], W3[8 + j, :, at])
            obuf[:, at] = t.astype(BF16)

    def hidden_back(lo, hi):
        @pl.loop(lo, hi)
        def _(k):
            r = pl.ds(pl.multiple_of(k * TILE, 32), TILE)
            t = lax.dot_general(
                dur(0)[r, :], W3[4], (((1,), (1,)), ((), ())), preferred_element_type=F32
            )
            for j in range(1, 4):
                t = t + lax.dot_general(
                    dur(j)[r, :], W3[4 + j], (((1,), (1,)), ((), ())), preferred_element_type=F32
                )
            unit, inverse = unit_rows(h1[r, :])
            gain[5:6, :] += jnp.sum(t * unit, axis=0, keepdims=True)
            t = cot[r, :].astype(F32) + back_rows(t, gain[1:2, :], unit, inverse)
            h1[r, :] = t
            obuf[r, :] = t.astype(BF16)

    def mixed_back():
        @pl.loop(0, WIDE // 256)
        def _(k):
            at = pl.ds(pl.multiple_of(k * 256, 256), 256)
            t = lax.dot_general(
                obuf[...], W3[7, at, :], (((1,), (1,)), ((), ())), preferred_element_type=F32
            )
            dob[:, at] = t.astype(BF16)

    def input_back(lo, hi):
        @pl.loop(lo, hi)
        def _(k):
            r = pl.ds(pl.multiple_of(k * TILE, 32), TILE)
            t = None
            for u, src in enumerate((Q, K, V)):
                d = lax.dot_general(
                    src[r, :], W3[4 + u], (((1,), (1,)), ((), ())), preferred_element_type=F32
                )
                t = d if t is None else t + d
            unit, inverse = unit_rows(x[r, :].astype(F32))
            gain[4:5, :] += jnp.sum(t * unit, axis=0, keepdims=True)
            t = h1[r, :] + back_rows(t, gain[0:1, :], unit, inverse)
            obuf[r, :] = t.astype(BF16)

    def local(k, src, dst):
        return pltpu.make_async_copy(src, dst, loc.at[k])

    def own_copies():
        pieces = [wq.at[:, pl.ds(k * WIDE, WIDE)] for k in range(3)] + [wp]
        pieces += [w1.at[:, pl.ds(k * WIDE, WIDE)] for k in range(4)]
        pieces += [w2.at[pl.ds(k * n_own, n_own)] for k in range(4)]
        return [
            local(8 + k, piece, h1.at[pl.ds(k * n_own, n_own)]) for k, piece in enumerate(pieces)
        ]

    def spill_copy(u):
        return local(4 + u, W.at[u], spill.at[u])

    def reload_copy(u):
        return local(4 + u, spill.at[u], W.at[4 + u])

    def grant(i):
        for q in p.peers():
            pl.semaphore_signal(credit.at[i], inc=1, device_id=q, device_id_type=MESH)

    shards = own_copies()
    for c in shards:
        c.start()
    place_gains()
    for c in shards[:2]:
        c.wait()
    place_own(0)
    place_own(1)
    pl.semaphore_wait(bar, 6)
    mini.first(0)
    mini.second(0)
    early = [u for u in range(NU) if u not in LINE_UNITS]
    ga.first(0)
    ga.second(0)
    ga.first(1)
    ga.second(1)
    load_rows(0, x_hbm, x)
    load_rows(1, cot_hbm, cot)
    for c in shards[2:]:
        c.wait()
    for u in range(2, NU):
        place_own(u)
        if u in LINE_UNITS[:1] and LINE_START[0] == 0:
            ga.line0(u)
        if u in early[2:FIRST_AHEAD]:
            ga.first(u)
        if u in early[2:SECOND_AHEAD]:
            ga.second(u)
    mini.g1(0)
    place_codes()
    mini.g2(0)
    tables()
    mini.g3(0)

    @pl.when(vis)
    def _():
        biases()

    mini.g4(0)
    gains()
    wait_rows(0, x_hbm, x)
    wait_rows(1, cot_hbm, cot)
    norm_one()

    def scatter_open(i):
        pl.semaphore_wait(credit.at[i], 6)
        sc.r0(i)

    def scatter_close(i):
        (sc.h4 if i in HALF_UNITS else sc.r4)(i)
        sc.flush(i)
        if i < 4:
            grant(i + 8)

    def row_gains():
        for y in range(2):
            for z in range(4):
                at = (y * 4 + z) * 128
                for b in range(2):
                    for c in range(2):
                        ggp[0, y, z, b, c] = gain[:, at : at + 128]

    def gather_close():
        ga.flush()
        for u in LINE_UNITS:
            ga.line_flush(u)

    def grants(lo, hi):
        for i in range(lo, hi):
            grant(i)

    def all_of(f, *args):
        for a in args:
            f(a)

    def spills(start):
        for u in range(4):
            if start:
                spill_copy(u).start()
            else:
                spill_copy(u).wait()

    def reloads(start):
        for u in range(4):
            if start:
                reload_copy(u).start()
            else:
                reload_copy(u).wait()

    def run_part(i):
        if i < 4:
            grad2(i)
        elif i < 8:
            grad1(i - 4)
        elif i == 8:
            weight_grad(8, lambda at: ob[:, at], lambda: obuf[...])
        else:
            src = (Q, K, V)[i - 9]
            weight_grad(i, lambda at: dur(0)[:, at], lambda: src[...])

    def run_hback(k):
        if k == 0:
            stored_rows(2, obuf, out_hbm)
        hidden_back(k, k + 1)

    def early_close():
        for u in range(4):
            ga.flush(u)

    actions = {
        FIRST: ga.first,
        SECOND: ga.second,
        G1: ga.g1,
        G2: ga.g2,
        G3: ga.g3,
        G4: ga.g4,
        LINE0: ga.line0,
        LINE1: ga.line1,
        LINE2: ga.line2,
        LINE31: lambda u: ga.line3(u, 1),
        LINE32: lambda u: ga.line3(u, 2),
        LINE33: lambda u: ga.line3(u, 3),
        LINE4: ga.line4,
        CLOSE0: early_close,
        CLOSE: gather_close,
        OPEN: scatter_open,
        R1: lambda i: (sc.h1 if i in HALF_UNITS else sc.r1)(i),
        R2: lambda i: (sc.h2 if i in HALF_UNITS else sc.r2)(i),
        R3: lambda i: (sc.h3 if i in HALF_UNITS else sc.r3)(i),
        R4: scatter_close,
        MINI: lambda k: (msc.r0, msc.r1, msc.r2, msc.r3, msc.r4)[k](0),
        PROJ: project,
        ATTEND: lambda k: attend(k * PAIRS, (k + 1) * PAIRS),
        HIDDEN: lambda: (pad_forward(), hidden(), spills(True)),
        INNER: inner,
        PART: run_part,
        GRANT0: lambda: (spills(False), grants(0, 4)),
        DU: du,
        RESULT: lambda k: result(2 * k, 2 * k + 2),
        GRANT4: lambda: (store_rows(2, obuf, out_hbm), grants(4, 8)),
        HBACK: run_hback,
        RELOAD: lambda: reloads(True),
        MIXED: lambda: (reloads(False), mixed_back(), pad_back()),
        ABACK: lambda k: attend_back(k * PAIRS, (k + 1) * PAIRS),
        AGAIN: norm_one,
        IBACK: lambda k: input_back(k, k + 1),
        ROWS: lambda: (store_rows(3, obuf, xg_hbm), row_gains()),
    }
    for name in full_order():
        actions[name[0]](*name[1:])
    sc.flush()
    msc.flush()
    mini.flush()
    stored_rows(3, obuf, xg_hbm)
    came_back(2, obuf, out_hbm)
    came_back(3, obuf, xg_hbm)


(
    FIRST, SECOND, G1, G2, G3, G4, LINE0, LINE1, LINE2, LINE31, LINE32, LINE33, LINE4, CLOSE0, CLOSE,
    OPEN, R1, R2, R3, R4, MINI, PROJ, ATTEND, HIDDEN, INNER, PART, GRANT0, DU, RESULT, GRANT4, HBACK,
    RELOAD, MIXED, ABACK, AGAIN, IBACK, ROWS,
) = range(37)
PAIRS = 2


LINE_UNITS = (9, 11)
LINE_START = (0, 3)
HALF_UNITS = ()
FIRST_AHEAD = 2
SECOND_AHEAD = 3


PLAN = (
    2, 19, 32, 121, 3, 20, 33, 48, 4, 21, 34, 49, 64, 107, 137, 5, 22, 35, 50, 80,
    336, 65, 123, 6, 23, 36, 51, 81, 337, 66, 153, 7, 24, 37, 52, 82, 338, 352, 67, 139,
    8, 26, 38, 353, 53, 83, 354, 208, 68, 169, 10, 39, 355, 54, 84, 69, 368, 155, 384, 40,
    55, 400, 85, 70, 385, 185, 401, 42, 56, 416, 86, 386, 71, 402, 201, 433, 171, 240, 241, 256,
    58, 87, 387, 403, 72, 242, 257, 272, 88, 432, 74, 187, 243, 258, 273, 90, 434, 203, 435, 448,
    224, 449, 464, 404, 244, 259, 480, 288, 274, 481, 405, 245, 260, 289, 496, 275, 512, 304, 406, 246,
    261, 528, 290, 276, 305, 407, 247, 262, 529, 291, 277, 306, 408, 248, 263, 530, 292, 278, 307, 531,
    544, 409, 249, 264, 293, 279, 308, 410, 250, 265, 411, 294, 280, 560, 309, 561, 251, 266, 295, 576,
    281, 310, 267, 296, 282, 311, 320, 297, 283, 312, 321, 298, 313, 322, 299, 314, 323, 315, 324,
)
BARE = (CLOSE0, CLOSE, HIDDEN, GRANT0, GRANT4, RELOAD, MIXED, AGAIN, ROWS)


def full_order():
    return [(v // 16,) if v // 16 in BARE else (v // 16, v % 16) for v in PLAN]


def hand_over_kernel(*refs):
    n = 6
    arrays, gg, outs, g1, g2 = refs[:n], refs[n], refs[n + 1 : 2 * n + 1], refs[2 * n + 1], refs[2 * n + 2]
    held, sems = refs[2 * n + 3 : 3 * n + 3], refs[3 * n + 3]
    pieces = []
    for a, h, o in zip(arrays, held, outs):
        count = 4 if a.shape[0] >= 512 else 1
        step = a.shape[0] // count
        pieces += [[r.at[pl.ds(k * step, step)] for r in (a, h, o)] for k in range(count)]
    into = [pltpu.make_async_copy(a, h, sems.at[2 * k]) for k, (a, h, o) in enumerate(pieces)]
    back = [pltpu.make_async_copy(h, o, sems.at[2 * k + 1]) for k, (a, h, o) in enumerate(pieces)]
    for c in into:
        c.start()
    lane = lax.rem(lax.axis_index("clip"), 4)
    for row, g in ((4, g1), (5, g2)):
        v = gg[row : row + 1, :]
        t = v[:, 0:32]
        for k in range(1, 4):
            t = jnp.where(lane == k, v[:, 32 * k : 32 * k + 32], t)
        g[...] = t
    for a, b in zip(into, back):
        a.wait()
        b.start()
    for b in back:
        b.wait()


def hand_over(arrays, gg, n):
    hbm = pl.BlockSpec(memory_space=pl.ANY)
    vmem = pl.BlockSpec(memory_space=pltpu.VMEM)
    shapes = [jax.ShapeDtypeStruct(a.shape, a.dtype) for a in arrays]
    return pl.pallas_call(
        hand_over_kernel,
        out_shape=shapes + [jax.ShapeDtypeStruct((1, n), F32)] * 2,
        in_specs=[hbm] * len(arrays) + [vmem],
        out_specs=[hbm] * len(arrays) + [vmem] * 2,
        scratch_shapes=[pltpu.VMEM(a.shape, a.dtype) for a in arrays]
        + [pltpu.SemaphoreType.DMA((24,))],
    )(*arrays, gg)


def fast_body(
    tokens, w_qkv, w_proj, w_fc1, w_fc2, norm1_gain, norm2_gain, clip_index, frame_index, cotangent
):
    rows, width = tokens.shape
    n = w_qkv.shape[0]
    R = rows + rows // FV * FA
    unit = (2, 4, 2, 2, n, width)
    hbm = pl.BlockSpec(memory_space=pl.ANY)
    vmem = pl.BlockSpec(memory_space=pltpu.VMEM)
    rows_low = pltpu.VMEM((R, width), BF16)
    lanes = pltpu.VMEM((R, 128), F32)
    out, xg, gq, gpr, gf1, gf2, gg, _ = pl.pallas_call(
        layer_kernel,
        out_shape=[
            jax.ShapeDtypeStruct((rows, width), BF16),
            jax.ShapeDtypeStruct((rows, width), BF16),
            jax.ShapeDtypeStruct(w_qkv.shape, F32),
            jax.ShapeDtypeStruct(w_proj.shape, F32),
            jax.ShapeDtypeStruct(w_fc1.shape, F32),
            jax.ShapeDtypeStruct(w_fc2.shape, F32),
            jax.ShapeDtypeStruct((8, 128), F32),
            jax.ShapeDtypeStruct((4,) + unit, BF16),
        ],
        in_specs=[hbm] * 6 + [vmem] * 4,
        out_specs=[hbm, hbm] + [vmem] * 5 + [hbm],
        scratch_shapes=[
            pltpu.VMEM((NU,) + unit, BF16),
            pltpu.VMEM((1, 2, 4, 2, 2, 8, 128), F32),
            pltpu.VMEM((8, -(-R // 128) * 128), F32),
            rows_low,
            rows_low,
            rows_low,
            rows_low,
            rows_low,
            rows_low,
            rows_low,
            pltpu.VMEM((R, width), F32),
            rows_low,
            pltpu.VMEM((2,) + unit, BF16),
            pltpu.VMEM((3,) + unit, BF16),
            pltpu.VMEM((4,) + unit, BF16),
            rows_low,
            pltpu.VMEM((R, rows), F32),
            lanes,
            lanes,
            lanes,
            pltpu.VMEM((8, 8, 256), F32),
            lanes,
            lanes,
            pltpu.VMEM((8, width), F32),
            pltpu.VMEM((1, 2, 4, 2, 2, 8, 128), F32),
            pltpu.VMEM((32, 8, 128), F32),
            pltpu.SemaphoreType.DMA((NU, 17)),
            pltpu.SemaphoreType.DMA((NU, 17)),
            pltpu.SemaphoreType.DMA((1, 17)),
            pltpu.SemaphoreType.DMA((1, 17)),
            pltpu.SemaphoreType.DMA((NU, 16)),
            pltpu.SemaphoreType.DMA((NU, 16)),
            pltpu.SemaphoreType.DMA((1, 12)),
            pltpu.SemaphoreType.DMA((1, 12)),
            pltpu.SemaphoreType.DMA((4,)),
            pltpu.SemaphoreType.DMA((4,)),
            pltpu.SemaphoreType.DMA((20,)),
            pltpu.SemaphoreType.REGULAR((NU,)),
        ],
        compiler_params=pltpu.CompilerParams(
            collective_id=0, has_side_effects=True, vmem_limit_bytes=VMEM_LIMIT
        ),
    )(
        tokens,
        cotangent,
        w_qkv,
        w_proj,
        w_fc1,
        w_fc2,
        norm1_gain.reshape(1, n),
        norm2_gain.reshape(1, n),
        clip_index.reshape(rows // 128, 128),
        frame_index.reshape(rows // 128, 128),
    )
    *arrays, gain1, gain2 = hand_over((out, xg, gq, gpr, gf1, gf2), gg, n)
    return *arrays, gain1.reshape(n), gain2.reshape(n)


def solution(mesh):
    placed = (
        P(("stream", "clip"), None),
        P(("stream", "clip"), None),
        P(("stream", "clip"), None),
        P(("stream", "clip"), None),
        P(("stream", "clip"), None),
        P(("stream", "clip")),
        P(("stream", "clip")),
        P(("stream", "clip")),
        P(("stream", "clip")),
        P(("stream", "clip"), None),
    )
    block = mesh.shape["stream"] == 2 and mesh.shape["clip"] == 16
    return jax.shard_map(
        fast_body if block else body,
        mesh=mesh,
        in_specs=placed,
        out_specs=(
            P(("stream", "clip"), None),
            P(("stream", "clip"), None),
            P(("stream", "clip"), None),
            P(("stream", "clip"), None),
            P(("stream", "clip"), None),
            P(("stream", "clip"), None),
            P(("stream", "clip")),
            P(("stream", "clip")),
        ),
        check_vma=False,
    )
```
